32 devices in a mesh: gs: 8 (over z, y), view: 4 (over x, core).
Axes of the slice: x: 2, y: 2, z: 4, core: 2. Of those that a mesh axis runs over, the one named last changes fastest.
Arguments:
- means: float32 [3, 8192], P(None, 'gs'), may hold values from -256 to 256, as said below
- quats: float32 [4, 8192], P(None, 'gs'), may hold values from -1 to 2, as said below
- log_scales: float32 [3, 8192], P(None, 'gs'), may hold values from -2.6 to -1.6
- opacity: float32 [8192], P('gs'), may hold values from -5.5 to -2.5
- sh_coeffs: float32 [48, 8192], P(None, 'gs'), may hold values from -1.8 to 1.8
- cameras: float32 [4, 2], P('view'), may hold values from -1 to 128
- targets: float32 [4, 3, 128, 128], P('view', None, 'gs'), may hold values from 0 to 1
- send_rows: int32 [8, 8, 128], P('gs'), may hold values from 0 to 1023, as said below
- tile_lists: int32 [4, 8, 8, 128], P('view', 'gs'), may hold values from 0 to 1023, as said below
- list_lengths: int32 [4, 8, 8], P('view', 'gs'), may hold values from 0 to 128
Outputs:
- rendered: float32 [4, 3, 128, 128], P('view', None, 'gs')
- grad_means: float32 [3, 8192], P(None, 'gs')
- grad_quats: float32 [4, 8192], P(None, 'gs')
- grad_log_scales: float32 [3, 8192], P(None, 'gs')
- grad_opacity: float32 [8192], P('gs')
- grad_sh: float32 [48, 8192], P(None, 'gs')
The draws below stay inside these ranges and needn't reach their ends.
Inputs may be any that keep to these rules, and one draw needn't show every extreme that they name: `send_rows`: slots k of a pair (source, owner) below that pair's count hold distinct rows, each row in at most one used slot of its source; every source fills all 128 slots of one owner. `tile_lists`: the used entries of a list are distinct used slots in increasing depth. `quats`: the real part lies in 1 to 2, the others in -1 to 1. `means`: depths lie in 10 to 10.5.
All inputs are finite; a program needn't handle non-finite values.
Results may differ from the reference program's by a relative error of at most 0.0003.
Values sent between devices are 32-bit elements; how exact they have to be, the bound alone decides.
A program may use at most 64 MiB of HBM per device.

```python
import math
from functools import partial
import jax
import jax.numpy as jnp
from jax import lax

TILE = 16
BLOCK = 64
LIST = 128
SH = 16
RADIUS = 5
SHIFT = 4
VIEW_DEV = 1
TC = 8
G_DEV = 1024
CAP = 128
G_TOTAL = 8192
VIEWS = 4
N_GS = 8
N_VIEW = 4


focal_length = 1000.0


depth_base = 10.0


def routing(key):
    key_load = jax.random.fold_in(key, 101)
    key_fill = jax.random.fold_in(key, 102)
    key_star = jax.random.fold_in(key, 103)
    key_perm = jax.random.fold_in(key, 104)
    key_column = jax.random.fold_in(key, 105)
    key_shift = jax.random.fold_in(key, 106)
    key_depth = jax.random.fold_in(key, 107)
    low_load = max(CAP // 4, 1)
    load = jax.random.randint(key_load, (N_GS,), low_load, CAP + 1)
    raw_fill = jax.random.randint(key_fill, (N_GS, N_GS), 0, 1 << 20)
    half_load = load[None, :] // 2
    counts = half_load + raw_fill % (load[None, :] - half_load + 1)
    star = (jnp.arange(N_GS, dtype=jnp.int32) + jax.random.randint(key_star, (), 0, N_GS)) % N_GS
    counts = jnp.where(jnp.arange(N_GS, dtype=jnp.int32)[None, :] == star[:, None], CAP, counts).astype(jnp.int32)
    ends = jnp.cumsum(counts, axis=1)
    starts = ends - counts
    perms = jax.vmap(lambda sub_key: jax.random.permutation(sub_key, G_DEV))(jax.random.split(key_perm, N_GS)).astype(jnp.int32)
    slot_pos = (starts[:, :, None] + jnp.arange(CAP, dtype=jnp.int32)[None, None, :]) % G_DEV
    send = jax.vmap(lambda perm_row, pos_row: jnp.take(perm_row, pos_row))(perms, slot_pos).astype(jnp.int32)
    dest_of_pos = jnp.sum((jnp.arange(G_DEV, dtype=jnp.int32)[None, :, None] >= ends[:, None, :]).astype(jnp.int32), axis=2)
    strip_local = jax.vmap(lambda perm_row, dest_row: jnp.zeros((G_DEV,), jnp.int32).at[perm_row].set(dest_row))(perms, dest_of_pos)
    strip_of = strip_local.reshape(G_DEV * N_GS)
    base_col = jax.random.randint(key_column, (G_DEV * N_GS,), 0, TC + SHIFT)
    shifts = jax.random.randint(key_shift, (VIEW_DEV * N_VIEW,), 0, SHIFT + 1)
    depth_key = jax.random.randint(key_depth, (G_DEV * N_GS,), 0, 1024)
    return (send, counts, strip_of, base_col, shifts, depth_key)


def listing(key):
    send, counts, strip_of, base_col, shifts, depth_key = routing(key)
    owners = jnp.arange(N_GS, dtype=jnp.int32) * G_DEV
    slot_ids = (send + owners[:, None, None]).transpose(1, 0, 2).reshape(N_GS, G_DEV)
    slot_live = (jnp.arange(CAP, dtype=jnp.int32)[None, None, :] < counts[:, :, None]).transpose(1, 0, 2).reshape(N_GS, G_DEV)
    slot_index = jnp.arange(G_DEV, dtype=jnp.int32)
    tile_index = jnp.arange(TC, dtype=jnp.int32)
    big_score = 1 << 30
    all_lists = []
    all_lengths = []
    for view_idx in range(VIEW_DEV * N_VIEW):
        column = jnp.take(base_col, slot_ids) - shifts[view_idx]
        member = slot_live[:, None, :] & (jnp.abs(column[:, None, :] - tile_index[None, :, None]) <= 1)
        order_key = jnp.take(depth_key, slot_ids) * G_DEV + slot_index[None, :]
        score = jnp.where(member, order_key[:, None, :], big_score + slot_index[None, None, :])
        ordered = jnp.argsort(score, axis=-1)[..., :LIST].astype(jnp.int32)
        all_lists.append(ordered)
        all_lengths.append(jnp.minimum(jnp.sum(member.astype(jnp.int32), axis=-1), LIST))
    return (jnp.stack(all_lists).astype(jnp.int32), jnp.stack(all_lengths).astype(jnp.int32))


def draw_send_rows(key, part):
    return routing(key)[0].astype(jnp.int32)


def draw_tile_lists(key, part):
    return listing(key)[0]


def draw_list_lengths(key, part):
    return listing(key)[1]


def draw_means(key, part):
    send, counts, strip_of, base_col, shifts, depth_key = routing(key)
    jitter_key = jax.random.fold_in(key, 500)
    jitter = jax.random.uniform(jitter_key, (2, G_DEV * N_GS), jnp.float32, -4.0, 4.0)
    depth_z = depth_base * (1.0 + 0.05 * depth_key.astype(jnp.float32) / 1024.0)
    centre_x = 0.5 * TC * TILE
    centre_y = 0.5 * N_GS * TILE
    target_u = (base_col * TILE).astype(jnp.float32) + 8.0 + jitter[0]
    target_v = jnp.where(strip_of < N_GS, (strip_of * TILE).astype(jnp.float32) + 8.0 + jitter[1], -400.0)
    world_x = (target_u - centre_x) * depth_z / focal_length
    world_y = (target_v - centre_y) * depth_z / focal_length
    return jnp.stack([world_x, world_y, depth_z]).astype(jnp.float32)


def draw_cameras(key, part):
    shifts = routing(key)[4]
    jitter = jax.random.uniform(jax.random.fold_in(key, 600), (VIEW_DEV * N_VIEW,), jnp.float32, -0.5, 0.5)
    pan_x = (shifts * TILE).astype(jnp.float32) * depth_base / focal_length
    pan_y = jitter * depth_base / focal_length
    return jnp.stack([pan_x, pan_y], axis=1).astype(jnp.float32)


def draw_quats(key, part):
    sub_key = jax.random.fold_in(key, 700)
    real_part = jax.random.uniform(jax.random.fold_in(sub_key, 1), (1, G_DEV * N_GS), jnp.float32, 1.0, 2.0)
    imag_part = jax.random.uniform(jax.random.fold_in(sub_key, 2), (3, G_DEV * N_GS), jnp.float32, -1.0, 1.0)
    return jnp.concatenate([real_part, imag_part], axis=0).astype(jnp.float32)


def levels(stream_key, shape, cuts, low, high):
    def one(dim, blocks):
        steps = jax.random.uniform(jax.random.fold_in(jax.random.fold_in(stream_key, 6), dim), (blocks,), jnp.float32, low / len(cuts), high / len(cuts))
        return jnp.repeat(jnp.exp(steps), shape[dim] // blocks).reshape((-1,) + (1,) * (len(shape) - dim - 1))

    factor_of = one(*cuts[0])
    for cut in cuts[1:]:
        factor_of = factor_of * one(*cut)
    return factor_of


def scatter_about(key, extent, width, reach, cuts=(), held_as=jnp.bfloat16):
    gain = levels(key, extent, cuts, -0.22, 0.18) if cuts else 1.0
    values = jax.random.normal(key, extent, jnp.float32) * width * gain
    return jnp.minimum(jnp.maximum(values, -reach), reach).astype(held_as)


def setup_inputs(seed: int = 0) -> dict:
    seeds = jax.random.split(jax.random.key(seed), 11)
    means = draw_means(jax.random.fold_in(seeds[10], 71), 0)
    quats = draw_quats(jax.random.fold_in(seeds[10], 71), 0)
    log_scales = jnp.clip(-2.6 + 0.9999999 * jax.random.uniform(seeds[2], (3, G_TOTAL), jnp.float32) ** levels(seeds[2], (3, G_TOTAL), ((1, 8),), -0.2, 0.2), -2.6, -1.6)
    opacity = jnp.clip(-5.5 + 3.0 * jax.random.uniform(seeds[3], (G_TOTAL,), jnp.float32) ** levels(seeds[3], (G_TOTAL,), ((0, 8),), -0.2, 0.2), -5.5, -2.5)
    sh_coeffs = scatter_about(seeds[4], (3 * SH, G_TOTAL), 0.3, 1.8, ((1, 8),), jnp.float32)
    cameras = draw_cameras(jax.random.fold_in(seeds[10], 71), 0)
    targets = jnp.clip(1.0 * jax.random.uniform(seeds[6], (VIEWS, 3, N_GS * TILE, TC * TILE), jnp.float32) ** levels(seeds[6], (VIEWS, 3, N_GS * TILE, TC * TILE), ((0, 4), (2, 8)), -0.2, 0.2), 0.0, 1.0)
    send_rows = draw_send_rows(jax.random.fold_in(seeds[10], 71), 0)
    tile_lists = draw_tile_lists(jax.random.fold_in(seeds[10], 71), 0)
    list_lengths = draw_list_lengths(jax.random.fold_in(seeds[10], 71), 0)
    return dict(means=means, quats=quats, log_scales=log_scales, opacity=opacity, sh_coeffs=sh_coeffs, cameras=cameras, targets=targets, send_rows=send_rows, tile_lists=tile_lists, list_lengths=list_lengths)


focal_length = 1000.0
cov_blur = 0.3
ssim_weight = 0.2
charb_eps = 0.0001
ssim_one = 0.0001
ssim_two = 0.0009
sh_c0 = 0.28209479177387814
sh_c1 = 0.4886025119029199
sh_c2 = [1.0925484305920792, -1.0925484305920792, 0.31539156525252005, -1.0925484305920792, 0.5462742152960396]
sh_c3 = [-0.5900435899266435, 2.890611442640554, -0.4570457994644658, 0.3731763325901154, -0.4570457994644658, 1.445305721320277, -0.5900435899266435]

def sh_basis(dir_x, dir_y, dir_z):
    sq_x = dir_x * dir_x
    sq_y = dir_y * dir_y
    sq_z = dir_z * dir_z
    return jnp.stack([sh_c0 * jnp.ones_like(dir_x), -sh_c1 * dir_y, sh_c1 * dir_z, -sh_c1 * dir_x, sh_c2[0] * dir_x * dir_y, sh_c2[1] * dir_y * dir_z, sh_c2[2] * (2.0 * sq_z - sq_x - sq_y), sh_c2[3] * dir_x * dir_z, sh_c2[4] * (sq_x - sq_y), sh_c3[0] * dir_y * (3.0 * sq_x - sq_y), sh_c3[1] * dir_x * dir_y * dir_z, sh_c3[2] * dir_y * (4.0 * sq_z - sq_x - sq_y), sh_c3[3] * dir_z * (2.0 * sq_z - 3.0 * sq_x - 3.0 * sq_y), sh_c3[4] * dir_x * (4.0 * sq_z - sq_x - sq_y), sh_c3[5] * dir_z * (sq_x - sq_y), sh_c3[6] * dir_x * (sq_x - 3.0 * sq_y)])

def project(means, quats, log_scales, opacity, sh_coeffs, camera, centre_x, centre_y):
    rel_x = means[0] - camera[0]
    rel_y = means[1] - camera[1]
    depth_z = means[2]
    inv_depth = 1.0 / depth_z
    pix_u = focal_length * rel_x * inv_depth + centre_x
    pix_v = focal_length * rel_y * inv_depth + centre_y
    quat_norm = jnp.sqrt(lax.optimization_barrier(jnp.sum(quats * quats, axis=0)))
    quat_w = quats[0] / quat_norm
    quat_x = quats[1] / quat_norm
    quat_y = quats[2] / quat_norm
    quat_z = quats[3] / quat_norm
    rotation = [[1.0 - 2.0 * (quat_y * quat_y + quat_z * quat_z), 2.0 * (quat_x * quat_y - quat_w * quat_z), 2.0 * (quat_x * quat_z + quat_w * quat_y)], [2.0 * (quat_x * quat_y + quat_w * quat_z), 1.0 - 2.0 * (quat_x * quat_x + quat_z * quat_z), 2.0 * (quat_y * quat_z - quat_w * quat_x)], [2.0 * (quat_x * quat_z - quat_w * quat_y), 2.0 * (quat_y * quat_z + quat_w * quat_x), 1.0 - 2.0 * (quat_x * quat_x + quat_y * quat_y)]]
    scales = jnp.exp(log_scales)
    jac_diag = focal_length * inv_depth
    jac_u = -focal_length * rel_x * inv_depth * inv_depth
    jac_v = -focal_length * rel_y * inv_depth * inv_depth
    top_row = [(jac_diag * rotation[0][col_idx] + jac_u * rotation[2][col_idx]) * scales[col_idx] for col_idx in range(3)]
    low_row = [(jac_diag * rotation[1][col_idx] + jac_v * rotation[2][col_idx]) * scales[col_idx] for col_idx in range(3)]
    cov_a = top_row[0] * top_row[0] + top_row[1] * top_row[1] + top_row[2] * top_row[2] + cov_blur
    cov_b = top_row[0] * low_row[0] + top_row[1] * low_row[1] + top_row[2] * low_row[2]
    cov_c = low_row[0] * low_row[0] + low_row[1] * low_row[1] + low_row[2] * low_row[2] + cov_blur
    determ = cov_a * cov_c - cov_b * cov_b
    distance = jnp.sqrt(rel_x * rel_x + rel_y * rel_y + depth_z * depth_z)
    basis = sh_basis(rel_x / distance, rel_y / distance, depth_z / distance)
    coeffs = sh_coeffs.reshape(3, SH, -1)
    colour = jnp.maximum(lax.optimization_barrier(jnp.sum(coeffs * basis[None], axis=1)) + 0.5, 0.0)
    return jnp.stack([pix_u, pix_v, cov_c / determ, -cov_b / determ, cov_a / determ, jax.nn.sigmoid(opacity), colour[0], colour[1], colour[2]])

def blend(col_px, row_px, carry_in, inputs):
    transmit, colour = carry_in
    block_rows, live_mask = inputs
    offset_x = block_rows[0][:, None, :] - col_px[:, :, None]
    offset_y = block_rows[1][:, None, :] - row_px[None, :, None]
    power = -0.5 * (block_rows[2][:, None, :] * offset_x * offset_x + block_rows[4][:, None, :] * offset_y * offset_y) - block_rows[3][:, None, :] * offset_x * offset_y
    alpha = block_rows[5][:, None, :] * jnp.exp(power) * live_mask[:, None, :]
    keep_frac = 1.0 - alpha
    running = jnp.cumprod(keep_frac, axis=2)
    prior_keep = jnp.concatenate([jnp.ones_like(running[:, :, :1]), running[:, :, :-1]], axis=2)
    weight = transmit[:, :, None] * prior_keep * alpha
    added = jnp.stack([lax.optimization_barrier(jnp.sum(weight * block_rows[6 + channel][:, None, :], axis=2)) for channel in range(3)])
    return ((transmit * running[:, :, -1], colour + added), None)

def composite(slot_rows, lengths, row_start):
    tile_count = slot_rows.shape[1]
    list_size = slot_rows.shape[2]
    pixel_idx = jnp.arange(TILE * TILE, dtype=jnp.int32)
    col_px = (jnp.arange(tile_count, dtype=jnp.int32)[:, None] * TILE + pixel_idx[None, :] % TILE).astype(jnp.float32)
    row_px = row_start + (pixel_idx // TILE).astype(jnp.float32)
    live_mask = (jnp.arange(list_size, dtype=jnp.int32)[None, :] < lengths[:, None]).astype(jnp.float32)
    block_count = list_size // BLOCK
    rows_blocked = slot_rows.reshape(9, tile_count, block_count, BLOCK).transpose(2, 0, 1, 3)
    live_blocked = live_mask.reshape(tile_count, block_count, BLOCK).transpose(1, 0, 2)
    initial = (jnp.ones((tile_count, TILE * TILE), jnp.float32), jnp.zeros((3, tile_count, TILE * TILE), jnp.float32))
    (transmit, colour), _ = lax.scan(jax.checkpoint(partial(blend, col_px, row_px)), initial, (rows_blocked, live_blocked))
    return colour.reshape(3, tile_count, TILE, TILE).transpose(0, 2, 1, 3).reshape(3, TILE, tile_count * TILE)

def window_taps():
    raw_taps = [math.exp(-(tap_idx - RADIUS) ** 2 / 4.5) for tap_idx in range(2 * RADIUS + 1)]
    total = sum(raw_taps)
    return [tap / total for tap in raw_taps]

def blur(padded, row_count):
    taps = window_taps()
    vertical = sum((taps[tap_idx] * padded[..., tap_idx:tap_idx + row_count, :] for tap_idx in range(2 * RADIUS + 1)))
    col_count = vertical.shape[-1]
    padded_wide = jnp.pad(vertical, [(0, 0)] * (vertical.ndim - 1) + [(RADIUS, RADIUS)])
    return sum((taps[tap_idx] * padded_wide[..., tap_idx:tap_idx + col_count] for tap_idx in range(2 * RADIUS + 1)))

def strip_loss(padded_image, padded_target):
    row_count = padded_image.shape[-2] - 2 * RADIUS
    mean_x = blur(padded_image, row_count)
    mean_y = blur(padded_target, row_count)
    var_x = blur(padded_image * padded_image, row_count) - mean_x * mean_x
    var_y = blur(padded_target * padded_target, row_count) - mean_y * mean_y
    cov_xy = blur(padded_image * padded_target, row_count) - mean_x * mean_y
    ssim_map = (2.0 * mean_x * mean_y + ssim_one) * (2.0 * cov_xy + ssim_two) / ((mean_x * mean_x + mean_y * mean_y + ssim_one) * (var_x + var_y + ssim_two))
    residual = padded_image[..., RADIUS:RADIUS + row_count, :] - padded_target[..., RADIUS:RADIUS + row_count, :]
    per_pixel = (1.0 - ssim_weight) * jnp.sqrt(residual * residual + charb_eps) + ssim_weight * (1.0 - ssim_map)
    return jnp.sum(per_pixel) / (TILE * TILE)

def reference(means, quats, log_scales, opacity, sh_coeffs, cameras, targets, send_rows, tile_lists, list_lengths):
    width_px = TC * TILE
    height_px = N_GS * TILE
    owners = jnp.arange(N_GS, dtype=jnp.int32) * G_DEV
    slot_ids = (send_rows + owners[:, None, None]).transpose(1, 0, 2).reshape(N_GS, N_GS * CAP).astype(jnp.int32)
    strip_ids = jnp.arange(N_GS, dtype=jnp.int32)

    def total(params):
        total_loss = jnp.float32(0.0)
        pictures = []
        for view_idx in range(VIEWS):
            proj_rows = project(*params, cameras[view_idx], 0.5 * width_px, 0.5 * height_px)
            global_lists = jax.vmap(lambda ids_row, lists_row: jnp.take(ids_row, lists_row))(slot_ids, tile_lists[view_idx]).astype(jnp.int32)

            def strip_image(inputs):
                id_table, lengths, strip_idx = inputs
                return composite(jnp.take(proj_rows, id_table, axis=1), lengths, (strip_idx * TILE).astype(jnp.float32))
            pieces = lax.map(strip_image, (global_lists, list_lengths[view_idx], strip_ids))
            picture = pieces.transpose(1, 0, 2, 3).reshape(3, height_px, width_px)
            pad_spec = ((0, 0), (RADIUS, RADIUS), (0, 0))
            total_loss = total_loss + strip_loss(jnp.pad(picture, pad_spec), jnp.pad(targets[view_idx], pad_spec))
            pictures.append(picture)
        return (total_loss, jnp.stack(pictures))
    (loss_value, rendered), grads = jax.value_and_grad(total, has_aux=True)((means, quats, log_scales, opacity, sh_coeffs))
    return (rendered, grads[0], grads[1], grads[2], grads[3], grads[4])
```

```python
import math

import jax
import jax.numpy as jnp
import ml_dtypes
import numpy as np
from jax import lax
from jax.experimental import pallas as pl
from jax.experimental.pallas import tpu as pltpu
from jax.sharding import PartitionSpec as P

TILE = 16
SH = 16
RADIUS = 5
LANES = 128
ROWS_MSG = 16
VMEM = pltpu.VMEM
MESH = pl.DeviceIdType.MESH

focal_length = 1000.0
cov_blur = 0.3
ssim_weight = 0.2
charb_eps = 0.0001
ssim_one = 0.0001
ssim_two = 0.0009
sh_c0 = 0.28209479177387814
sh_c1 = 0.4886025119029199
sh_c2 = [
    1.0925484305920792,
    -1.0925484305920792,
    0.31539156525252005,
    -1.0925484305920792,
    0.5462742152960396,
]
sh_c3 = [
    -0.5900435899266435,
    2.890611442640554,
    -0.4570457994644658,
    0.3731763325901154,
    -0.4570457994644658,
    1.445305721320277,
    -0.5900435899266435,
]

f32 = jnp.float32
bf16 = jnp.bfloat16


def sh_basis(dir_x, dir_y, dir_z):
    sq_x = dir_x * dir_x
    sq_y = dir_y * dir_y
    sq_z = dir_z * dir_z
    return [
        None,
        -sh_c1 * dir_y,
        sh_c1 * dir_z,
        -sh_c1 * dir_x,
        sh_c2[0] * dir_x * dir_y,
        sh_c2[1] * dir_y * dir_z,
        sh_c2[2] * (2.0 * sq_z - sq_x - sq_y),
        sh_c2[3] * dir_x * dir_z,
        sh_c2[4] * (sq_x - sq_y),
        sh_c3[0] * dir_y * (3.0 * sq_x - sq_y),
        sh_c3[1] * dir_x * dir_y * dir_z,
        sh_c3[2] * dir_y * (4.0 * sq_z - sq_x - sq_y),
        sh_c3[3] * dir_z * (2.0 * sq_z - 3.0 * sq_x - 3.0 * sq_y),
        sh_c3[4] * dir_x * (4.0 * sq_z - sq_x - sq_y),
        sh_c3[5] * dir_z * (sq_x - sq_y),
        sh_c3[6] * dir_x * (sq_x - 3.0 * sq_y),
    ]


def project(means, quats, log_scales, opacity, coeffs, cameras, centre_x, centre_y):
    inv_norm = 1.0 / jnp.sqrt(
        quats[0] * quats[0] + quats[1] * quats[1] + quats[2] * quats[2] + quats[3] * quats[3]
    )
    quat_w, quat_x, quat_y, quat_z = [quat * inv_norm for quat in quats]
    scales = [jnp.exp(log_scale) for log_scale in log_scales]
    rotation = [
        [
            1.0 - 2.0 * (quat_y * quat_y + quat_z * quat_z),
            2.0 * (quat_x * quat_y - quat_w * quat_z),
            2.0 * (quat_x * quat_z + quat_w * quat_y),
        ],
        [
            2.0 * (quat_x * quat_y + quat_w * quat_z),
            1.0 - 2.0 * (quat_x * quat_x + quat_z * quat_z),
            2.0 * (quat_y * quat_z - quat_w * quat_x),
        ],
        [
            2.0 * (quat_x * quat_z - quat_w * quat_y),
            2.0 * (quat_y * quat_z + quat_w * quat_x),
            1.0 - 2.0 * (quat_x * quat_x + quat_y * quat_y),
        ],
    ]
    spread = [[rotation[i][j] * scales[j] for j in range(3)] for i in range(3)]
    depth_z = means[2]
    inv_depth = 1.0 / depth_z
    jac_diag = focal_length * inv_depth
    diag_top = [jac_diag * spread[0][j] for j in range(3)]
    diag_low = [jac_diag * spread[1][j] for j in range(3)]
    log_alpha = -jnp.log(1.0 + jnp.exp(-opacity))
    views = []
    for cam_x, cam_y in cameras:
        rel_x = means[0] - cam_x
        rel_y = means[1] - cam_y
        ratio_u = jac_diag * rel_x
        ratio_v = jac_diag * rel_y
        jac_u = -ratio_u * inv_depth
        jac_v = -ratio_v * inv_depth
        top = [diag_top[j] + jac_u * spread[2][j] for j in range(3)]
        low = [diag_low[j] + jac_v * spread[2][j] for j in range(3)]
        cov_a = top[0] * top[0] + top[1] * top[1] + top[2] * top[2] + cov_blur
        cov_b = top[0] * low[0] + top[1] * low[1] + top[2] * low[2]
        cov_c = low[0] * low[0] + low[1] * low[1] + low[2] * low[2] + cov_blur
        inv_det = 1.0 / (cov_a * cov_c - cov_b * cov_b)
        inv_dist = 1.0 / jnp.sqrt(rel_x * rel_x + rel_y * rel_y + depth_z * depth_z)
        basis = sh_basis(rel_x * inv_dist, rel_y * inv_dist, depth_z * inv_dist)
        colours = []
        for channel in range(3):
            total = sh_c0 * coeffs[channel * SH] + 0.5
            for k in range(1, SH):
                total = total + coeffs[channel * SH + k] * basis[k]
            colours.append(jnp.maximum(total, 0.0))
        views.append(
            [
                ratio_u + centre_x,
                ratio_v + centre_y,
                cov_c * inv_det,
                -cov_b * inv_det,
                cov_a * inv_det,
                log_alpha,
            ]
            + colours
        )
    return views


def window_taps():
    raw_taps = [math.exp(-((tap_idx - RADIUS) ** 2) / 4.5) for tap_idx in range(2 * RADIUS + 1)]
    total = sum(raw_taps)
    return [tap / total for tap in raw_taps]


def band(out_count, in_count, offset):
    taps = window_taps()
    shape = (out_count, in_count)
    gap = lax.broadcasted_iota(jnp.int32, shape, 1) - lax.broadcasted_iota(jnp.int32, shape, 0)
    gap = jnp.abs(gap - offset)
    matrix = jnp.zeros(shape, f32)
    for far in range(RADIUS + 1):
        matrix = jnp.where(gap == far, taps[RADIUS + far], matrix)
    return matrix


def pieces(x, count):
    out = []
    for _ in range(count - 1):
        part = x.astype(bf16).astype(f32)
        out.append(part)
        x = x - part
    out.append(x)
    return out


def stack(x, count, axis=0):
    return jnp.concatenate(pieces(x, count), axis=axis).astype(bf16)


def dot(a, b):
    return lax.dot_general(a, b, (((1,), (0,)), ((), ())), preferred_element_type=f32)


def dot_t(a, b):
    return lax.dot_general(a, b, (((1,), (1,)), ((), ())), preferred_element_type=f32)


def dot_exact(a, b):
    return lax.dot_general(
        a, b, (((1,), (0,)), ((), ())), precision=lax.Precision.HIGHEST, preferred_element_type=f32
    )


def fold(x, count):
    size = x.shape[0] // count
    total = x[:size]
    for i in range(1, count):
        total = total + x[i * size : (i + 1) * size]
    return total


def loop(low, high, step):
    if high - low <= 8:
        for i in range(low, high):
            step(i)
    else:

        @pl.loop(low, high)
        def _(i):
            step(i)


def params(par, opacity):
    return (
        [par[:, 48 + i, :] for i in range(3)],
        [par[:, 56 + i, :] for i in range(4)],
        [par[:, 64 + i, :] for i in range(3)],
        opacity[...],
        [par[:, i, :] for i in range(48)],
    )


def pick_of(send, d, shard):
    local_row = lax.broadcasted_iota(jnp.int32, (shard, send.shape[2]), 0)
    return jnp.where(local_row == send[0, pl.ds(d, 1), :], 1.0, 0.0).astype(bf16)


def split_taps():
    high = [float(np.asarray(tap, ml_dtypes.bfloat16)) for tap in window_taps()]
    return high, [float(tap) - top for tap, top in zip(window_taps(), high)]


def band_split(out_count, in_rows, offset, axis):
    high, low = split_taps()
    count = len(in_rows)
    shape = (out_count, 3 * count) if axis == 1 else (3 * count, out_count)
    inner = lax.broadcasted_iota(jnp.int32, shape, axis)
    part = inner // count
    place = lax.rem(inner, count)
    start = in_rows[0]
    jump = [k for k in range(1, count) if in_rows[k] != in_rows[k - 1] + 1]
    row = place + start
    for k in jump:
        row = row + jnp.where(place >= k, in_rows[k] - in_rows[k - 1] - 1, 0)
    gap = jnp.abs(row - lax.broadcasted_iota(jnp.int32, shape, 1 - axis) - offset)
    matrix = jnp.zeros(shape, f32)
    for far in range(RADIUS + 1):
        tap = jnp.where(part == 2, low[RADIUS + far], high[RADIUS + far])
        matrix = jnp.where(gap == far, tap, matrix)
    return matrix.astype(bf16)


def stack_mixed(x, axis):
    high, low = pieces(x, 2)
    return jnp.concatenate([high, low, high], axis=axis).astype(bf16)


def side_by_side(x, count):
    size = x.shape[1] // count
    return jnp.concatenate([x[:, i * size : (i + 1) * size] for i in range(count)], axis=0)


def pad_rows(x):
    return jnp.concatenate([x, jnp.zeros((ROWS_MSG - x.shape[0], x.shape[1]), f32)], axis=0)


def flip(index, bits):
    bit = 1
    while bit <= bits:
        if bits & bit:
            index = index + bit * (1 - 2 * lax.rem(lax.div(index, bit), 2))
        bit *= 2
    return index


def spread_of(quats, log_scales):
    inv_norm = 1.0 / jnp.sqrt(
        quats[0] * quats[0] + quats[1] * quats[1] + quats[2] * quats[2] + quats[3] * quats[3]
    )
    w, x, y, z = [quat * inv_norm for quat in quats]
    rotation = [
        [1.0 - 2.0 * (y * y + z * z), 2.0 * (x * y - w * z), 2.0 * (x * z + w * y)],
        [2.0 * (x * y + w * z), 1.0 - 2.0 * (x * x + z * z), 2.0 * (y * z - w * x)],
        [2.0 * (x * z - w * y), 2.0 * (y * z + w * x), 1.0 - 2.0 * (x * x + y * y)],
    ]
    scales = [jnp.exp(log_scale) for log_scale in log_scales]
    return [[rotation[i][j] * scales[j] for j in range(3)] for i in range(3)]


def colours_of(coeffs, rel_x, rel_y, depth_z):
    inv_dist = 1.0 / jnp.sqrt(rel_x * rel_x + rel_y * rel_y + depth_z * depth_z)
    basis = sh_basis(rel_x * inv_dist, rel_y * inv_dist, depth_z * inv_dist)
    out = []
    for channel in range(3):
        total = sh_c0 * coeffs[channel * SH] + 0.5
        for k in range(1, SH):
            total = total + coeffs[channel * SH + k] * basis[k]
        out.append(total)
    return out, basis


N_KEPT = 45


def keep_view(kept, coeffs, spread, means, inv_depth, jac_diag, cam_x, cam_y):
    rel_x = means[0] - cam_x
    rel_y = means[1] - cam_y
    ratio_u = jac_diag * rel_x
    ratio_v = jac_diag * rel_y
    jac_u = -ratio_u * inv_depth
    jac_v = -ratio_v * inv_depth
    top = [jac_diag * spread[0][j] + jac_u * spread[2][j] for j in range(3)]
    low = [jac_diag * spread[1][j] + jac_v * spread[2][j] for j in range(3)]
    cov_a = top[0] * top[0] + top[1] * top[1] + top[2] * top[2] + cov_blur
    cov_b = top[0] * low[0] + top[1] * low[1] + top[2] * low[2]
    cov_c = low[0] * low[0] + low[1] * low[1] + low[2] * low[2] + cov_blur
    inv_det = 1.0 / (cov_a * cov_c - cov_b * cov_b)
    raw, pull, basis = jax.vjp(
        lambda x, y, z: colours_of(coeffs, x, y, z), rel_x, rel_y, means[2], has_aux=True
    )
    out = [rel_x, rel_y, ratio_u, ratio_v, jac_u, jac_v] + top + low
    out += [cov_c * inv_det, -cov_b * inv_det, cov_a * inv_det]
    zero = jnp.zeros_like(rel_x)
    one = jnp.ones_like(rel_x)
    for channel in range(3):
        out += pull([one if i == channel else zero for i in range(3)])
    out += [jnp.where(x > 0.0, 1.0, jnp.where(x == 0.0, 0.5, 0.0)) for x in raw]
    out += basis[1:]
    for i, x in enumerate(out):
        kept[i] = x


def pull_view(kept, cots, inv_depth, jac_diag, spread):
    rel_x, rel_y, ratio_u, ratio_v, jac_u, jac_v = [kept[i] for i in range(6)]
    top = [kept[6 + j] for j in range(3)]
    low = [kept[9 + j] for j in range(3)]
    k0, k1, k2 = [kept[12 + i] for i in range(3)]
    g0, g1, g2 = cots[2], cots[3], cots[4]
    cov_a = -(k0 * k0 * g0 + k0 * k1 * g1 + k1 * k1 * g2)
    cov_b = -2.0 * (k0 * k1 * g0 + k1 * k2 * g2) - (k0 * k2 + k1 * k1) * g1
    cov_c = -(k1 * k1 * g0 + k1 * k2 * g1 + k2 * k2 * g2)
    d_top = [2.0 * cov_a * top[j] + cov_b * low[j] for j in range(3)]
    d_low = [2.0 * cov_c * low[j] + cov_b * top[j] for j in range(3)]
    d_base = [jac_u * d_top[j] + jac_v * d_low[j] for j in range(3)]
    d_jac_u = d_top[0] * spread[2][0] + d_top[1] * spread[2][1] + d_top[2] * spread[2][2]
    d_jac_v = d_low[0] * spread[2][0] + d_low[1] * spread[2][1] + d_low[2] * spread[2][2]
    d_ratio_u = cots[0] - inv_depth * d_jac_u
    d_ratio_v = cots[1] - inv_depth * d_jac_v
    shades = [cots[6 + c] * kept[24 + c] for c in range(3)]
    turn = [
        shades[0] * kept[15 + i] + shades[1] * kept[18 + i] + shades[2] * kept[21 + i]
        for i in range(3)
    ]
    d_x = jac_diag * d_ratio_u + turn[0]
    d_y = jac_diag * d_ratio_v + turn[1]
    d_diag = rel_x * d_ratio_u + rel_y * d_ratio_v
    d_inv = -(ratio_u * d_jac_u + ratio_v * d_jac_v)
    return d_top + d_low + d_base + [d_x, d_y, turn[2], d_diag, d_inv, cots[5]], shades


def near_kernel(
    n_gs,
    n_view,
    means_in,
    quats_in,
    scales_in,
    opacity_in,
    sh_in,
    camera_in,
    targets_in,
    send_in,
    lists_in,
    lens_in,
    pic_out,
    means_out,
    quats_out,
    scales_out,
    opacity_out,
    sh_out,
    par,
    opacity,
    send,
    means,
    quats,
    scales,
    sh,
    camera,
    targets,
    lists,
    lens,
    cams,
    row_buf,
    msg_out,
    msg_in,
    slot_mask,
    slot_mask_t,
    row_mask,
    bases,
    tile_buf,
    ratio_buf,
    weight_buf,
    share_buf,
    split_buf,
    pic,
    halo,
    t_halo,
    cot,
    back_out,
    back_in,
    placed,
    kept,
    cot_views,
    g_sum,
    g_par,
    load_sems,
    send_cam,
    recv_cam,
    send_one,
    recv_one,
    send_halo,
    recv_halo,
    send_tgt,
    recv_tgt,
    send_two,
    recv_two,
    send_three,
    recv_three,
):
    loads = [
        pltpu.make_async_copy(src, dst, load_sems.at[k])
        for k, (src, dst) in enumerate(
            [
                (sh_in, sh),
                (means_in, means),
                (quats_in, quats),
                (scales_in, scales),
                (opacity_in, opacity),
                (camera_in, camera),
                (send_in, send),
                (lists_in.at[0, 0], lists),
                (lens_in.at[0], lens),
                (targets_in, targets),
            ]
        )
    ]
    for load in loads:
        load.start()
    gs = lax.axis_index("gs")
    view = lax.axis_index("view")
    shard = means.shape[1]
    chunks = shard // LANES
    cap = send.shape[2]
    tiles, list_size = lists.shape
    groups = n_view // 2
    core = lax.rem(view, 2)
    group = lax.div(view, 2)
    has_up = gs > 0
    has_down = gs < n_gs - 1
    near = range(1, n_gs)
    far = range(n_gs - 1, 0, -1)

    def cousin(j):
        return lax.rem(view + 2 * j, n_view)

    barrier = pltpu.get_barrier_semaphore()

    def greet(strip, cam):
        pl.semaphore_signal(barrier, inc=1, device_id=(strip, cam), device_id_type=MESH)

    for k in near:
        greet(flip(gs, k), view)
    for j in range(1, groups):
        for k in range(n_gs):
            greet(flip(gs, k), cousin(j))
    for j in range(groups):
        greet(gs, flip(cousin(j), 1))
    greeted = n_gs - 1 + (groups - 1) * n_gs + groups

    for load in loads[:7]:
        load.wait()

    for c in range(chunks):
        cols = slice(c * LANES, (c + 1) * LANES)
        par[c, 0:48, :] = sh[:, cols]
        par[c, 48:51, :] = means[:, cols]
        par[c, 56:60, :] = quats[:, cols]
        par[c, 64:67, :] = scales[:, cols]

    centre_x = 0.5 * tiles * TILE
    centre_y = 0.5 * n_gs * TILE
    cam_x = camera[0:1, 0:1]
    cam_y = camera[0:1, 1:2]
    rows = project(*params(par, opacity), [(cam_x, cam_y)], centre_x, centre_y)[0]
    row_buf[...] = jnp.zeros_like(row_buf)
    for i in range(9):
        row_buf[:, i, :] = rows[i]
    table = stack(jnp.concatenate([row_buf[c] for c in range(chunks)], axis=1), 3)

    def fill(d):
        msg_out[d] = fold(dot(table, pick_of(send, d, shard)), 3)[0:9]

    def first_copy(d, s):
        return pltpu.make_async_remote_copy(
            src_ref=msg_out.at[d],
            dst_ref=msg_in.at[s],
            send_sem=send_one.at[d],
            recv_sem=recv_one.at[s],
            device_id=(d, view),
            device_id_type=MESH,
        )

    pl.semaphore_wait(barrier, greeted)

    for k in far:
        fill(flip(gs, k))
        first_copy(flip(gs, k), gs).start()
    fill(gs)
    msg_in[gs] = msg_out[gs]

    def cam_copy(to, of):
        return pltpu.make_async_remote_copy(
            src_ref=cams.at[of],
            dst_ref=cams.at[of],
            send_sem=send_cam.at[to],
            recv_sem=recv_cam.at[of],
            device_id=(gs, to),
            device_id_type=MESH,
        )

    lane_one = lax.broadcasted_iota(jnp.int32, (1, LANES), 1)
    cams[view] = jnp.where(lane_one == 0, cam_x, cam_y)
    for k in range(1, n_view):
        cam_copy(lax.rem(view + k, n_view), view).start()

    def halo_copy(src, dst, sends, recvs, side):
        other = gs + 1 if side == 0 else gs - 1
        return pltpu.make_async_remote_copy(
            src_ref=src,
            dst_ref=dst.at[side],
            send_sem=sends.at[side],
            recv_sem=recvs.at[side],
            device_id=(other, view),
            device_id_type=MESH,
        )

    def exchange(src, dst, sends, recvs, start, ends=(False, True)):
        def act(copy, recv):
            if start:
                copy.start()
            elif recv:
                copy.wait_recv()
            else:
                copy.wait_send()

        for recv in ends:
            if start and recv:
                continue

            @pl.when(has_down)
            def _():
                act(halo_copy(src, dst, sends, recvs, 1 if recv else 0), recv)

            @pl.when(has_up)
            def _():
                act(halo_copy(src, dst, sends, recvs, 0 if recv else 1), recv)

    for load in loads[7:]:
        load.wait()
    exchange(targets.at[0], t_halo, send_tgt, recv_tgt, True)

    @pl.when(jnp.logical_not(has_up))
    def _():
        halo[0] = jnp.zeros_like(halo[0])
        t_halo[0] = jnp.zeros_like(t_halo[0])

    @pl.when(jnp.logical_not(has_down))
    def _():
        halo[1] = jnp.zeros_like(halo[1])
        t_halo[1] = jnp.zeros_like(t_halo[1])

    n_chunk, _, wide = weight_buf.shape
    width = tiles * TILE
    per = wide // width
    slot_row = lax.broadcasted_iota(jnp.int32, (cap, list_size), 0)
    for k in range(n_gs):
        here = slot_row + flip(gs, k) * cap
        for t in range(tiles):
            slot_mask[k, :, t * list_size : (t + 1) * list_size] = jnp.where(
                here == lists[t : t + 1, :], 1.0, 0.0
            ).astype(bf16)
    lists_t = jnp.transpose(lists[...].astype(f32))
    slot_lane = lax.broadcasted_iota(jnp.int32, (list_size, cap), 1)
    for t in range(tiles):
        listed = jnp.broadcast_to(lists_t[:, t : t + 1], (list_size, cap))
        for k in range(n_gs):
            here = (slot_lane + flip(gs, k) * cap).astype(f32)
            slot_mask_t[k, t * list_size : (t + 1) * list_size, :] = jnp.where(
                here == listed, 1.0, 0.0
            ).astype(bf16)

    lane = lax.broadcasted_iota(jnp.int32, (tiles, wide), 1)
    in_tile = lax.rem(lane, width) // TILE == lax.broadcasted_iota(jnp.int32, (tiles, wide), 0)
    off_q = (lax.rem(lane, TILE) - TILE // 2).astype(f32)
    half_r = (lane // width).astype(f32)
    for i in range(n_chunk):
        off_r = half_r + float(i * per - TILE // 2)
        out = [jnp.ones_like(off_q), off_q, off_r, off_q * off_q, off_q * off_r, off_r * off_r]
        bases[i] = jnp.concatenate([jnp.where(in_tile, x, 0.0) for x in out], axis=0).astype(bf16)
    shape = (list_size, 2 * list_size)
    list_row = lax.broadcasted_iota(jnp.int32, shape, 0)
    list_col = lax.rem(lax.broadcasted_iota(jnp.int32, shape, 1), list_size)
    prefix = jnp.where(list_col < list_row, 1.0, 0.0).astype(bf16)
    suffix = jnp.where(list_col > list_row, 1.0, 0.0).astype(bf16)
    for t in range(tiles):
        tile_buf[t] = jnp.zeros((ROWS_MSG, list_size), f32)

    def gather(k, s):
        got = fold(dot(stack(pad_rows(msg_in[s]), 3), slot_mask[k]), 3)
        for t in range(tiles):
            tile_buf[t] += got[:, t * list_size : (t + 1) * list_size]

    gather(0, gs)
    for k in near:
        s = flip(gs, k)
        first_copy(gs, s).wait_recv()
        gather(k, s)

    diagonal = lax.broadcasted_iota(jnp.int32, (tiles, tiles), 0) == lax.broadcasted_iota(
        jnp.int32, (tiles, tiles), 1
    )
    used = jnp.sum(jnp.where(diagonal, lens[...].astype(f32), 0.0), axis=1, keepdims=True)
    entry = lax.broadcasted_iota(jnp.int32, (tiles, list_size), 1)
    live = entry.astype(f32) < used
    mid_q = (lax.broadcasted_iota(jnp.int32, (tiles, list_size), 0) * TILE + TILE // 2).astype(f32)
    mid_r = (gs * TILE + TILE // 2).astype(f32)
    off_u = tile_buf[:, 0, :] - mid_q
    off_w = tile_buf[:, 1, :] - mid_r
    k0 = tile_buf[:, 2, :]
    k1 = tile_buf[:, 3, :]
    k2 = tile_buf[:, 4, :]
    lin_u = k0 * off_u + k1 * off_w
    lin_w = k2 * off_w + k1 * off_u
    terms = [
        jnp.where(live, tile_buf[:, 5, :] - 0.5 * (off_u * lin_u + off_w * lin_w), -10000.0),
        jnp.where(live, lin_u, 0.0),
        jnp.where(live, lin_w, 0.0),
        jnp.where(live, -0.5 * k0, 0.0),
        jnp.where(live, -k1, 0.0),
        jnp.where(live, -0.5 * k2, 0.0),
    ]
    term_t = jnp.transpose(jnp.concatenate(pieces(jnp.concatenate(terms, axis=0), 3), axis=0))
    term_t = term_t.astype(bf16)
    colour = jnp.concatenate([tile_buf[:, 6 + c, :] for c in range(3)], axis=0)
    col_hi, col_lo = pieces(colour, 2)
    col_two = jnp.concatenate([col_hi, col_lo], axis=0)
    col_wide = jnp.concatenate([col_two, col_two], axis=1).astype(bf16)
    col_t = jnp.transpose(jnp.concatenate([col_hi, col_lo, col_hi], axis=0)).astype(bf16)

    for i in range(n_chunk):
        base = bases[i]
        ratio_buf[i] = jnp.exp(dot(term_t, jnp.concatenate([base, base, base], axis=0)))
    for i in range(n_chunk):
        alpha = ratio_buf[i]
        weight = alpha * jnp.exp(dot(prefix, stack(jnp.log(1.0 - alpha), 2)))
        weight_buf[i] = weight
        split_buf[i] = stack(weight, 2)
    for i in range(n_chunk):
        drawn = fold(dot(col_wide, split_buf[i]), 2)
        for c in range(3):
            mine = jnp.where(in_tile, drawn[c * tiles : (c + 1) * tiles], 0.0)
            line = jnp.sum(mine, axis=0, keepdims=True)
            for half in range(per):
                row = i * per + half
                pic[c, row : row + 1, :] = line[:, half * width : (half + 1) * width]

    exchange(pic, halo, send_halo, recv_halo, True)
    pic_out[0] = pic[...]
    exchange(targets.at[0], t_halo, send_tgt, recv_tgt, False)
    tall = 2 * TILE
    across = band_split(width, list(range(width)), 0, 0)
    tgts = [
        jnp.concatenate([t_halo[0, c], targets[0, c], t_halo[1, c]], axis=0) for c in range(3)
    ]
    planes = []
    for c in range(3):
        planes += [tgts[c], tgts[c] * tgts[c]]
    rows_all = list(range(3 * TILE))
    band_all = band_split(tall, rows_all, TILE // 2, 1)
    down = dot(band_all, stack_mixed(jnp.concatenate(planes, axis=1), 0))
    blur_tgt = dot(stack_mixed(side_by_side(down, 6), 1), across)
    own = []
    for c in range(3):
        img = pic[c]
        own += [img, img * img, img * targets[0, c]]
    band_own = band_split(tall, rows_all[TILE : 2 * TILE], TILE // 2, 1)
    down_own = dot(band_own, stack_mixed(jnp.concatenate(own, axis=1), 0))
    band_far = band_split(tall, rows_all[:TILE] + rows_all[2 * TILE :], TILE // 2, 1)
    band_back = band_split(TILE, list(range(tall)), TILE // 2, 1)
    directs = []
    for c in range(3):
        res = pic[c] - targets[0, c]
        directs.append(
            (1.0 - ssim_weight) / (TILE * TILE) * res / jnp.sqrt(res * res + charb_eps)
        )
    for i in range(n_chunk):
        alpha = ratio_buf[i]
        ratio_buf[i] = alpha / (1.0 - alpha)
    exchange(pic, halo, send_halo, recv_halo, False)

    beyond = []
    for c in range(3):
        img = jnp.concatenate([halo[0, c], halo[1, c]], axis=0)
        tgt = jnp.concatenate([t_halo[0, c], t_halo[1, c]], axis=0)
        beyond += [img, img * img, img * tgt]
    down = down_own + dot(band_far, stack_mixed(jnp.concatenate(beyond, axis=1), 0))
    blurred = dot(stack_mixed(side_by_side(down, 9), 1), across)
    at_row = lax.broadcasted_iota(jnp.int32, (tall, width), 0) + gs * TILE - TILE // 2
    inside = jnp.logical_and(at_row >= 0, at_row < n_gs * TILE)
    scale = -ssim_weight / (TILE * TILE)
    cots = []
    for c in range(3):
        mean_x, raw_xx, raw_xy = [
            blurred[(3 * c + i) * tall : (3 * c + i + 1) * tall] for i in range(3)
        ]
        mean_y, raw_yy = [
            blur_tgt[(2 * c + i) * tall : (2 * c + i + 1) * tall] for i in range(2)
        ]
        top_a = 2.0 * mean_x * mean_y + ssim_one
        top_b = 2.0 * (raw_xy - mean_x * mean_y) + ssim_two
        low_c = mean_x * mean_x + mean_y * mean_y + ssim_one
        low_d = (raw_xx - mean_x * mean_x) + (raw_yy - mean_y * mean_y) + ssim_two
        inv_cd = 1.0 / (low_c * low_d)
        inv_dd = inv_cd * low_c
        ssim = top_a * top_b * inv_cd
        d_mean = 2.0 * mean_y * (top_b - top_a) * inv_cd - 2.0 * mean_x * ssim * (
            inv_cd * low_d - inv_dd
        )
        d_xx = -ssim * inv_dd
        d_xy = 2.0 * top_a * inv_cd
        cots += [jnp.where(inside, scale * part, 0.0) for part in (d_mean, d_xx, d_xy)]
    spread = dot(band_back, stack_mixed(jnp.concatenate(cots, axis=1), 0))
    spread = dot(stack_mixed(side_by_side(spread, 9), 1), across)
    grad_rows = []
    for c in range(3):
        s_mean, s_xx, s_xy = [spread[(3 * c + i) * TILE : (3 * c + i + 1) * TILE] for i in range(3)]
        grad_rows.append(directs[c] + s_mean + 2.0 * pic[c] * s_xx + targets[0, c] * s_xy)

    shades = []
    for i in range(n_chunk):
        parts = []
        for c in range(3):
            line = jnp.concatenate(
                [grad_rows[c][i * per + half : i * per + half + 1] for half in range(per)], axis=1
            )
            parts.append(jnp.where(in_tile, line, 0.0))
        hi, lo = pieces(jnp.concatenate(parts, axis=0), 2)
        shades.append(jnp.concatenate([hi, lo], axis=0).astype(bf16))
        shade = dot(col_t, jnp.concatenate([hi, hi, lo], axis=0).astype(bf16))
        share_buf[i] = weight_buf[i] * shade
    for i in range(n_chunk):
        share = share_buf[i]
        share_buf[i] = share - ratio_buf[i] * dot(suffix, stack(share, 2))
    d_terms = jnp.zeros((6 * tiles, 2 * list_size), f32)
    d_colour = jnp.zeros((6 * tiles, 2 * list_size), f32)
    for i in range(n_chunk):
        d_terms = d_terms + dot_t(bases[i], stack(share_buf[i], 2))
        d_colour = d_colour + dot_t(shades[i], split_buf[i])
    d_terms = d_terms[:, :list_size] + d_terms[:, list_size:]
    d_colour = fold(d_colour[:, :list_size] + d_colour[:, list_size:], 2)

    d0, d1, d2, d3, d4, d5 = [d_terms[k * tiles : (k + 1) * tiles] for k in range(6)]
    e1 = d1 - off_u * d0
    e2 = d2 - off_w * d0
    cot[...] = jnp.zeros_like(cot)
    cot[:, 0, :] = k0 * e1 + k1 * e2
    cot[:, 1, :] = k2 * e2 + k1 * e1
    cot[:, 2, :] = -0.5 * d3 + off_u * (d1 - 0.5 * off_u * d0)
    cot[:, 3, :] = off_w * e1 + off_u * d2 - d4
    cot[:, 4, :] = -0.5 * d5 + off_w * (d2 - 0.5 * off_w * d0)
    cot[:, 5, :] = d0
    for c in range(3):
        cot[:, 6 + c, :] = d_colour[c * tiles : (c + 1) * tiles]
    cots = jnp.concatenate([stack(cot[t], 2) for t in range(tiles)], axis=1)

    def out_copy(j, d):
        return pltpu.make_async_remote_copy(
            src_ref=back_out.at[d],
            dst_ref=back_in.at[group, gs],
            send_sem=send_two.at[j, d],
            recv_sem=recv_two.at[group, gs],
            device_id=(d, cousin(j)),
            device_id_type=MESH,
        )

    def in_copy(j, s):
        of = lax.div(cousin(j), 2)
        return pltpu.make_async_remote_copy(
            src_ref=back_out.at[s],
            dst_ref=back_in.at[of, s],
            send_sem=send_two.at[j, s],
            recv_sem=recv_two.at[of, s],
            device_id=(s, cousin(j)),
            device_id_type=MESH,
        )

    for k in list(far) + [0]:
        d = flip(gs, k)
        back_out[d] = fold(dot(cots, slot_mask_t[k]), 2)[0:9]
        for j in range(groups):
            if k or j:
                out_copy(j, d).start()
    back_in[group, gs] = back_out[gs]

    send_t = jnp.transpose(send[0].astype(f32))
    shard_lane = lax.broadcasted_iota(jnp.int32, (cap, shard), 1).astype(f32)
    for s in range(n_gs):
        row_mask[s] = jnp.where(shard_lane == send_t[:, s : s + 1], 1.0, 0.0).astype(bf16)
    for k in range(1, n_view):
        cam_copy(view, lax.rem(view + n_view - k, n_view)).wait_recv()
    p_means, p_quats, p_scales, p_opacity, p_coeffs = params(par, opacity)
    spread, pull_spread = jax.vjp(spread_of, p_quats, p_scales)
    inv_depth = 1.0 / p_means[2]
    jac_diag = focal_length * inv_depth
    for h in range(2):
        for j in range(groups):
            of = 2 * j + (core if h == 0 else 1 - core)
            at = cams[of]
            keep_view(
                kept.at[h, j], p_coeffs, spread, p_means, inv_depth, jac_diag, at[:, 0:1], at[:, 1:2]
            )

    placed[...] = jnp.zeros_like(placed)

    def put_back(s):
        both = [stack(pad_rows(back_in[j, s]), 2) for j in range(groups)]
        placed[...] += dot(jnp.concatenate(both, axis=0), row_mask[s])

    for k in range(n_gs):
        s = flip(gs, k)
        for j in range(groups):
            if k or j:
                in_copy(j, s).wait_recv()
        put_back(s)
    for j in range(groups):
        mine = fold(placed[2 * ROWS_MSG * j : 2 * ROWS_MSG * (j + 1)], 2)
        for c in range(chunks):
            cot_views[core, j, :, c, :] = mine[0:9, c * LANES : (c + 1) * LANES]

    def third_copy(of):
        return pltpu.make_async_remote_copy(
            src_ref=cot_views.at[of],
            dst_ref=cot_views.at[of],
            send_sem=send_three.at[0],
            recv_sem=recv_three.at[0],
            device_id=(gs, flip(view, 1)),
            device_id_type=MESH,
        )

    third_copy(core).start()

    def pull_half(h):
        side = core if h == 0 else 1 - core
        total = None
        tints = []
        for j in range(groups):
            cots = [cot_views[side, j, i] for i in range(9)]
            got, shades = pull_view(kept.at[h, j], cots, inv_depth, jac_diag, spread)
            total = got if total is None else [a + b for a, b in zip(total, got)]
            tints.append(shades)
        for i in range(15):
            if h == 0:
                g_sum[i] = total[i]
            else:
                total[i] = total[i] + g_sum[i]
        for k in range(SH):
            for c in range(3):
                part = None
                for j in range(groups):
                    term = tints[j][c] * (sh_c0 if k == 0 else kept[h, j, 26 + k])
                    part = term if part is None else part + term
                if h == 1:
                    part = part + g_par[:, c * SH + k, :]
                g_par[:, c * SH + k, :] = part
        return total

    pull_half(0)
    third_copy(1 - core).wait_recv()
    total = pull_half(1)
    d_top, d_low, d_base = total[0:3], total[3:6], total[6:9]
    d_x, d_y, d_z, d_diag, d_inv, d_log = total[9:15]
    for j in range(3):
        d_diag = d_diag + d_top[j] * spread[0][j] + d_low[j] * spread[1][j]
    d_inv = d_inv + focal_length * d_diag
    d_z = d_z - inv_depth * inv_depth * d_inv
    d_quats, d_scales = pull_spread(
        [[jac_diag * x for x in d_top], [jac_diag * x for x in d_low], list(d_base)]
    )
    decay = jnp.exp(-p_opacity)
    opacity_out[...] = d_log * decay / (1.0 + decay)
    for i, x in enumerate([d_x, d_y, d_z]):
        g_par[:, 48 + i, :] = x
    for i in range(4):
        g_par[:, 56 + i, :] = d_quats[i]
    for i in range(3):
        g_par[:, 64 + i, :] = d_scales[i]
    for c in range(chunks):
        cols = slice(c * LANES, (c + 1) * LANES)
        sh_out[:, cols] = g_par[c, 0:48, :]
        means_out[:, cols] = g_par[c, 48:51, :]
        quats_out[:, cols] = g_par[c, 56:60, :]
        scales_out[:, cols] = g_par[c, 64:67, :]

    for k in near:
        first_copy(flip(gs, k), gs).wait_send()
    for k in range(1, n_view):
        cam_copy(lax.rem(view + k, n_view), view).wait_send()
    for k in range(n_gs):
        for j in range(groups):
            if k or j:
                out_copy(j, flip(gs, k)).wait_send()
    third_copy(core).wait_send()


def store_kernel(*refs):
    count = len(refs) // 2
    sources, places, sems = refs[:count], refs[count : 2 * count], refs[-1]
    stores = [
        pltpu.make_async_copy(src, dst, sems.at[k])
        for k, (src, dst) in enumerate(zip(sources, places))
    ]
    for store in stores:
        store.start()
    for store in stores:
        store.wait()


def far_kernel(
    n_gs,
    n_view,
    means_in,
    quats_in,
    scales_in,
    opacity_in,
    sh_in,
    camera_in,
    targets_in,
    send_in,
    lists_in,
    lens_in,
    pic_out,
    views_out,
    par,
    opacity,
    send,
    means,
    quats,
    scales,
    sh,
    camera,
    targets,
    lists,
    lens,
    row_buf,
    msg_out,
    msg_in,
    tile_buf,
    ratio_buf,
    weight_buf,
    pic,
    halo,
    t_halo,
    cot,
    back_out,
    back_in,
    placed,
    load_sems,
    send_one,
    recv_one,
    send_halo,
    recv_halo,
    send_tgt,
    recv_tgt,
    send_two,
    recv_two,
    send_three,
    recv_three,
):
    loads = [
        pltpu.make_async_copy(src, dst, load_sems.at[k])
        for k, (src, dst) in enumerate(
            [
                (sh_in, sh),
                (means_in, means),
                (quats_in, quats),
                (scales_in, scales),
                (opacity_in, opacity),
                (camera_in, camera),
                (send_in, send),
                (targets_in, targets),
                (lists_in.at[0, 0], lists),
                (lens_in.at[0], lens),
            ]
        )
    ]
    for load in loads:
        load.start()
    gs = lax.axis_index("gs")
    view = lax.axis_index("view")
    chunks = means.shape[1] // LANES
    cap = send.shape[2]
    shard = means.shape[1]
    tiles = lists.shape[0]
    list_size = lists.shape[1]
    has_up = gs > 0
    has_down = gs < n_gs - 1

    barrier = pltpu.get_barrier_semaphore()

    def greet(strip, cam):
        pl.semaphore_signal(barrier, inc=1, device_id=(strip, cam), device_id_type=MESH)

    loop(1, n_gs, lambda k: greet(lax.rem(gs + k, n_gs), view))
    loop(1, n_view, lambda k: greet(gs, lax.rem(view + k, n_view)))

    for load in loads:
        load.wait()

    for c in range(chunks):
        cols = slice(c * LANES, (c + 1) * LANES)
        par[c, 0:48, :] = sh[:, cols]
        par[c, 48:51, :] = means[:, cols]
        par[c, 56:60, :] = quats[:, cols]
        par[c, 64:67, :] = scales[:, cols]

    centre_x = 0.5 * tiles * TILE
    centre_y = 0.5 * n_gs * TILE
    cam_x = camera[0:1, 0:1]
    cam_y = camera[0:1, 1:2]
    rows = project(*params(par, opacity), [(cam_x, cam_y)], centre_x, centre_y)[0]
    row_buf[...] = jnp.zeros_like(row_buf)
    for i in range(9):
        row_buf[:, i, :] = rows[i]
    table = stack(jnp.concatenate([row_buf[c] for c in range(chunks)], axis=1), 3)

    def fill(d):
        msg_out[d] = fold(dot(table, pick_of(send, d, shard)), 3)

    def first_copy(d, s):
        return pltpu.make_async_remote_copy(
            src_ref=msg_out.at[d],
            dst_ref=msg_in.at[s],
            send_sem=send_one.at[d],
            recv_sem=recv_one.at[s],
            device_id=(d, view),
            device_id_type=MESH,
        )

    pl.semaphore_wait(barrier, n_gs + n_view - 2)

    def send_first(k):
        d = lax.rem(gs + k, n_gs)
        fill(d)
        first_copy(d, gs).start()

    loop(1, n_gs, send_first)
    fill(gs)
    msg_in[gs] = msg_out[gs]

    def halo_copy(src, dst, sends, recvs, side):
        other = gs + 1 if side == 0 else gs - 1
        return pltpu.make_async_remote_copy(
            src_ref=src,
            dst_ref=dst.at[side],
            send_sem=sends.at[side],
            recv_sem=recvs.at[side],
            device_id=(other, view),
            device_id_type=MESH,
        )

    def exchange(src, dst, sends, recvs, start):
        def act(copy, recv):
            if start:
                if not recv:
                    copy.start()
            elif recv:
                copy.wait_recv()
            else:
                copy.wait_send()

        for recv in (False, True):
            if start and recv:
                continue

            @pl.when(has_down)
            def _():
                act(halo_copy(src, dst, sends, recvs, 1 if recv else 0), recv)

            @pl.when(has_up)
            def _():
                act(halo_copy(src, dst, sends, recvs, 0 if recv else 1), recv)

    exchange(targets.at[0], t_halo, send_tgt, recv_tgt, True)

    @pl.when(jnp.logical_not(has_up))
    def _():
        halo[0] = jnp.zeros_like(halo[0])
        t_halo[0] = jnp.zeros_like(t_halo[0])

    @pl.when(jnp.logical_not(has_down))
    def _():
        halo[1] = jnp.zeros_like(halo[1])
        t_halo[1] = jnp.zeros_like(t_halo[1])


    slot_row = lax.broadcasted_iota(jnp.int32, (cap, list_size), 0)

    def slot_pick(s, t):
        return jnp.where(slot_row + s * cap == lists[t : t + 1, :], 1.0, 0.0).astype(bf16)

    tile_buf[...] = jnp.zeros_like(tile_buf)

    def gather(s):
        got = stack(msg_in[s], 3)
        for t in range(tiles):
            tile_buf[t] += fold(dot(got, slot_pick(s, t)), 3)

    gather(gs)

    def gather_next(k):
        s = lax.rem(gs + n_gs - k, n_gs)
        first_copy(gs, s).wait_recv()
        gather(s)

    loop(1, n_gs, gather_next)

    diagonal = lax.broadcasted_iota(jnp.int32, (tiles, tiles), 0) == lax.broadcasted_iota(
        jnp.int32, (tiles, tiles), 1
    )
    used = jnp.sum(jnp.where(diagonal, lens[...].astype(f32), 0.0), axis=1, keepdims=True)
    entry = lax.broadcasted_iota(jnp.int32, (tiles, list_size), 1)
    live = entry.astype(f32) < used
    mid_q = (lax.broadcasted_iota(jnp.int32, (tiles, list_size), 0) * TILE + TILE // 2).astype(f32)
    mid_r = (gs * TILE + TILE // 2).astype(f32)
    off_u = tile_buf[:, 0, :] - mid_q
    off_w = tile_buf[:, 1, :] - mid_r
    k0 = tile_buf[:, 2, :]
    k1 = tile_buf[:, 3, :]
    k2 = tile_buf[:, 4, :]
    lin_u = k0 * off_u + k1 * off_w
    lin_w = k2 * off_w + k1 * off_u
    terms = [
        jnp.where(live, tile_buf[:, 5, :] - 0.5 * (off_u * lin_u + off_w * lin_w), -10000.0),
        jnp.where(live, lin_u, 0.0),
        jnp.where(live, lin_w, 0.0),
        jnp.where(live, -0.5 * k0, 0.0),
        jnp.where(live, -k1, 0.0),
        jnp.where(live, -0.5 * k2, 0.0),
    ]
    term_t = jnp.transpose(jnp.concatenate(pieces(jnp.concatenate(terms, axis=0), 3), axis=0))
    term_t = term_t.astype(bf16)
    colour = jnp.concatenate([tile_buf[:, 6 + c, :] for c in range(3)], axis=0)
    col_hi, col_lo = pieces(colour, 2)
    col_two = jnp.concatenate([col_hi, col_lo], axis=0)
    col_wide = jnp.concatenate([col_two, col_two], axis=1).astype(bf16)
    col_t = jnp.transpose(jnp.concatenate([col_hi, col_lo, col_hi], axis=0)).astype(bf16)

    n_chunk, _, wide = weight_buf.shape
    width = tiles * TILE
    lane = lax.broadcasted_iota(jnp.int32, (tiles, wide), 1)
    in_tile = lax.rem(lane, width) // TILE == lax.broadcasted_iota(jnp.int32, (tiles, wide), 0)

    off_q = (lax.rem(lane, TILE) - TILE // 2).astype(f32)
    half_r = (lane // width).astype(f32)

    def basis(i):
        off_r = half_r + float(i * (wide // width) - TILE // 2)
        out = [jnp.ones_like(off_q), off_q, off_r, off_q * off_q, off_q * off_r, off_r * off_r]
        return jnp.concatenate([jnp.where(in_tile, x, 0.0) for x in out], axis=0).astype(bf16)

    shape = (list_size, 2 * list_size)
    list_row = lax.broadcasted_iota(jnp.int32, shape, 0)
    list_col = lax.rem(lax.broadcasted_iota(jnp.int32, shape, 1), list_size)
    prefix = jnp.where(list_col < list_row, 1.0, 0.0).astype(bf16)
    suffix = jnp.where(list_col > list_row, 1.0, 0.0).astype(bf16)

    for i in range(n_chunk):
        base = basis(i)
        alpha = jnp.exp(dot(term_t, jnp.concatenate([base, base, base], axis=0)))
        keep = 1.0 - alpha
        weight = alpha * jnp.exp(dot(prefix, stack(jnp.log(keep), 2)))
        ratio_buf[i] = alpha / keep
        weight_buf[i] = weight
        drawn = fold(dot(col_wide, stack(weight, 2)), 2)
        for c in range(3):
            mine = jnp.where(in_tile, drawn[c * tiles : (c + 1) * tiles], 0.0)
            line = jnp.sum(mine, axis=0, keepdims=True)
            for half in range(wide // width):
                row = i * (wide // width) + half
                pic[c, row : row + 1, :] = line[:, half * width : (half + 1) * width]

    exchange(pic, halo, send_halo, recv_halo, True)
    pic_out[0] = pic[...]
    exchange(targets.at[0], t_halo, send_tgt, recv_tgt, False)
    exchange(pic, halo, send_halo, recv_halo, False)

    tall = 2 * TILE
    across = band(width, width, 0)
    stacked = []
    images = []
    for c in range(3):
        img = jnp.concatenate([halo[0, c], pic[c], halo[1, c]], axis=0)
        tgt = jnp.concatenate([t_halo[0, c], targets[0, c], t_halo[1, c]], axis=0)
        images.append((img, tgt))
        stacked += [img, tgt, img * img, tgt * tgt, img * tgt]
    down = dot_exact(band(tall, 3 * TILE, TILE // 2), jnp.concatenate(stacked, axis=1))
    down = jnp.concatenate([down[:, i * width : (i + 1) * width] for i in range(15)], axis=0)
    blurred = dot_exact(down, across)
    at_row = lax.broadcasted_iota(jnp.int32, (tall, width), 0) + gs * TILE - TILE // 2
    inside = jnp.logical_and(at_row >= 0, at_row < n_gs * TILE)
    scale = -ssim_weight / (TILE * TILE)
    cots = []
    for c in range(3):
        mean_x, mean_y, raw_xx, raw_yy, raw_xy = [
            blurred[(5 * c + i) * tall : (5 * c + i + 1) * tall] for i in range(5)
        ]
        top_a = 2.0 * mean_x * mean_y + ssim_one
        top_b = 2.0 * (raw_xy - mean_x * mean_y) + ssim_two
        low_c = mean_x * mean_x + mean_y * mean_y + ssim_one
        low_d = (raw_xx - mean_x * mean_x) + (raw_yy - mean_y * mean_y) + ssim_two
        inv_cd = 1.0 / (low_c * low_d)
        inv_dd = inv_cd * low_c
        ssim = top_a * top_b * inv_cd
        d_mean = 2.0 * mean_y * (top_b - top_a) * inv_cd - 2.0 * mean_x * ssim * (
            inv_cd * low_d - inv_dd
        )
        d_xx = -ssim * inv_dd
        d_xy = 2.0 * top_a * inv_cd
        cots += [jnp.where(inside, scale * part, 0.0) for part in (d_mean, d_xx, d_xy)]
    spread = dot_exact(band(TILE, tall, TILE // 2), jnp.concatenate(cots, axis=1))
    spread = jnp.concatenate([spread[:, i * width : (i + 1) * width] for i in range(9)], axis=0)
    spread = dot_exact(spread, across)
    grad_rows = []
    for c in range(3):
        img = pic[c]
        tgt = targets[0, c]
        s_mean, s_xx, s_xy = [spread[(3 * c + i) * TILE : (3 * c + i + 1) * TILE] for i in range(3)]
        res = img - tgt
        direct = (1.0 - ssim_weight) / (TILE * TILE) * res / jnp.sqrt(res * res + charb_eps)
        grad_rows.append(direct + s_mean + 2.0 * img * s_xx + tgt * s_xy)

    d_terms = jnp.zeros((6 * tiles, list_size), f32)
    d_colour = jnp.zeros((3 * tiles, list_size), f32)
    for i in range(n_chunk):
        per = wide // width
        parts = []
        for c in range(3):
            line = jnp.concatenate(
                [grad_rows[c][i * per + half : i * per + half + 1] for half in range(per)], axis=1
            )
            parts.append(jnp.where(in_tile, line, 0.0))
        hi, lo = pieces(jnp.concatenate(parts, axis=0), 2)
        shade = dot(col_t, jnp.concatenate([hi, hi, lo], axis=0).astype(bf16))
        weight = weight_buf[i]
        share = weight * shade
        d_power = share - ratio_buf[i] * dot(suffix, stack(share, 2))
        both = dot_t(basis(i), stack(d_power, 2))
        d_terms = d_terms + both[:, :list_size] + both[:, list_size:]
        both = fold(dot_t(jnp.concatenate([hi, lo], axis=0).astype(bf16), stack(weight, 2)), 2)
        d_colour = d_colour + both[:, :list_size] + both[:, list_size:]

    d0, d1, d2, d3, d4, d5 = [d_terms[k * tiles : (k + 1) * tiles] for k in range(6)]
    e1 = d1 - off_u * d0
    e2 = d2 - off_w * d0
    cot[...] = jnp.zeros_like(cot)
    cot[:, 0, :] = k0 * e1 + k1 * e2
    cot[:, 1, :] = k2 * e2 + k1 * e1
    cot[:, 2, :] = -0.5 * d3 + off_u * (d1 - 0.5 * off_u * d0)
    cot[:, 3, :] = off_w * e1 + off_u * d2 - d4
    cot[:, 4, :] = -0.5 * d5 + off_w * (d2 - 0.5 * off_w * d0)
    cot[:, 5, :] = d0
    for c in range(3):
        cot[:, 6 + c, :] = d_colour[c * tiles : (c + 1) * tiles]
    cot_pieces = [stack(cot[t], 3) for t in range(tiles)]

    def scatter(s):
        total = jnp.zeros((3 * ROWS_MSG, cap), f32)
        for t in range(tiles):
            total = total + dot_t(cot_pieces[t], slot_pick(s, t))
        back_out[s] = fold(total, 3)

    def second_copy(d, s):
        return pltpu.make_async_remote_copy(
            src_ref=back_out.at[d],
            dst_ref=back_in.at[s],
            send_sem=send_two.at[d],
            recv_sem=recv_two.at[s],
            device_id=(d, view),
            device_id_type=MESH,
        )

    def send_second(k):
        d = lax.rem(gs + k, n_gs)
        scatter(d)
        second_copy(d, gs).start()

    loop(1, n_gs, send_second)
    scatter(gs)
    back_in[gs] = back_out[gs]
    placed[...] = jnp.zeros_like(placed)

    def put_back(s):
        placed[...] += dot_t(stack(back_in[s], 3), pick_of(send, s, shard))

    put_back(gs)

    def put_next(k):
        s = lax.rem(gs + n_gs - k, n_gs)
        second_copy(gs, s).wait_recv()
        put_back(s)

    loop(1, n_gs, put_next)
    whole = fold(placed[...], 3)
    for c in range(chunks):
        views_out[view, 0:9, c, :] = whole[0:9, c * LANES : (c + 1) * LANES]
    first_row = lax.broadcasted_iota(jnp.int32, (chunks, LANES), 0) == 0
    views_out[view, 9] = jnp.where(first_row, cam_x, cam_y)

    def third_copy(to, of):
        return pltpu.make_async_remote_copy(
            src_ref=views_out.at[of],
            dst_ref=views_out.at[of],
            send_sem=send_three.at[to],
            recv_sem=recv_three.at[of],
            device_id=(gs, to),
            device_id_type=MESH,
        )

    def send_third(k):
        third_copy(lax.rem(view + k, n_view), view).start()

    def wait_third(k):
        third_copy(view, lax.rem(view + n_view - k, n_view)).wait_recv()

    loop(1, n_view, send_third)
    loop(1, n_view, wait_third)

    def done_first(k):
        first_copy(lax.rem(gs + k, n_gs), gs).wait_send()
        second_copy(lax.rem(gs + k, n_gs), gs).wait_send()

    def done_third(k):
        third_copy(lax.rem(view + k, n_view), view).wait_send()

    loop(1, n_gs, done_first)
    loop(1, n_view, done_third)


def pull_kernel(
    n_view,
    pic,
    views,
    par,
    opacity,
    pic_out,
    means_out,
    quats_out,
    scales_out,
    opacity_out,
    sh_out,
    g_par,
    g_means,
    g_quats,
    g_scales,
    g_opacity,
    g_sh,
    store_sems,
):
    chunks = par.shape[0]
    pic_copy = pltpu.make_async_copy(pic, pic_out, store_sems.at[0])
    pic_copy.start()
    cams = [(views[v, 9, 0:1, 0:1], views[v, 9, 1:2, 0:1]) for v in range(n_view)]
    _, pull = jax.vjp(lambda *args: project(*args, cams, 0.0, 0.0), *params(par, opacity))
    grads = pull([[views[v, i] for i in range(9)] for v in range(n_view)])
    for i in range(3):
        g_par[:, 48 + i, :] = grads[0][i]
        g_par[:, 64 + i, :] = grads[2][i]
    for i in range(4):
        g_par[:, 56 + i, :] = grads[1][i]
    for i in range(48):
        g_par[:, i, :] = grads[4][i]
    g_opacity[...] = grads[3]
    for c in range(chunks):
        cols = slice(c * LANES, (c + 1) * LANES)
        g_sh[:, cols] = g_par[c, 0:48, :]
        g_means[:, cols] = g_par[c, 48:51, :]
        g_quats[:, cols] = g_par[c, 56:60, :]
        g_scales[:, cols] = g_par[c, 64:67, :]
    stores = [
        pltpu.make_async_copy(src, dst, store_sems.at[k + 1])
        for k, (src, dst) in enumerate(
            [
                (g_sh, sh_out),
                (g_means, means_out),
                (g_quats, quats_out),
                (g_scales, scales_out),
                (g_opacity, opacity_out),
            ]
        )
    ]
    for store in stores:
        store.start()
    pic_copy.wait()
    for store in stores:
        store.wait()


def far_shards(
    means, quats, log_scales, opacity, sh_coeffs, cameras, targets, send_rows, tile_lists, list_lengths
):
    n_gs = lax.axis_size("gs")
    n_view = lax.axis_size("view")
    shard = means.shape[1]
    chunks = shard // LANES
    cap = send_rows.shape[2]
    tiles, list_size = tile_lists.shape[2:]
    width = tiles * TILE
    n_chunk = TILE // 2
    wide = 2 * width
    opacity = opacity.reshape(chunks, LANES)
    args = (
        means,
        quats,
        log_scales,
        opacity,
        sh_coeffs,
        cameras,
        targets,
        send_rows,
        tile_lists,
        list_lengths,
    )
    shape = jax.ShapeDtypeStruct
    dma = pltpu.SemaphoreType.DMA
    vmem = pl.BlockSpec(memory_space=VMEM)
    hbm = pl.BlockSpec(memory_space=pltpu.HBM)
    mids = pl.pallas_call(
        lambda *refs: far_kernel(n_gs, n_view, *refs),
        out_shape=(
            shape(targets.shape, f32),
            shape((n_view, 10, chunks, LANES), f32),
            shape((chunks, 72, LANES), f32),
            shape((chunks, LANES), f32),
        ),
        in_specs=[hbm] * len(args),
        out_specs=(vmem,) * 4,
        scratch_shapes=[
            VMEM(send_rows.shape, jnp.int32),
            VMEM(means.shape, f32),
            VMEM(quats.shape, f32),
            VMEM(log_scales.shape, f32),
            VMEM(sh_coeffs.shape, f32),
            VMEM(cameras.shape, f32),
            VMEM(targets.shape, f32),
            VMEM((tiles, list_size), jnp.int32),
            VMEM((1, tiles), jnp.int32),
            VMEM((chunks, ROWS_MSG, LANES), f32),
            VMEM((n_gs, ROWS_MSG, cap), f32),
            VMEM((n_gs, ROWS_MSG, cap), f32),
            VMEM((tiles, ROWS_MSG, list_size), f32),
            VMEM((n_chunk, list_size, wide), f32),
            VMEM((n_chunk, list_size, wide), f32),
            VMEM((3, TILE, width), f32),
            VMEM((2, 3, TILE, width), f32),
            VMEM((2, 3, TILE, width), f32),
            VMEM((tiles, ROWS_MSG, list_size), f32),
            VMEM((n_gs, ROWS_MSG, cap), f32),
            VMEM((n_gs, ROWS_MSG, cap), f32),
            VMEM((3 * ROWS_MSG, shard), f32),
            dma((10,)),
            dma((n_gs,)),
            dma((n_gs,)),
            dma((2,)),
            dma((2,)),
            dma((2,)),
            dma((2,)),
            dma((n_gs,)),
            dma((n_gs,)),
            dma((n_view,)),
            dma((n_view,)),
        ],
        compiler_params=pltpu.CompilerParams(
            collective_id=0, has_side_effects=True, vmem_limit_bytes=48 * 1024 * 1024
        ),
    )(*[pltpu.with_memory_space_constraint(x, pltpu.HBM) for x in args])
    outs = pl.pallas_call(
        lambda *refs: pull_kernel(n_view, *refs),
        out_shape=(
            shape(targets.shape, f32),
            shape(means.shape, f32),
            shape(quats.shape, f32),
            shape(log_scales.shape, f32),
            shape((chunks, LANES), f32),
            shape(sh_coeffs.shape, f32),
        ),
        in_specs=[vmem] * 4,
        out_specs=(hbm,) * 6,
        scratch_shapes=[
            VMEM((chunks, 72, LANES), f32),
            VMEM(means.shape, f32),
            VMEM(quats.shape, f32),
            VMEM(log_scales.shape, f32),
            VMEM((chunks, LANES), f32),
            VMEM(sh_coeffs.shape, f32),
            dma((6,)),
        ],
        compiler_params=pltpu.CompilerParams(vmem_limit_bytes=48 * 1024 * 1024),
    )(*mids)
    return (*outs[:4], outs[4].reshape(shard), outs[5])


def shards(
    means, quats, log_scales, opacity, sh_coeffs, cameras, targets, send_rows, tile_lists, list_lengths
):
    n_gs = lax.axis_size("gs")
    n_view = lax.axis_size("view")
    shard = means.shape[1]
    cap = send_rows.shape[2]
    args = (
        means,
        quats,
        log_scales,
        opacity,
        sh_coeffs,
        cameras,
        targets,
        send_rows,
        tile_lists,
        list_lengths,
    )
    if n_gs not in (2, 4, 8) or cap % LANES or n_view % 2:
        return far_shards(*args)
    chunks = shard // LANES
    tiles, list_size = tile_lists.shape[2:]
    width = tiles * TILE
    n_chunk = TILE // 2
    wide = 2 * width
    groups = n_view // 2
    args = args[:3] + (opacity.reshape(chunks, LANES),) + args[4:]
    shape = jax.ShapeDtypeStruct
    dma = pltpu.SemaphoreType.DMA
    vmem = pl.BlockSpec(memory_space=VMEM)
    hbm = pl.BlockSpec(memory_space=pltpu.HBM)
    out_shape = (
        shape(targets.shape, f32),
        shape(means.shape, f32),
        shape(quats.shape, f32),
        shape(log_scales.shape, f32),
        shape((chunks, LANES), f32),
        shape(sh_coeffs.shape, f32),
    )
    mids = pl.pallas_call(
        lambda *refs: near_kernel(n_gs, n_view, *refs),
        out_shape=out_shape,
        in_specs=[hbm] * len(args),
        out_specs=(vmem,) * 6,
        scratch_shapes=[
            VMEM((chunks, 72, LANES), f32),
            VMEM((chunks, LANES), f32),
            VMEM(send_rows.shape, jnp.int32),
            VMEM(means.shape, f32),
            VMEM(quats.shape, f32),
            VMEM(log_scales.shape, f32),
            VMEM(sh_coeffs.shape, f32),
            VMEM(cameras.shape, f32),
            VMEM(targets.shape, f32),
            VMEM((tiles, list_size), jnp.int32),
            VMEM((1, tiles), jnp.int32),
            VMEM((n_view, 1, LANES), f32),
            VMEM((chunks, ROWS_MSG, LANES), f32),
            VMEM((n_gs, 9, cap), f32),
            VMEM((n_gs, 9, cap), f32),
            VMEM((n_gs, cap, tiles * list_size), bf16),
            VMEM((n_gs, tiles * list_size, cap), bf16),
            VMEM((n_gs, cap, shard), bf16),
            VMEM((n_chunk, 6 * tiles, wide), bf16),
            VMEM((tiles, ROWS_MSG, list_size), f32),
            VMEM((n_chunk, list_size, wide), f32),
            VMEM((n_chunk, list_size, wide), f32),
            VMEM((n_chunk, list_size, wide), f32),
            VMEM((n_chunk, 2 * list_size, wide), bf16),
            VMEM((3, TILE, width), f32),
            VMEM((2, 3, TILE, width), f32),
            VMEM((2, 3, TILE, width), f32),
            VMEM((tiles, ROWS_MSG, list_size), f32),
            VMEM((n_gs, 9, cap), f32),
            VMEM((groups, n_gs, 9, cap), f32),
            VMEM((2 * ROWS_MSG * groups, shard), f32),
            VMEM((2, groups, N_KEPT, chunks, LANES), f32),
            VMEM((2, groups, 9, chunks, LANES), f32),
            VMEM((15, chunks, LANES), f32),
            VMEM((chunks, 72, LANES), f32),
            dma((10,)),
            dma((n_view,)),
            dma((n_view,)),
            dma((n_gs,)),
            dma((n_gs,)),
            dma((2,)),
            dma((2,)),
            dma((2,)),
            dma((2,)),
            dma((groups, n_gs)),
            dma((groups, n_gs)),
            dma((1,)),
            dma((1,)),
        ],
        compiler_params=pltpu.CompilerParams(
            collective_id=1, has_side_effects=True, vmem_limit_bytes=48 * 1024 * 1024
        ),
    )(*[pltpu.with_memory_space_constraint(x, pltpu.HBM) for x in args])
    outs = pl.pallas_call(
        store_kernel,
        out_shape=out_shape,
        in_specs=[vmem] * 6,
        out_specs=(hbm,) * 6,
        scratch_shapes=[dma((6,))],
        compiler_params=pltpu.CompilerParams(vmem_limit_bytes=48 * 1024 * 1024),
    )(*mids)
    return (*outs[:4], outs[4].reshape(shard), outs[5])


def solution(mesh):
    return jax.shard_map(
        shards,
        mesh=mesh,
        in_specs=(
            P(None, "gs"),
            P(None, "gs"),
            P(None, "gs"),
            P("gs"),
            P(None, "gs"),
            P("view", None),
            P("view", None, "gs", None),
            P("gs", None, None),
            P("view", "gs", None, None),
            P("view", "gs", None),
        ),
        out_specs=(
            P("view", None, "gs", None),
            P(None, "gs"),
            P(None, "gs"),
            P(None, "gs"),
            P("gs"),
            P(None, "gs"),
        ),
        check_vma=False,
    )
```

```python
import math

import jax
import jax.numpy as jnp
import ml_dtypes
import numpy as np
from jax import lax
from jax.experimental import pallas as pl
from jax.experimental.pallas import tpu as pltpu
from jax.sharding import PartitionSpec as P

TILE = 16
SH = 16
RADIUS = 5
LANES = 128
ROWS_MSG = 16
VMEM = pltpu.VMEM
MESH = pl.DeviceIdType.MESH

focal_length = 1000.0
cov_blur = 0.3
ssim_weight = 0.2
charb_eps = 0.0001
ssim_one = 0.0001
ssim_two = 0.0009
sh_c0 = 0.28209479177387814
sh_c1 = 0.4886025119029199
sh_c2 = [
    1.0925484305920792,
    -1.0925484305920792,
    0.31539156525252005,
    -1.0925484305920792,
    0.5462742152960396,
]
sh_c3 = [
    -0.5900435899266435,
    2.890611442640554,
    -0.4570457994644658,
    0.3731763325901154,
    -0.4570457994644658,
    1.445305721320277,
    -0.5900435899266435,
]

f32 = jnp.float32
bf16 = jnp.bfloat16


def sh_basis(dir_x, dir_y, dir_z):
    sq_x = dir_x * dir_x
    sq_y = dir_y * dir_y
    sq_z = dir_z * dir_z
    return [
        None,
        -sh_c1 * dir_y,
        sh_c1 * dir_z,
        -sh_c1 * dir_x,
        sh_c2[0] * dir_x * dir_y,
        sh_c2[1] * dir_y * dir_z,
        sh_c2[2] * (2.0 * sq_z - sq_x - sq_y),
        sh_c2[3] * dir_x * dir_z,
        sh_c2[4] * (sq_x - sq_y),
        sh_c3[0] * dir_y * (3.0 * sq_x - sq_y),
        sh_c3[1] * dir_x * dir_y * dir_z,
        sh_c3[2] * dir_y * (4.0 * sq_z - sq_x - sq_y),
        sh_c3[3] * dir_z * (2.0 * sq_z - 3.0 * sq_x - 3.0 * sq_y),
        sh_c3[4] * dir_x * (4.0 * sq_z - sq_x - sq_y),
        sh_c3[5] * dir_z * (sq_x - sq_y),
        sh_c3[6] * dir_x * (sq_x - 3.0 * sq_y),
    ]


def project(means, quats, log_scales, opacity, coeffs, cameras, centre_x, centre_y):
    inv_norm = 1.0 / jnp.sqrt(
        quats[0] * quats[0] + quats[1] * quats[1] + quats[2] * quats[2] + quats[3] * quats[3]
    )
    quat_w, quat_x, quat_y, quat_z = [quat * inv_norm for quat in quats]
    scales = [jnp.exp(log_scale) for log_scale in log_scales]
    rotation = [
        [
            1.0 - 2.0 * (quat_y * quat_y + quat_z * quat_z),
            2.0 * (quat_x * quat_y - quat_w * quat_z),
            2.0 * (quat_x * quat_z + quat_w * quat_y),
        ],
        [
            2.0 * (quat_x * quat_y + quat_w * quat_z),
            1.0 - 2.0 * (quat_x * quat_x + quat_z * quat_z),
            2.0 * (quat_y * quat_z - quat_w * quat_x),
        ],
        [
            2.0 * (quat_x * quat_z - quat_w * quat_y),
            2.0 * (quat_y * quat_z + quat_w * quat_x),
            1.0 - 2.0 * (quat_x * quat_x + quat_y * quat_y),
        ],
    ]
    spread = [[rotation[i][j] * scales[j] for j in range(3)] for i in range(3)]
    depth_z = means[2]
    inv_depth = 1.0 / depth_z
    jac_diag = focal_length * inv_depth
    diag_top = [jac_diag * spread[0][j] for j in range(3)]
    diag_low = [jac_diag * spread[1][j] for j in range(3)]
    log_alpha = -jnp.log(1.0 + jnp.exp(-opacity))
    views = []
    for cam_x, cam_y in cameras:
        rel_x = means[0] - cam_x
        rel_y = means[1] - cam_y
        ratio_u = jac_diag * rel_x
        ratio_v = jac_diag * rel_y
        jac_u = -ratio_u * inv_depth
        jac_v = -ratio_v * inv_depth
        top = [diag_top[j] + jac_u * spread[2][j] for j in range(3)]
        low = [diag_low[j] + jac_v * spread[2][j] for j in range(3)]
        cov_a = top[0] * top[0] + top[1] * top[1] + top[2] * top[2] + cov_blur
        cov_b = top[0] * low[0] + top[1] * low[1] + top[2] * low[2]
        cov_c = low[0] * low[0] + low[1] * low[1] + low[2] * low[2] + cov_blur
        inv_det = 1.0 / (cov_a * cov_c - cov_b * cov_b)
        inv_dist = 1.0 / jnp.sqrt(rel_x * rel_x + rel_y * rel_y + depth_z * depth_z)
        basis = sh_basis(rel_x * inv_dist, rel_y * inv_dist, depth_z * inv_dist)
        colours = []
        for channel in range(3):
            total = sh_c0 * coeffs[channel * SH] + 0.5
            for k in range(1, SH):
                total = total + coeffs[channel * SH + k] * basis[k]
            colours.append(jnp.maximum(total, 0.0))
        views.append(
            [
                ratio_u + centre_x,
                ratio_v + centre_y,
                cov_c * inv_det,
                -cov_b * inv_det,
                cov_a * inv_det,
                log_alpha,
            ]
            + colours
        )
    return views


def window_taps():
    raw_taps = [math.exp(-((tap_idx - RADIUS) ** 2) / 4.5) for tap_idx in range(2 * RADIUS + 1)]
    total = sum(raw_taps)
    return [tap / total for tap in raw_taps]


def band(out_count, in_count, offset):
    taps = window_taps()
    shape = (out_count, in_count)
    gap = lax.broadcasted_iota(jnp.int32, shape, 1) - lax.broadcasted_iota(jnp.int32, shape, 0)
    gap = jnp.abs(gap - offset)
    matrix = jnp.zeros(shape, f32)
    for far in range(RADIUS + 1):
        matrix = jnp.where(gap == far, taps[RADIUS + far], matrix)
    return matrix


def pieces(x, count):
    out = []
    for _ in range(count - 1):
        part = x.astype(bf16).astype(f32)
        out.append(part)
        x = x - part
    out.append(x)
    return out


def stack(x, count, axis=0):
    return jnp.concatenate(pieces(x, count), axis=axis).astype(bf16)


def dot(a, b):
    return lax.dot_general(a, b, (((1,), (0,)), ((), ())), preferred_element_type=f32)


def dot_t(a, b):
    return lax.dot_general(a, b, (((1,), (1,)), ((), ())), preferred_element_type=f32)


def dot_exact(a, b):
    return lax.dot_general(
        a, b, (((1,), (0,)), ((), ())), precision=lax.Precision.HIGHEST, preferred_element_type=f32
    )


def fold(x, count):
    size = x.shape[0] // count
    total = x[:size]
    for i in range(1, count):
        total = total + x[i * size : (i + 1) * size]
    return total


def loop(low, high, step):
    if high - low <= 8:
        for i in range(low, high):
            step(i)
    else:

        @pl.loop(low, high)
        def _(i):
            step(i)


def params(par, opacity):
    return (
        [par[:, 48 + i, :] for i in range(3)],
        [par[:, 56 + i, :] for i in range(4)],
        [par[:, 64 + i, :] for i in range(3)],
        opacity[...],
        [par[:, i, :] for i in range(48)],
    )


def pick_of(send, d, shard):
    local_row = lax.broadcasted_iota(jnp.int32, (shard, send.shape[2]), 0)
    return jnp.where(local_row == send[0, pl.ds(d, 1), :], 1.0, 0.0).astype(bf16)


def split_taps():
    high = [float(np.asarray(tap, ml_dtypes.bfloat16)) for tap in window_taps()]
    return high, [float(tap) - top for tap, top in zip(window_taps(), high)]


def band_split(out_count, in_rows, offset, axis):
    high, low = split_taps()
    count = len(in_rows)
    shape = (out_count, 3 * count) if axis == 1 else (3 * count, out_count)
    inner = lax.broadcasted_iota(jnp.int32, shape, axis)
    part = inner // count
    place = lax.rem(inner, count)
    start = in_rows[0]
    jump = [k for k in range(1, count) if in_rows[k] != in_rows[k - 1] + 1]
    row = place + start
    for k in jump:
        row = row + jnp.where(place >= k, in_rows[k] - in_rows[k - 1] - 1, 0)
    gap = jnp.abs(row - lax.broadcasted_iota(jnp.int32, shape, 1 - axis) - offset)
    matrix = jnp.zeros(shape, f32)
    for far in range(RADIUS + 1):
        tap = jnp.where(part == 2, low[RADIUS + far], high[RADIUS + far])
        matrix = jnp.where(gap == far, tap, matrix)
    return matrix.astype(bf16)


def stack_mixed(x, axis):
    high, low = pieces(x, 2)
    return jnp.concatenate([high, low, high], axis=axis).astype(bf16)


def side_by_side(x, count):
    size = x.shape[1] // count
    return jnp.concatenate([x[:, i * size : (i + 1) * size] for i in range(count)], axis=0)


def pad_rows(x):
    return jnp.concatenate([x, jnp.zeros((ROWS_MSG - x.shape[0], x.shape[1]), f32)], axis=0)


def flip(index, bits):
    bit = 1
    while bit <= bits:
        if bits & bit:
            index = index + bit * (1 - 2 * lax.rem(lax.div(index, bit), 2))
        bit *= 2
    return index


def spread_of(quats, log_scales):
    inv_norm = 1.0 / jnp.sqrt(
        quats[0] * quats[0] + quats[1] * quats[1] + quats[2] * quats[2] + quats[3] * quats[3]
    )
    w, x, y, z = [quat * inv_norm for quat in quats]
    rotation = [
        [1.0 - 2.0 * (y * y + z * z), 2.0 * (x * y - w * z), 2.0 * (x * z + w * y)],
        [2.0 * (x * y + w * z), 1.0 - 2.0 * (x * x + z * z), 2.0 * (y * z - w * x)],
        [2.0 * (x * z - w * y), 2.0 * (y * z + w * x), 1.0 - 2.0 * (x * x + y * y)],
    ]
    scales = [jnp.exp(log_scale) for log_scale in log_scales]
    return [[rotation[i][j] * scales[j] for j in range(3)] for i in range(3)]


def basis_slopes(x, y, z):
    xx, yy, zz = x * x, y * y, z * z
    xy, yz, xz = x * y, y * z, x * z
    gap = xx - yy
    four = 4.0 * zz
    return [
        {
            3: -sh_c1,
            4: sh_c2[0] * y,
            6: -2.0 * sh_c2[2] * x,
            7: sh_c2[3] * z,
            8: 2.0 * sh_c2[4] * x,
            9: 6.0 * sh_c3[0] * xy,
            10: sh_c3[1] * yz,
            11: -2.0 * sh_c3[2] * xy,
            12: -6.0 * sh_c3[3] * xz,
            13: sh_c3[4] * (four - 3.0 * xx - yy),
            14: 2.0 * sh_c3[5] * xz,
            15: 3.0 * sh_c3[6] * gap,
        },
        {
            1: -sh_c1,
            4: sh_c2[0] * x,
            5: sh_c2[1] * z,
            6: -2.0 * sh_c2[2] * y,
            8: -2.0 * sh_c2[4] * y,
            9: 3.0 * sh_c3[0] * gap,
            10: sh_c3[1] * xz,
            11: sh_c3[2] * (four - xx - 3.0 * yy),
            12: -6.0 * sh_c3[3] * yz,
            13: -2.0 * sh_c3[4] * xy,
            14: -2.0 * sh_c3[5] * yz,
            15: -6.0 * sh_c3[6] * xy,
        },
        {
            2: sh_c1,
            5: sh_c2[1] * y,
            6: 4.0 * sh_c2[2] * z,
            7: sh_c2[3] * x,
            10: sh_c3[1] * xy,
            11: 8.0 * sh_c3[2] * yz,
            12: sh_c3[3] * (6.0 * zz - 3.0 * xx - 3.0 * yy),
            13: 8.0 * sh_c3[4] * xz,
            14: sh_c3[5] * gap,
        },
    ]


N_KEPT = 42


def keep_view(kept, par, spread, means, inv_depth, jac_diag, cam_x, cam_y):
    rel_x = means[0] - cam_x
    rel_y = means[1] - cam_y
    ratio_u = jac_diag * rel_x
    ratio_v = jac_diag * rel_y
    jac_u = -ratio_u * inv_depth
    jac_v = -ratio_v * inv_depth
    top = [jac_diag * spread[0][j] + jac_u * spread[2][j] for j in range(3)]
    low = [jac_diag * spread[1][j] + jac_v * spread[2][j] for j in range(3)]
    cov_a = top[0] * top[0] + top[1] * top[1] + top[2] * top[2] + cov_blur
    cov_b = top[0] * low[0] + top[1] * low[1] + top[2] * low[2]
    cov_c = low[0] * low[0] + low[1] * low[1] + low[2] * low[2] + cov_blur
    inv_det = 1.0 / (cov_a * cov_c - cov_b * cov_b)
    out = [rel_x, rel_y, ratio_u, ratio_v, jac_u, jac_v] + top + low
    out += [cov_c * inv_det, -cov_b * inv_det, cov_a * inv_det]
    for i, x in enumerate(out):
        kept[i] = x
    inv_dist = 1.0 / jnp.sqrt(rel_x * rel_x + rel_y * rel_y + means[2] * means[2])
    turn = [rel_x * inv_dist, rel_y * inv_dist, means[2] * inv_dist]
    basis = sh_basis(*turn)
    slopes = basis_slopes(*turn)
    for k in range(1, SH):
        kept[26 + k] = basis[k]
    for channel in range(3):
        raw = sh_c0 * par[:, channel * SH, :] + 0.5
        slope = [None, None, None]
        for k in range(1, SH):
            coeff = par[:, channel * SH + k, :]
            raw = raw + coeff * basis[k]
            for i in range(3):
                if k in slopes[i]:
                    term = coeff * slopes[i][k]
                    slope[i] = term if slope[i] is None else slope[i] + term
        along = turn[0] * slope[0] + turn[1] * slope[1] + turn[2] * slope[2]
        for i in range(3):
            kept[15 + 3 * channel + i] = (slope[i] - turn[i] * along) * inv_dist
        kept[24 + channel] = jnp.where(raw > 0.0, 1.0, jnp.where(raw == 0.0, 0.5, 0.0))


def pull_view(kept, cots, inv_depth, jac_diag, spread):
    rel_x, rel_y, ratio_u, ratio_v, jac_u, jac_v = [kept[i] for i in range(6)]
    top = [kept[6 + j] for j in range(3)]
    low = [kept[9 + j] for j in range(3)]
    k0, k1, k2 = [kept[12 + i] for i in range(3)]
    g0, g1, g2 = cots[2], cots[3], cots[4]
    cov_a = -(k0 * k0 * g0 + k0 * k1 * g1 + k1 * k1 * g2)
    cov_b = -2.0 * (k0 * k1 * g0 + k1 * k2 * g2) - (k0 * k2 + k1 * k1) * g1
    cov_c = -(k1 * k1 * g0 + k1 * k2 * g1 + k2 * k2 * g2)
    d_top = [2.0 * cov_a * top[j] + cov_b * low[j] for j in range(3)]
    d_low = [2.0 * cov_c * low[j] + cov_b * top[j] for j in range(3)]
    d_base = [jac_u * d_top[j] + jac_v * d_low[j] for j in range(3)]
    d_jac_u = d_top[0] * spread[2][0] + d_top[1] * spread[2][1] + d_top[2] * spread[2][2]
    d_jac_v = d_low[0] * spread[2][0] + d_low[1] * spread[2][1] + d_low[2] * spread[2][2]
    d_ratio_u = cots[0] - inv_depth * d_jac_u
    d_ratio_v = cots[1] - inv_depth * d_jac_v
    shades = [cots[6 + c] * kept[24 + c] for c in range(3)]
    turn = [
        shades[0] * kept[15 + i] + shades[1] * kept[18 + i] + shades[2] * kept[21 + i]
        for i in range(3)
    ]
    d_x = jac_diag * d_ratio_u + turn[0]
    d_y = jac_diag * d_ratio_v + turn[1]
    d_diag = rel_x * d_ratio_u + rel_y * d_ratio_v
    d_inv = -(ratio_u * d_jac_u + ratio_v * d_jac_v)
    return d_top + d_low + d_base + [d_x, d_y, turn[2], d_diag, d_inv, cots[5]], shades


def octets(x):
    return [x[k : k + 8] for k in range(0, x.shape[0], 8)]


def products_before(parts):
    sub = lax.broadcasted_iota(jnp.int32, parts[0].shape, 0)
    run, before = parts[0], [None]
    for part in parts[1:]:
        before.append(run)
        run = run * part
    lead = jnp.where(sub >= 1, pltpu.roll(run, 1, 0), 1.0)
    for step in (1, 2, 4):
        lead = lead * jnp.where(sub >= step, pltpu.roll(lead, step, 0), 1.0)
    return [lead if x is None else x * lead for x in before]


def sums_after(parts):
    sub = lax.broadcasted_iota(jnp.int32, parts[0].shape, 0)
    run, after = parts[-1], [None]
    for part in parts[-2::-1]:
        after.append(run)
        run = run + part
    tail = jnp.where(sub < 7, pltpu.roll(run, 7, 0), 0.0)
    for step in (1, 2, 4):
        tail = tail + jnp.where(sub < 8 - step, pltpu.roll(tail, 8 - step, 0), 0.0)
    return [tail if x is None else x + tail for x in after[::-1]]


def near_kernel(
    n_gs,
    n_view,
    means_in,
    quats_in,
    scales_in,
    opacity_in,
    sh_in,
    camera_in,
    targets_in,
    send_in,
    lists_in,
    lens_in,
    pic_out,
    means_out,
    quats_out,
    scales_out,
    opacity_out,
    sh_out,
    par,
    opacity,
    send,
    means,
    quats,
    scales,
    sh,
    camera,
    targets,
    lists,
    lens,
    cams,
    row_buf,
    msg_out,
    msg_in,
    slot_mask,
    slot_mask_t,
    row_mask,
    bases,
    bases_t,
    tile_buf,
    ratio_buf,
    weight_buf,
    shade_buf,
    split_buf,
    power_buf,
    pic,
    halo,
    t_halo,
    cot,
    back_out,
    back_in,
    placed,
    kept,
    cot_views,
    g_sum,
    g_par,
    load_sems,
    send_cam,
    recv_cam,
    send_one,
    recv_one,
    send_halo,
    recv_halo,
    send_tgt,
    recv_tgt,
    send_two,
    recv_two,
    send_three,
    recv_three,
):
    loads = [
        pltpu.make_async_copy(src, dst, load_sems.at[k])
        for k, (src, dst) in enumerate(
            [
                (sh_in, sh),
                (means_in, means),
                (quats_in, quats),
                (scales_in, scales),
                (opacity_in, opacity),
                (camera_in, camera),
                (send_in, send),
                (lists_in.at[0, 0], lists),
                (lens_in.at[0], lens),
                (targets_in, targets),
            ]
        )
    ]
    for load in loads:
        load.start()
    gs = lax.axis_index("gs")
    view = lax.axis_index("view")
    shard = means.shape[1]
    chunks = shard // LANES
    cap = send.shape[2]
    tiles, list_size = lists.shape
    groups = n_view // 2
    core = lax.rem(view, 2)
    group = lax.div(view, 2)
    has_up = gs > 0
    has_down = gs < n_gs - 1
    near = range(1, n_gs)
    far = range(n_gs - 1, 0, -1)

    def cousin(j):
        return lax.rem(view + 2 * j, n_view)

    barrier = pltpu.get_barrier_semaphore()

    def greet(strip, cam):
        pl.semaphore_signal(barrier, inc=1, device_id=(strip, cam), device_id_type=MESH)

    for k in near:
        greet(flip(gs, k), view)
    for j in range(1, groups):
        for k in range(n_gs):
            greet(flip(gs, k), cousin(j))
    for j in range(groups):
        greet(gs, flip(cousin(j), 1))
    greeted = n_gs - 1 + (groups - 1) * n_gs + groups

    for load in loads[:7]:
        load.wait()

    for c in range(chunks):
        cols = slice(c * LANES, (c + 1) * LANES)
        par[c, 0:48, :] = sh[:, cols]
        par[c, 48:51, :] = means[:, cols]
        par[c, 56:60, :] = quats[:, cols]
        par[c, 64:67, :] = scales[:, cols]

    centre_x = 0.5 * tiles * TILE
    centre_y = 0.5 * n_gs * TILE
    cam_x = camera[0:1, 0:1]
    cam_y = camera[0:1, 1:2]
    rows = project(*params(par, opacity), [(cam_x, cam_y)], centre_x, centre_y)[0]
    row_buf[...] = jnp.zeros_like(row_buf)
    for i in range(9):
        row_buf[:, i, :] = rows[i]
    table = stack(jnp.concatenate([row_buf[c] for c in range(chunks)], axis=1), 3)

    def fill(d):
        msg_out[d] = fold(dot(table, pick_of(send, d, shard)), 3)[0:9]

    def first_copy(d, s):
        return pltpu.make_async_remote_copy(
            src_ref=msg_out.at[d],
            dst_ref=msg_in.at[s],
            send_sem=send_one.at[d],
            recv_sem=recv_one.at[s],
            device_id=(d, view),
            device_id_type=MESH,
        )

    pl.semaphore_wait(barrier, greeted)

    for k in far:
        fill(flip(gs, k))
        first_copy(flip(gs, k), gs).start()
    fill(gs)
    msg_in[gs] = msg_out[gs]

    def cam_copy(to, of):
        return pltpu.make_async_remote_copy(
            src_ref=cams.at[of],
            dst_ref=cams.at[of],
            send_sem=send_cam.at[to],
            recv_sem=recv_cam.at[of],
            device_id=(gs, to),
            device_id_type=MESH,
        )

    lane_one = lax.broadcasted_iota(jnp.int32, (1, LANES), 1)
    cams[view] = jnp.where(lane_one == 0, cam_x, cam_y)
    for k in range(1, n_view):
        cam_copy(lax.rem(view + k, n_view), view).start()

    def halo_copy(src, dst, sends, recvs, side):
        other = gs + 1 if side == 0 else gs - 1
        return pltpu.make_async_remote_copy(
            src_ref=src,
            dst_ref=dst.at[side],
            send_sem=sends.at[side],
            recv_sem=recvs.at[side],
            device_id=(other, view),
            device_id_type=MESH,
        )

    def exchange(src, dst, sends, recvs, start, ends=(False, True)):
        def act(copy, recv):
            if start:
                copy.start()
            elif recv:
                copy.wait_recv()
            else:
                copy.wait_send()

        for recv in ends:
            if start and recv:
                continue

            @pl.when(has_down)
            def _():
                act(halo_copy(src, dst, sends, recvs, 1 if recv else 0), recv)

            @pl.when(has_up)
            def _():
                act(halo_copy(src, dst, sends, recvs, 0 if recv else 1), recv)

    for load in loads[7:]:
        load.wait()
    exchange(targets.at[0], t_halo, send_tgt, recv_tgt, True)

    @pl.when(jnp.logical_not(has_up))
    def _():
        halo[0] = jnp.zeros_like(halo[0])
        t_halo[0] = jnp.zeros_like(t_halo[0])

    @pl.when(jnp.logical_not(has_down))
    def _():
        halo[1] = jnp.zeros_like(halo[1])
        t_halo[1] = jnp.zeros_like(t_halo[1])

    n_chunk, _, wide = weight_buf.shape
    width = tiles * TILE
    per = wide // width
    deep = list_size // 8
    place = lax.broadcasted_iota(jnp.int32, (list_size, list_size), 1)
    moved = lax.broadcasted_iota(jnp.int32, (list_size, list_size), 0) == (
        lax.rem(place, 8) * deep + place // 8
    )
    placed_lists = dot_exact(lists[...].astype(f32), jnp.where(moved, 1.0, 0.0))
    placed_lists = jnp.floor(placed_lists + 0.5)
    whole_lists = placed_lists.astype(jnp.int32)
    slot_row = lax.broadcasted_iota(jnp.int32, (cap, list_size), 0)
    for k in range(n_gs):
        here = slot_row + flip(gs, k) * cap
        for t in range(tiles):
            slot_mask[k, :, t * list_size : (t + 1) * list_size] = jnp.where(
                here == whole_lists[t : t + 1, :], 1.0, 0.0
            ).astype(bf16)
    lists_t = jnp.transpose(placed_lists)
    slot_lane = lax.broadcasted_iota(jnp.int32, (list_size, cap), 1)
    for t in range(tiles):
        listed = jnp.broadcast_to(lists_t[:, t : t + 1], (list_size, cap))
        for k in range(n_gs):
            here = (slot_lane + flip(gs, k) * cap).astype(f32)
            slot_mask_t[k, t * list_size : (t + 1) * list_size, :] = jnp.where(
                here == listed, 1.0, 0.0
            ).astype(bf16)

    lane = lax.broadcasted_iota(jnp.int32, (tiles, wide), 1)
    in_tile = lax.rem(lane, width) // TILE == lax.broadcasted_iota(jnp.int32, (tiles, wide), 0)
    off_q = (lax.rem(lane, TILE) - TILE // 2).astype(f32)
    half_r = (lane // width).astype(f32)
    for i in range(n_chunk):
        off_r = half_r + float(i * per - TILE // 2)
        out = [jnp.ones_like(off_q), off_q, off_r, off_q * off_q, off_q * off_r, off_r * off_r]
        base = jnp.concatenate([jnp.where(in_tile, x, 0.0) for x in out], axis=0)
        bases[i] = base.astype(bf16)
        bases_t[i * wide : (i + 1) * wide, :] = jnp.transpose(base).astype(bf16)
    shape = (9 * tiles, 3 * width)
    row_of, lane_of = [lax.broadcasted_iota(jnp.int32, shape, k) for k in range(2)]
    at_tile = lax.rem(row_of, tiles) == lax.rem(lane_of, width) // TILE
    at_channel = lax.rem(row_of // tiles, 3) == lane_of // width
    widen = jnp.where(jnp.logical_and(at_tile, at_channel), 1.0, 0.0).astype(bf16)
    p_means, p_quats, p_scales, p_opacity, _ = params(par, opacity)
    spread, pull_spread = jax.vjp(spread_of, p_quats, p_scales)
    inv_depth = 1.0 / p_means[2]
    jac_diag = focal_length * inv_depth

    def keep(h, j, of):
        at = cams[of]
        keep_view(
            kept.at[h, j], par, spread, p_means, inv_depth, jac_diag, at[:, 0:1], at[:, 1:2]
        )

    keep(0, group, view)
    for t in range(tiles):
        tile_buf[t] = jnp.zeros((ROWS_MSG, list_size), f32)

    def gather(k, s):
        got = fold(dot(stack(pad_rows(msg_in[s]), 3), slot_mask[k]), 3)
        for t in range(tiles):
            tile_buf[t] += got[:, t * list_size : (t + 1) * list_size]

    gather(0, gs)
    for k in near:
        s = flip(gs, k)
        first_copy(gs, s).wait_recv()
        gather(k, s)

    diagonal = lax.broadcasted_iota(jnp.int32, (tiles, tiles), 0) == lax.broadcasted_iota(
        jnp.int32, (tiles, tiles), 1
    )
    used = jnp.sum(jnp.where(diagonal, lens[...].astype(f32), 0.0), axis=1, keepdims=True)
    entry = lax.broadcasted_iota(jnp.int32, (tiles, list_size), 1)
    entry = lax.rem(entry, 8) * deep + entry // 8
    live = entry.astype(f32) < used
    mid_q = (lax.broadcasted_iota(jnp.int32, (tiles, list_size), 0) * TILE + TILE // 2).astype(f32)
    mid_r = (gs * TILE + TILE // 2).astype(f32)
    off_u = tile_buf[:, 0, :] - mid_q
    off_w = tile_buf[:, 1, :] - mid_r
    k0 = tile_buf[:, 2, :]
    k1 = tile_buf[:, 3, :]
    k2 = tile_buf[:, 4, :]
    lin_u = k0 * off_u + k1 * off_w
    lin_w = k2 * off_w + k1 * off_u
    terms = [
        jnp.where(live, tile_buf[:, 5, :] - 0.5 * (off_u * lin_u + off_w * lin_w), -10000.0),
        jnp.where(live, lin_u, 0.0),
        jnp.where(live, lin_w, 0.0),
        jnp.where(live, -0.5 * k0, 0.0),
        jnp.where(live, -k1, 0.0),
        jnp.where(live, -0.5 * k2, 0.0),
    ]
    term_t = jnp.transpose(jnp.concatenate(pieces(jnp.concatenate(terms, axis=0), 3), axis=0))
    term_t = term_t.astype(bf16)
    colour = jnp.concatenate([tile_buf[:, 6 + c, :] for c in range(3)], axis=0)
    col_t = jnp.transpose(jnp.concatenate(pieces(colour, 3), axis=0)).astype(bf16)
    shade_buf[...] = dot(col_t, widen)

    for i in range(n_chunk):
        base = bases[i]
        ratio_buf[i] = jnp.exp(dot(term_t, jnp.concatenate([base, base, base], axis=0)))
    for i in range(n_chunk):
        for half in range(per):
            lanes = slice(half * width, (half + 1) * width)
            alpha = octets(ratio_buf[i, :, lanes])
            before = products_before([1.0 - x for x in alpha])
            weight = [x * y for x, y in zip(alpha, before)]
            weight_buf[i, :, lanes] = jnp.concatenate(weight, axis=0)
            row = i * per + half
            for c in range(3):
                shade = octets(shade_buf[:, c * width : (c + 1) * width])
                total = weight[0] * shade[0]
                for x, y in zip(weight[1:], shade[1:]):
                    total = total + x * y
                pic[c, row : row + 1, :] = jnp.sum(total, axis=0, keepdims=True)

    exchange(pic, halo, send_halo, recv_halo, True)
    pic_out[0] = pic[...]
    exchange(targets.at[0], t_halo, send_tgt, recv_tgt, False)
    tall = 2 * TILE
    across = band_split(width, list(range(width)), 0, 0)
    tgts = [
        jnp.concatenate([t_halo[0, c], targets[0, c], t_halo[1, c]], axis=0) for c in range(3)
    ]
    planes = []
    for c in range(3):
        planes += [tgts[c], tgts[c] * tgts[c]]
    rows_all = list(range(3 * TILE))
    band_all = band_split(tall, rows_all, TILE // 2, 1)
    down = dot(band_all, stack_mixed(jnp.concatenate(planes, axis=1), 0))
    blur_tgt = dot(stack_mixed(side_by_side(down, 6), 1), across)
    own = []
    for c in range(3):
        img = pic[c]
        own += [img, img * img, img * targets[0, c]]
    band_own = band_split(tall, rows_all[TILE : 2 * TILE], TILE // 2, 1)
    down_own = dot(band_own, stack_mixed(jnp.concatenate(own, axis=1), 0))
    band_far = band_split(tall, rows_all[:TILE] + rows_all[2 * TILE :], TILE // 2, 1)
    band_back = band_split(TILE, list(range(tall)), TILE // 2, 1)
    directs = []
    for c in range(3):
        res = pic[c] - targets[0, c]
        directs.append(
            (1.0 - ssim_weight) / (TILE * TILE) * res / jnp.sqrt(res * res + charb_eps)
        )
    for i in range(n_chunk):
        split_buf[i] = stack(jnp.transpose(weight_buf[i]), 2, 1)
        for half in range(per):
            lanes = slice(half * width, (half + 1) * width)
            alpha = ratio_buf[i, :, lanes]
            ratio = alpha / (1.0 - alpha)
            weight = weight_buf[i, :, lanes]
            for c in range(3):
                share = weight * shade_buf[:, c * width : (c + 1) * width]
                after = jnp.concatenate(sums_after(octets(share)), axis=0)
                power_buf[c, i, :, lanes] = share - ratio * after
    exchange(pic, halo, send_halo, recv_halo, False)

    beyond = []
    for c in range(3):
        img = jnp.concatenate([halo[0, c], halo[1, c]], axis=0)
        tgt = jnp.concatenate([t_halo[0, c], t_halo[1, c]], axis=0)
        beyond += [img, img * img, img * tgt]
    down = down_own + dot(band_far, stack_mixed(jnp.concatenate(beyond, axis=1), 0))
    blurred = dot(stack_mixed(side_by_side(down, 9), 1), across)
    at_row = lax.broadcasted_iota(jnp.int32, (tall, width), 0) + gs * TILE - TILE // 2
    inside = jnp.logical_and(at_row >= 0, at_row < n_gs * TILE)
    scale = -ssim_weight / (TILE * TILE)
    cots = []
    for c in range(3):
        mean_x, raw_xx, raw_xy = [
            blurred[(3 * c + i) * tall : (3 * c + i + 1) * tall] for i in range(3)
        ]
        mean_y, raw_yy = [
            blur_tgt[(2 * c + i) * tall : (2 * c + i + 1) * tall] for i in range(2)
        ]
        top_a = 2.0 * mean_x * mean_y + ssim_one
        top_b = 2.0 * (raw_xy - mean_x * mean_y) + ssim_two
        low_c = mean_x * mean_x + mean_y * mean_y + ssim_one
        low_d = (raw_xx - mean_x * mean_x) + (raw_yy - mean_y * mean_y) + ssim_two
        inv_cd = 1.0 / (low_c * low_d)
        inv_dd = inv_cd * low_c
        ssim = top_a * top_b * inv_cd
        d_mean = 2.0 * mean_y * (top_b - top_a) * inv_cd - 2.0 * mean_x * ssim * (
            inv_cd * low_d - inv_dd
        )
        d_xx = -ssim * inv_dd
        d_xy = 2.0 * top_a * inv_cd
        cots += [jnp.where(inside, scale * part, 0.0) for part in (d_mean, d_xx, d_xy)]
    spread_rows = dot(band_back, stack_mixed(jnp.concatenate(cots, axis=1), 0))
    spread_rows = dot(stack_mixed(side_by_side(spread_rows, 9), 1), across)
    grad_rows = []
    for c in range(3):
        s_mean, s_xx, s_xy = [spread_rows[(3 * c + i) * TILE : (3 * c + i + 1) * TILE] for i in range(3)]
        grad_rows.append(directs[c] + s_mean + 2.0 * pic[c] * s_xx + targets[0, c] * s_xy)

    d_terms = jnp.zeros((2 * list_size, 6 * tiles), f32)
    d_colour = jnp.zeros((6 * tiles, 2 * list_size), f32)
    for i in range(n_chunk):
        lines = [
            jnp.concatenate(
                [grad_rows[c][i * per + half : i * per + half + 1] for half in range(per)], axis=1
            )
            for c in range(3)
        ]
        shades = stack(jnp.concatenate([jnp.where(in_tile, x, 0.0) for x in lines], axis=0), 2)
        d_power = lines[0] * power_buf[0, i] + lines[1] * power_buf[1, i] + lines[2] * power_buf[2, i]
        d_terms = d_terms + dot(stack(d_power, 2), bases_t[i * wide : (i + 1) * wide, :])
        d_colour = d_colour + dot(shades, split_buf[i])
    d_terms = jnp.transpose(fold(d_terms, 2))
    d_colour = fold(d_colour[:, :list_size] + d_colour[:, list_size:], 2)

    d0, d1, d2, d3, d4, d5 = [d_terms[k * tiles : (k + 1) * tiles] for k in range(6)]
    e1 = d1 - off_u * d0
    e2 = d2 - off_w * d0
    cot[...] = jnp.zeros_like(cot)
    cot[:, 0, :] = k0 * e1 + k1 * e2
    cot[:, 1, :] = k2 * e2 + k1 * e1
    cot[:, 2, :] = -0.5 * d3 + off_u * (d1 - 0.5 * off_u * d0)
    cot[:, 3, :] = off_w * e1 + off_u * d2 - d4
    cot[:, 4, :] = -0.5 * d5 + off_w * (d2 - 0.5 * off_w * d0)
    cot[:, 5, :] = d0
    for c in range(3):
        cot[:, 6 + c, :] = d_colour[c * tiles : (c + 1) * tiles]
    cots = jnp.concatenate([stack(cot[t], 2) for t in range(tiles)], axis=1)

    def out_copy(j, d):
        return pltpu.make_async_remote_copy(
            src_ref=back_out.at[d],
            dst_ref=back_in.at[group, gs],
            send_sem=send_two.at[j, d],
            recv_sem=recv_two.at[group, gs],
            device_id=(d, cousin(j)),
            device_id_type=MESH,
        )

    def in_copy(j, s):
        of = lax.div(cousin(j), 2)
        return pltpu.make_async_remote_copy(
            src_ref=back_out.at[s],
            dst_ref=back_in.at[of, s],
            send_sem=send_two.at[j, s],
            recv_sem=recv_two.at[of, s],
            device_id=(s, cousin(j)),
            device_id_type=MESH,
        )

    for k in list(far) + [0]:
        d = flip(gs, k)
        back_out[d] = fold(dot(cots, slot_mask_t[k]), 2)[0:9]
        for j in range(groups):
            if k or j:
                out_copy(j, d).start()
    back_in[group, gs] = back_out[gs]

    send_t = jnp.transpose(send[0].astype(f32))
    shard_lane = lax.broadcasted_iota(jnp.int32, (cap, shard), 1).astype(f32)
    for s in range(n_gs):
        row_mask[s] = jnp.where(shard_lane == send_t[:, s : s + 1], 1.0, 0.0).astype(bf16)
    for k in range(1, n_view):
        cam_copy(view, lax.rem(view + n_view - k, n_view)).wait_recv()
    for j in range(1, groups):
        keep(0, lax.div(cousin(j), 2), cousin(j))
    for j in range(groups):
        keep(1, j, 2 * j + 1 - core)


    def put_back(s, first):
        both = [stack(pad_rows(back_in[j, s]), 2) for j in range(groups)]
        got = dot(jnp.concatenate(both, axis=0), row_mask[s])
        placed[...] = got if first else placed[...] + got

    for k in range(n_gs):
        s = flip(gs, k)
        for j in range(groups):
            if k or j:
                in_copy(j, s).wait_recv()
        put_back(s, k == 0)
    for j in range(groups):
        mine = fold(placed[2 * ROWS_MSG * j : 2 * ROWS_MSG * (j + 1)], 2)
        for c in range(chunks):
            cot_views[core, j, :, c, :] = mine[0:9, c * LANES : (c + 1) * LANES]

    def third_copy(of):
        return pltpu.make_async_remote_copy(
            src_ref=cot_views.at[of],
            dst_ref=cot_views.at[of],
            send_sem=send_three.at[0],
            recv_sem=recv_three.at[0],
            device_id=(gs, flip(view, 1)),
            device_id_type=MESH,
        )

    third_copy(core).start()

    def pull_half(h):
        side = core if h == 0 else 1 - core
        total = None
        tints = []
        for j in range(groups):
            cots = [cot_views[side, j, i] for i in range(9)]
            got, shades = pull_view(kept.at[h, j], cots, inv_depth, jac_diag, spread)
            total = got if total is None else [a + b for a, b in zip(total, got)]
            tints.append(shades)
        for i in range(15):
            if h == 0:
                g_sum[i] = total[i]
            else:
                total[i] = total[i] + g_sum[i]
        for k in range(SH):
            for c in range(3):
                part = None
                for j in range(groups):
                    term = tints[j][c] * (sh_c0 if k == 0 else kept[h, j, 26 + k])
                    part = term if part is None else part + term
                if h == 1:
                    part = part + g_par[:, c * SH + k, :]
                g_par[:, c * SH + k, :] = part
        return total

    pull_half(0)
    third_copy(1 - core).wait_recv()
    total = pull_half(1)
    d_top, d_low, d_base = total[0:3], total[3:6], total[6:9]
    d_x, d_y, d_z, d_diag, d_inv, d_log = total[9:15]
    for j in range(3):
        d_diag = d_diag + d_top[j] * spread[0][j] + d_low[j] * spread[1][j]
    d_inv = d_inv + focal_length * d_diag
    d_z = d_z - inv_depth * inv_depth * d_inv
    d_quats, d_scales = pull_spread(
        [[jac_diag * x for x in d_top], [jac_diag * x for x in d_low], list(d_base)]
    )
    decay = jnp.exp(-p_opacity)
    opacity_out[...] = d_log * decay / (1.0 + decay)
    for i, x in enumerate([d_x, d_y, d_z]):
        g_par[:, 48 + i, :] = x
    for i in range(4):
        g_par[:, 56 + i, :] = d_quats[i]
    for i in range(3):
        g_par[:, 64 + i, :] = d_scales[i]
    for c in range(chunks):
        cols = slice(c * LANES, (c + 1) * LANES)
        sh_out[:, cols] = g_par[c, 0:48, :]
        means_out[:, cols] = g_par[c, 48:51, :]
        quats_out[:, cols] = g_par[c, 56:60, :]
        scales_out[:, cols] = g_par[c, 64:67, :]

    for k in near:
        first_copy(flip(gs, k), gs).wait_send()
    for k in range(1, n_view):
        cam_copy(lax.rem(view + k, n_view), view).wait_send()
    for k in range(n_gs):
        for j in range(groups):
            if k or j:
                out_copy(j, flip(gs, k)).wait_send()
    third_copy(core).wait_send()


def store_kernel(*refs):
    count = len(refs) // 2
    sources, places, sems = refs[:count], refs[count : 2 * count], refs[-1]
    stores = [
        pltpu.make_async_copy(src, dst, sems.at[k])
        for k, (src, dst) in enumerate(zip(sources, places))
    ]
    for store in stores:
        store.start()
    for store in stores:
        store.wait()


def far_kernel(
    n_gs,
    n_view,
    means_in,
    quats_in,
    scales_in,
    opacity_in,
    sh_in,
    camera_in,
    targets_in,
    send_in,
    lists_in,
    lens_in,
    pic_out,
    views_out,
    par,
    opacity,
    send,
    means,
    quats,
    scales,
    sh,
    camera,
    targets,
    lists,
    lens,
    row_buf,
    msg_out,
    msg_in,
    tile_buf,
    ratio_buf,
    weight_buf,
    pic,
    halo,
    t_halo,
    cot,
    back_out,
    back_in,
    placed,
    load_sems,
    send_one,
    recv_one,
    send_halo,
    recv_halo,
    send_tgt,
    recv_tgt,
    send_two,
    recv_two,
    send_three,
    recv_three,
):
    loads = [
        pltpu.make_async_copy(src, dst, load_sems.at[k])
        for k, (src, dst) in enumerate(
            [
                (sh_in, sh),
                (means_in, means),
                (quats_in, quats),
                (scales_in, scales),
                (opacity_in, opacity),
                (camera_in, camera),
                (send_in, send),
                (targets_in, targets),
                (lists_in.at[0, 0], lists),
                (lens_in.at[0], lens),
            ]
        )
    ]
    for load in loads:
        load.start()
    gs = lax.axis_index("gs")
    view = lax.axis_index("view")
    chunks = means.shape[1] // LANES
    cap = send.shape[2]
    shard = means.shape[1]
    tiles = lists.shape[0]
    list_size = lists.shape[1]
    has_up = gs > 0
    has_down = gs < n_gs - 1

    barrier = pltpu.get_barrier_semaphore()

    def greet(strip, cam):
        pl.semaphore_signal(barrier, inc=1, device_id=(strip, cam), device_id_type=MESH)

    loop(1, n_gs, lambda k: greet(lax.rem(gs + k, n_gs), view))
    loop(1, n_view, lambda k: greet(gs, lax.rem(view + k, n_view)))

    for load in loads:
        load.wait()

    for c in range(chunks):
        cols = slice(c * LANES, (c + 1) * LANES)
        par[c, 0:48, :] = sh[:, cols]
        par[c, 48:51, :] = means[:, cols]
        par[c, 56:60, :] = quats[:, cols]
        par[c, 64:67, :] = scales[:, cols]

    centre_x = 0.5 * tiles * TILE
    centre_y = 0.5 * n_gs * TILE
    cam_x = camera[0:1, 0:1]
    cam_y = camera[0:1, 1:2]
    rows = project(*params(par, opacity), [(cam_x, cam_y)], centre_x, centre_y)[0]
    row_buf[...] = jnp.zeros_like(row_buf)
    for i in range(9):
        row_buf[:, i, :] = rows[i]
    table = stack(jnp.concatenate([row_buf[c] for c in range(chunks)], axis=1), 3)

    def fill(d):
        msg_out[d] = fold(dot(table, pick_of(send, d, shard)), 3)

    def first_copy(d, s):
        return pltpu.make_async_remote_copy(
            src_ref=msg_out.at[d],
            dst_ref=msg_in.at[s],
            send_sem=send_one.at[d],
            recv_sem=recv_one.at[s],
            device_id=(d, view),
            device_id_type=MESH,
        )

    pl.semaphore_wait(barrier, n_gs + n_view - 2)

    def send_first(k):
        d = lax.rem(gs + k, n_gs)
        fill(d)
        first_copy(d, gs).start()

    loop(1, n_gs, send_first)
    fill(gs)
    msg_in[gs] = msg_out[gs]

    def halo_copy(src, dst, sends, recvs, side):
        other = gs + 1 if side == 0 else gs - 1
        return pltpu.make_async_remote_copy(
            src_ref=src,
            dst_ref=dst.at[side],
            send_sem=sends.at[side],
            recv_sem=recvs.at[side],
            device_id=(other, view),
            device_id_type=MESH,
        )

    def exchange(src, dst, sends, recvs, start):
        def act(copy, recv):
            if start:
                if not recv:
                    copy.start()
            elif recv:
                copy.wait_recv()
            else:
                copy.wait_send()

        for recv in (False, True):
            if start and recv:
                continue

            @pl.when(has_down)
            def _():
                act(halo_copy(src, dst, sends, recvs, 1 if recv else 0), recv)

            @pl.when(has_up)
            def _():
                act(halo_copy(src, dst, sends, recvs, 0 if recv else 1), recv)

    exchange(targets.at[0], t_halo, send_tgt, recv_tgt, True)

    @pl.when(jnp.logical_not(has_up))
    def _():
        halo[0] = jnp.zeros_like(halo[0])
        t_halo[0] = jnp.zeros_like(t_halo[0])

    @pl.when(jnp.logical_not(has_down))
    def _():
        halo[1] = jnp.zeros_like(halo[1])
        t_halo[1] = jnp.zeros_like(t_halo[1])


    slot_row = lax.broadcasted_iota(jnp.int32, (cap, list_size), 0)

    def slot_pick(s, t):
        return jnp.where(slot_row + s * cap == lists[t : t + 1, :], 1.0, 0.0).astype(bf16)

    tile_buf[...] = jnp.zeros_like(tile_buf)

    def gather(s):
        got = stack(msg_in[s], 3)
        for t in range(tiles):
            tile_buf[t] += fold(dot(got, slot_pick(s, t)), 3)

    gather(gs)

    def gather_next(k):
        s = lax.rem(gs + n_gs - k, n_gs)
        first_copy(gs, s).wait_recv()
        gather(s)

    loop(1, n_gs, gather_next)

    diagonal = lax.broadcasted_iota(jnp.int32, (tiles, tiles), 0) == lax.broadcasted_iota(
        jnp.int32, (tiles, tiles), 1
    )
    used = jnp.sum(jnp.where(diagonal, lens[...].astype(f32), 0.0), axis=1, keepdims=True)
    entry = lax.broadcasted_iota(jnp.int32, (tiles, list_size), 1)
    live = entry.astype(f32) < used
    mid_q = (lax.broadcasted_iota(jnp.int32, (tiles, list_size), 0) * TILE + TILE // 2).astype(f32)
    mid_r = (gs * TILE + TILE // 2).astype(f32)
    off_u = tile_buf[:, 0, :] - mid_q
    off_w = tile_buf[:, 1, :] - mid_r
    k0 = tile_buf[:, 2, :]
    k1 = tile_buf[:, 3, :]
    k2 = tile_buf[:, 4, :]
    lin_u = k0 * off_u + k1 * off_w
    lin_w = k2 * off_w + k1 * off_u
    terms = [
        jnp.where(live, tile_buf[:, 5, :] - 0.5 * (off_u * lin_u + off_w * lin_w), -10000.0),
        jnp.where(live, lin_u, 0.0),
        jnp.where(live, lin_w, 0.0),
        jnp.where(live, -0.5 * k0, 0.0),
        jnp.where(live, -k1, 0.0),
        jnp.where(live, -0.5 * k2, 0.0),
    ]
    term_t = jnp.transpose(jnp.concatenate(pieces(jnp.concatenate(terms, axis=0), 3), axis=0))
    term_t = term_t.astype(bf16)
    colour = jnp.concatenate([tile_buf[:, 6 + c, :] for c in range(3)], axis=0)
    col_hi, col_lo = pieces(colour, 2)
    col_two = jnp.concatenate([col_hi, col_lo], axis=0)
    col_wide = jnp.concatenate([col_two, col_two], axis=1).astype(bf16)
    col_t = jnp.transpose(jnp.concatenate([col_hi, col_lo, col_hi], axis=0)).astype(bf16)

    n_chunk, _, wide = weight_buf.shape
    width = tiles * TILE
    lane = lax.broadcasted_iota(jnp.int32, (tiles, wide), 1)
    in_tile = lax.rem(lane, width) // TILE == lax.broadcasted_iota(jnp.int32, (tiles, wide), 0)

    off_q = (lax.rem(lane, TILE) - TILE // 2).astype(f32)
    half_r = (lane // width).astype(f32)

    def basis(i):
        off_r = half_r + float(i * (wide // width) - TILE // 2)
        out = [jnp.ones_like(off_q), off_q, off_r, off_q * off_q, off_q * off_r, off_r * off_r]
        return jnp.concatenate([jnp.where(in_tile, x, 0.0) for x in out], axis=0).astype(bf16)

    shape = (list_size, 2 * list_size)
    list_row = lax.broadcasted_iota(jnp.int32, shape, 0)
    list_col = lax.rem(lax.broadcasted_iota(jnp.int32, shape, 1), list_size)
    prefix = jnp.where(list_col < list_row, 1.0, 0.0).astype(bf16)
    suffix = jnp.where(list_col > list_row, 1.0, 0.0).astype(bf16)

    for i in range(n_chunk):
        base = basis(i)
        alpha = jnp.exp(dot(term_t, jnp.concatenate([base, base, base], axis=0)))
        keep = 1.0 - alpha
        weight = alpha * jnp.exp(dot(prefix, stack(jnp.log(keep), 2)))
        ratio_buf[i] = alpha / keep
        weight_buf[i] = weight
        drawn = fold(dot(col_wide, stack(weight, 2)), 2)
        for c in range(3):
            mine = jnp.where(in_tile, drawn[c * tiles : (c + 1) * tiles], 0.0)
            line = jnp.sum(mine, axis=0, keepdims=True)
            for half in range(wide // width):
                row = i * (wide // width) + half
                pic[c, row : row + 1, :] = line[:, half * width : (half + 1) * width]

    exchange(pic, halo, send_halo, recv_halo, True)
    pic_out[0] = pic[...]
    exchange(targets.at[0], t_halo, send_tgt, recv_tgt, False)
    exchange(pic, halo, send_halo, recv_halo, False)

    tall = 2 * TILE
    across = band(width, width, 0)
    stacked = []
    images = []
    for c in range(3):
        img = jnp.concatenate([halo[0, c], pic[c], halo[1, c]], axis=0)
        tgt = jnp.concatenate([t_halo[0, c], targets[0, c], t_halo[1, c]], axis=0)
        images.append((img, tgt))
        stacked += [img, tgt, img * img, tgt * tgt, img * tgt]
    down = dot_exact(band(tall, 3 * TILE, TILE // 2), jnp.concatenate(stacked, axis=1))
    down = jnp.concatenate([down[:, i * width : (i + 1) * width] for i in range(15)], axis=0)
    blurred = dot_exact(down, across)
    at_row = lax.broadcasted_iota(jnp.int32, (tall, width), 0) + gs * TILE - TILE // 2
    inside = jnp.logical_and(at_row >= 0, at_row < n_gs * TILE)
    scale = -ssim_weight / (TILE * TILE)
    cots = []
    for c in range(3):
        mean_x, mean_y, raw_xx, raw_yy, raw_xy = [
            blurred[(5 * c + i) * tall : (5 * c + i + 1) * tall] for i in range(5)
        ]
        top_a = 2.0 * mean_x * mean_y + ssim_one
        top_b = 2.0 * (raw_xy - mean_x * mean_y) + ssim_two
        low_c = mean_x * mean_x + mean_y * mean_y + ssim_one
        low_d = (raw_xx - mean_x * mean_x) + (raw_yy - mean_y * mean_y) + ssim_two
        inv_cd = 1.0 / (low_c * low_d)
        inv_dd = inv_cd * low_c
        ssim = top_a * top_b * inv_cd
        d_mean = 2.0 * mean_y * (top_b - top_a) * inv_cd - 2.0 * mean_x * ssim * (
            inv_cd * low_d - inv_dd
        )
        d_xx = -ssim * inv_dd
        d_xy = 2.0 * top_a * inv_cd
        cots += [jnp.where(inside, scale * part, 0.0) for part in (d_mean, d_xx, d_xy)]
    spread = dot_exact(band(TILE, tall, TILE // 2), jnp.concatenate(cots, axis=1))
    spread = jnp.concatenate([spread[:, i * width : (i + 1) * width] for i in range(9)], axis=0)
    spread = dot_exact(spread, across)
    grad_rows = []
    for c in range(3):
        img = pic[c]
        tgt = targets[0, c]
        s_mean, s_xx, s_xy = [spread[(3 * c + i) * TILE : (3 * c + i + 1) * TILE] for i in range(3)]
        res = img - tgt
        direct = (1.0 - ssim_weight) / (TILE * TILE) * res / jnp.sqrt(res * res + charb_eps)
        grad_rows.append(direct + s_mean + 2.0 * img * s_xx + tgt * s_xy)

    d_terms = jnp.zeros((6 * tiles, list_size), f32)
    d_colour = jnp.zeros((3 * tiles, list_size), f32)
    for i in range(n_chunk):
        per = wide // width
        parts = []
        for c in range(3):
            line = jnp.concatenate(
                [grad_rows[c][i * per + half : i * per + half + 1] for half in range(per)], axis=1
            )
            parts.append(jnp.where(in_tile, line, 0.0))
        hi, lo = pieces(jnp.concatenate(parts, axis=0), 2)
        shade = dot(col_t, jnp.concatenate([hi, hi, lo], axis=0).astype(bf16))
        weight = weight_buf[i]
        share = weight * shade
        d_power = share - ratio_buf[i] * dot(suffix, stack(share, 2))
        both = dot_t(basis(i), stack(d_power, 2))
        d_terms = d_terms + both[:, :list_size] + both[:, list_size:]
        both = fold(dot_t(jnp.concatenate([hi, lo], axis=0).astype(bf16), stack(weight, 2)), 2)
        d_colour = d_colour + both[:, :list_size] + both[:, list_size:]

    d0, d1, d2, d3, d4, d5 = [d_terms[k * tiles : (k + 1) * tiles] for k in range(6)]
    e1 = d1 - off_u * d0
    e2 = d2 - off_w * d0
    cot[...] = jnp.zeros_like(cot)
    cot[:, 0, :] = k0 * e1 + k1 * e2
    cot[:, 1, :] = k2 * e2 + k1 * e1
    cot[:, 2, :] = -0.5 * d3 + off_u * (d1 - 0.5 * off_u * d0)
    cot[:, 3, :] = off_w * e1 + off_u * d2 - d4
    cot[:, 4, :] = -0.5 * d5 + off_w * (d2 - 0.5 * off_w * d0)
    cot[:, 5, :] = d0
    for c in range(3):
        cot[:, 6 + c, :] = d_colour[c * tiles : (c + 1) * tiles]
    cot_pieces = [stack(cot[t], 3) for t in range(tiles)]

    def scatter(s):
        total = jnp.zeros((3 * ROWS_MSG, cap), f32)
        for t in range(tiles):
            total = total + dot_t(cot_pieces[t], slot_pick(s, t))
        back_out[s] = fold(total, 3)

    def second_copy(d, s):
        return pltpu.make_async_remote_copy(
            src_ref=back_out.at[d],
            dst_ref=back_in.at[s],
            send_sem=send_two.at[d],
            recv_sem=recv_two.at[s],
            device_id=(d, view),
            device_id_type=MESH,
        )

    def send_second(k):
        d = lax.rem(gs + k, n_gs)
        scatter(d)
        second_copy(d, gs).start()

    loop(1, n_gs, send_second)
    scatter(gs)
    back_in[gs] = back_out[gs]
    placed[...] = jnp.zeros_like(placed)

    def put_back(s):
        placed[...] += dot_t(stack(back_in[s], 3), pick_of(send, s, shard))

    put_back(gs)

    def put_next(k):
        s = lax.rem(gs + n_gs - k, n_gs)
        second_copy(gs, s).wait_recv()
        put_back(s)

    loop(1, n_gs, put_next)
    whole = fold(placed[...], 3)
    for c in range(chunks):
        views_out[view, 0:9, c, :] = whole[0:9, c * LANES : (c + 1) * LANES]
    first_row = lax.broadcasted_iota(jnp.int32, (chunks, LANES), 0) == 0
    views_out[view, 9] = jnp.where(first_row, cam_x, cam_y)

    def third_copy(to, of):
        return pltpu.make_async_remote_copy(
            src_ref=views_out.at[of],
            dst_ref=views_out.at[of],
            send_sem=send_three.at[to],
            recv_sem=recv_three.at[of],
            device_id=(gs, to),
            device_id_type=MESH,
        )

    def send_third(k):
        third_copy(lax.rem(view + k, n_view), view).start()

    def wait_third(k):
        third_copy(view, lax.rem(view + n_view - k, n_view)).wait_recv()

    loop(1, n_view, send_third)
    loop(1, n_view, wait_third)

    def done_first(k):
        first_copy(lax.rem(gs + k, n_gs), gs).wait_send()
        second_copy(lax.rem(gs + k, n_gs), gs).wait_send()

    def done_third(k):
        third_copy(lax.rem(view + k, n_view), view).wait_send()

    loop(1, n_gs, done_first)
    loop(1, n_view, done_third)


def pull_kernel(
    n_view,
    pic,
    views,
    par,
    opacity,
    pic_out,
    means_out,
    quats_out,
    scales_out,
    opacity_out,
    sh_out,
    g_par,
    g_means,
    g_quats,
    g_scales,
    g_opacity,
    g_sh,
    store_sems,
):
    chunks = par.shape[0]
    pic_copy = pltpu.make_async_copy(pic, pic_out, store_sems.at[0])
    pic_copy.start()
    cams = [(views[v, 9, 0:1, 0:1], views[v, 9, 1:2, 0:1]) for v in range(n_view)]
    _, pull = jax.vjp(lambda *args: project(*args, cams, 0.0, 0.0), *params(par, opacity))
    grads = pull([[views[v, i] for i in range(9)] for v in range(n_view)])
    for i in range(3):
        g_par[:, 48 + i, :] = grads[0][i]
        g_par[:, 64 + i, :] = grads[2][i]
    for i in range(4):
        g_par[:, 56 + i, :] = grads[1][i]
    for i in range(48):
        g_par[:, i, :] = grads[4][i]
    g_opacity[...] = grads[3]
    for c in range(chunks):
        cols = slice(c * LANES, (c + 1) * LANES)
        g_sh[:, cols] = g_par[c, 0:48, :]
        g_means[:, cols] = g_par[c, 48:51, :]
        g_quats[:, cols] = g_par[c, 56:60, :]
        g_scales[:, cols] = g_par[c, 64:67, :]
    stores = [
        pltpu.make_async_copy(src, dst, store_sems.at[k + 1])
        for k, (src, dst) in enumerate(
            [
                (g_sh, sh_out),
                (g_means, means_out),
                (g_quats, quats_out),
                (g_scales, scales_out),
                (g_opacity, opacity_out),
            ]
        )
    ]
    for store in stores:
        store.start()
    pic_copy.wait()
    for store in stores:
        store.wait()


def far_shards(
    means, quats, log_scales, opacity, sh_coeffs, cameras, targets, send_rows, tile_lists, list_lengths
):
    n_gs = lax.axis_size("gs")
    n_view = lax.axis_size("view")
    shard = means.shape[1]
    chunks = shard // LANES
    cap = send_rows.shape[2]
    tiles, list_size = tile_lists.shape[2:]
    width = tiles * TILE
    n_chunk = TILE // 2
    wide = 2 * width
    opacity = opacity.reshape(chunks, LANES)
    args = (
        means,
        quats,
        log_scales,
        opacity,
        sh_coeffs,
        cameras,
        targets,
        send_rows,
        tile_lists,
        list_lengths,
    )
    shape = jax.ShapeDtypeStruct
    dma = pltpu.SemaphoreType.DMA
    vmem = pl.BlockSpec(memory_space=VMEM)
    hbm = pl.BlockSpec(memory_space=pltpu.HBM)
    mids = pl.pallas_call(
        lambda *refs: far_kernel(n_gs, n_view, *refs),
        out_shape=(
            shape(targets.shape, f32),
            shape((n_view, 10, chunks, LANES), f32),
            shape((chunks, 72, LANES), f32),
            shape((chunks, LANES), f32),
        ),
        in_specs=[hbm] * len(args),
        out_specs=(vmem,) * 4,
        scratch_shapes=[
            VMEM(send_rows.shape, jnp.int32),
            VMEM(means.shape, f32),
            VMEM(quats.shape, f32),
            VMEM(log_scales.shape, f32),
            VMEM(sh_coeffs.shape, f32),
            VMEM(cameras.shape, f32),
            VMEM(targets.shape, f32),
            VMEM((tiles, list_size), jnp.int32),
            VMEM((1, tiles), jnp.int32),
            VMEM((chunks, ROWS_MSG, LANES), f32),
            VMEM((n_gs, ROWS_MSG, cap), f32),
            VMEM((n_gs, ROWS_MSG, cap), f32),
            VMEM((tiles, ROWS_MSG, list_size), f32),
            VMEM((n_chunk, list_size, wide), f32),
            VMEM((n_chunk, list_size, wide), f32),
            VMEM((3, TILE, width), f32),
            VMEM((2, 3, TILE, width), f32),
            VMEM((2, 3, TILE, width), f32),
            VMEM((tiles, ROWS_MSG, list_size), f32),
            VMEM((n_gs, ROWS_MSG, cap), f32),
            VMEM((n_gs, ROWS_MSG, cap), f32),
            VMEM((3 * ROWS_MSG, shard), f32),
            dma((10,)),
            dma((n_gs,)),
            dma((n_gs,)),
            dma((2,)),
            dma((2,)),
            dma((2,)),
            dma((2,)),
            dma((n_gs,)),
            dma((n_gs,)),
            dma((n_view,)),
            dma((n_view,)),
        ],
        compiler_params=pltpu.CompilerParams(
            collective_id=0, has_side_effects=True, vmem_limit_bytes=48 * 1024 * 1024
        ),
    )(*[pltpu.with_memory_space_constraint(x, pltpu.HBM) for x in args])
    outs = pl.pallas_call(
        lambda *refs: pull_kernel(n_view, *refs),
        out_shape=(
            shape(targets.shape, f32),
            shape(means.shape, f32),
            shape(quats.shape, f32),
            shape(log_scales.shape, f32),
            shape((chunks, LANES), f32),
            shape(sh_coeffs.shape, f32),
        ),
        in_specs=[vmem] * 4,
        out_specs=(hbm,) * 6,
        scratch_shapes=[
            VMEM((chunks, 72, LANES), f32),
            VMEM(means.shape, f32),
            VMEM(quats.shape, f32),
            VMEM(log_scales.shape, f32),
            VMEM((chunks, LANES), f32),
            VMEM(sh_coeffs.shape, f32),
            dma((6,)),
        ],
        compiler_params=pltpu.CompilerParams(vmem_limit_bytes=48 * 1024 * 1024),
    )(*mids)
    return (*outs[:4], outs[4].reshape(shard), outs[5])


def shards(
    means, quats, log_scales, opacity, sh_coeffs, cameras, targets, send_rows, tile_lists, list_lengths
):
    n_gs = lax.axis_size("gs")
    n_view = lax.axis_size("view")
    shard = means.shape[1]
    cap = send_rows.shape[2]
    args = (
        means,
        quats,
        log_scales,
        opacity,
        sh_coeffs,
        cameras,
        targets,
        send_rows,
        tile_lists,
        list_lengths,
    )
    if n_gs not in (2, 4, 8) or cap % LANES or n_view % 2:
        return far_shards(*args)
    chunks = shard // LANES
    tiles, list_size = tile_lists.shape[2:]
    width = tiles * TILE
    n_chunk = TILE // 2
    wide = 2 * width
    groups = n_view // 2
    args = args[:3] + (opacity.reshape(chunks, LANES),) + args[4:]
    shape = jax.ShapeDtypeStruct
    dma = pltpu.SemaphoreType.DMA
    vmem = pl.BlockSpec(memory_space=VMEM)
    hbm = pl.BlockSpec(memory_space=pltpu.HBM)
    out_shape = (
        shape(targets.shape, f32),
        shape(means.shape, f32),
        shape(quats.shape, f32),
        shape(log_scales.shape, f32),
        shape((chunks, LANES), f32),
        shape(sh_coeffs.shape, f32),
    )
    mids = pl.pallas_call(
        lambda *refs: near_kernel(n_gs, n_view, *refs),
        out_shape=out_shape,
        in_specs=[hbm] * len(args),
        out_specs=(vmem,) * 6,
        scratch_shapes=[
            VMEM((chunks, 72, LANES), f32),
            VMEM((chunks, LANES), f32),
            VMEM(send_rows.shape, jnp.int32),
            VMEM(means.shape, f32),
            VMEM(quats.shape, f32),
            VMEM(log_scales.shape, f32),
            VMEM(sh_coeffs.shape, f32),
            VMEM(cameras.shape, f32),
            VMEM(targets.shape, f32),
            VMEM((tiles, list_size), jnp.int32),
            VMEM((1, tiles), jnp.int32),
            VMEM((n_view, 1, LANES), f32),
            VMEM((chunks, ROWS_MSG, LANES), f32),
            VMEM((n_gs, 9, cap), f32),
            VMEM((n_gs, 9, cap), f32),
            VMEM((n_gs, cap, tiles * list_size), bf16),
            VMEM((n_gs, tiles * list_size, cap), bf16),
            VMEM((n_gs, cap, shard), bf16),
            VMEM((n_chunk, 6 * tiles, wide), bf16),
            VMEM((n_chunk * wide, 6 * tiles), bf16),
            VMEM((tiles, ROWS_MSG, list_size), f32),
            VMEM((n_chunk, list_size, wide), f32),
            VMEM((n_chunk, list_size, wide), f32),
            VMEM((list_size, 3 * width), f32),
            VMEM((n_chunk, wide, 2 * list_size), bf16),
            VMEM((3, n_chunk, list_size, wide), f32),
            VMEM((3, TILE, width), f32),
            VMEM((2, 3, TILE, width), f32),
            VMEM((2, 3, TILE, width), f32),
            VMEM((tiles, ROWS_MSG, list_size), f32),
            VMEM((n_gs, 9, cap), f32),
            VMEM((groups, n_gs, 9, cap), f32),
            VMEM((2 * ROWS_MSG * groups, shard), f32),
            VMEM((2, groups, N_KEPT, chunks, LANES), f32),
            VMEM((2, groups, 9, chunks, LANES), f32),
            VMEM((15, chunks, LANES), f32),
            VMEM((chunks, 72, LANES), f32),
            dma((10,)),
            dma((n_view,)),
            dma((n_view,)),
            dma((n_gs,)),
            dma((n_gs,)),
            dma((2,)),
            dma((2,)),
            dma((2,)),
            dma((2,)),
            dma((groups, n_gs)),
            dma((groups, n_gs)),
            dma((1,)),
            dma((1,)),
        ],
        compiler_params=pltpu.CompilerParams(
            collective_id=1, has_side_effects=True, vmem_limit_bytes=48 * 1024 * 1024
        ),
    )(*[pltpu.with_memory_space_constraint(x, pltpu.HBM) for x in args])
    outs = pl.pallas_call(
        store_kernel,
        out_shape=out_shape,
        in_specs=[vmem] * 6,
        out_specs=(hbm,) * 6,
        scratch_shapes=[dma((6,))],
        compiler_params=pltpu.CompilerParams(vmem_limit_bytes=48 * 1024 * 1024),
    )(*mids)
    return (*outs[:4], outs[4].reshape(shard), outs[5])


def solution(mesh):
    return jax.shard_map(
        shards,
        mesh=mesh,
        in_specs=(
            P(None, "gs"),
            P(None, "gs"),
            P(None, "gs"),
            P("gs"),
            P(None, "gs"),
            P("view", None),
            P("view", None, "gs", None),
            P("gs", None, None),
            P("view", "gs", None, None),
            P("view", "gs", None),
        ),
        out_specs=(
            P("view", None, "gs", None),
            P(None, "gs"),
            P(None, "gs"),
            P(None, "gs"),
            P("gs"),
            P(None, "gs"),
        ),
        check_vma=False,
    )
```

```python
import math

import jax
import jax.numpy as jnp
import ml_dtypes
import numpy as np
from jax import lax
from jax.experimental import pallas as pl
from jax.experimental.pallas import tpu as pltpu
from jax.sharding import PartitionSpec as P

TILE = 16
SH = 16
RADIUS = 5
LANES = 128
ROWS_MSG = 16
VMEM = pltpu.VMEM
MESH = pl.DeviceIdType.MESH

focal_length = 1000.0
cov_blur = 0.3
ssim_weight = 0.2
charb_eps = 0.0001
ssim_one = 0.0001
ssim_two = 0.0009
sh_c0 = 0.28209479177387814
sh_c1 = 0.4886025119029199
sh_c2 = [
    1.0925484305920792,
    -1.0925484305920792,
    0.31539156525252005,
    -1.0925484305920792,
    0.5462742152960396,
]
sh_c3 = [
    -0.5900435899266435,
    2.890611442640554,
    -0.4570457994644658,
    0.3731763325901154,
    -0.4570457994644658,
    1.445305721320277,
    -0.5900435899266435,
]

f32 = jnp.float32
bf16 = jnp.bfloat16


def sh_basis(dir_x, dir_y, dir_z):
    sq_x = dir_x * dir_x
    sq_y = dir_y * dir_y
    sq_z = dir_z * dir_z
    return [
        None,
        -sh_c1 * dir_y,
        sh_c1 * dir_z,
        -sh_c1 * dir_x,
        sh_c2[0] * dir_x * dir_y,
        sh_c2[1] * dir_y * dir_z,
        sh_c2[2] * (2.0 * sq_z - sq_x - sq_y),
        sh_c2[3] * dir_x * dir_z,
        sh_c2[4] * (sq_x - sq_y),
        sh_c3[0] * dir_y * (3.0 * sq_x - sq_y),
        sh_c3[1] * dir_x * dir_y * dir_z,
        sh_c3[2] * dir_y * (4.0 * sq_z - sq_x - sq_y),
        sh_c3[3] * dir_z * (2.0 * sq_z - 3.0 * sq_x - 3.0 * sq_y),
        sh_c3[4] * dir_x * (4.0 * sq_z - sq_x - sq_y),
        sh_c3[5] * dir_z * (sq_x - sq_y),
        sh_c3[6] * dir_x * (sq_x - 3.0 * sq_y),
    ]


def project(means, quats, log_scales, opacity, coeffs, cameras, centre_x, centre_y):
    inv_norm = 1.0 / jnp.sqrt(
        quats[0] * quats[0] + quats[1] * quats[1] + quats[2] * quats[2] + quats[3] * quats[3]
    )
    quat_w, quat_x, quat_y, quat_z = [quat * inv_norm for quat in quats]
    scales = [jnp.exp(log_scale) for log_scale in log_scales]
    rotation = [
        [
            1.0 - 2.0 * (quat_y * quat_y + quat_z * quat_z),
            2.0 * (quat_x * quat_y - quat_w * quat_z),
            2.0 * (quat_x * quat_z + quat_w * quat_y),
        ],
        [
            2.0 * (quat_x * quat_y + quat_w * quat_z),
            1.0 - 2.0 * (quat_x * quat_x + quat_z * quat_z),
            2.0 * (quat_y * quat_z - quat_w * quat_x),
        ],
        [
            2.0 * (quat_x * quat_z - quat_w * quat_y),
            2.0 * (quat_y * quat_z + quat_w * quat_x),
            1.0 - 2.0 * (quat_x * quat_x + quat_y * quat_y),
        ],
    ]
    spread = [[rotation[i][j] * scales[j] for j in range(3)] for i in range(3)]
    depth_z = means[2]
    inv_depth = 1.0 / depth_z
    jac_diag = focal_length * inv_depth
    diag_top = [jac_diag * spread[0][j] for j in range(3)]
    diag_low = [jac_diag * spread[1][j] for j in range(3)]
    log_alpha = -jnp.log(1.0 + jnp.exp(-opacity))
    views = []
    for cam_x, cam_y in cameras:
        rel_x = means[0] - cam_x
        rel_y = means[1] - cam_y
        ratio_u = jac_diag * rel_x
        ratio_v = jac_diag * rel_y
        jac_u = -ratio_u * inv_depth
        jac_v = -ratio_v * inv_depth
        top = [diag_top[j] + jac_u * spread[2][j] for j in range(3)]
        low = [diag_low[j] + jac_v * spread[2][j] for j in range(3)]
        cov_a = top[0] * top[0] + top[1] * top[1] + top[2] * top[2] + cov_blur
        cov_b = top[0] * low[0] + top[1] * low[1] + top[2] * low[2]
        cov_c = low[0] * low[0] + low[1] * low[1] + low[2] * low[2] + cov_blur
        inv_det = 1.0 / (cov_a * cov_c - cov_b * cov_b)
        inv_dist = 1.0 / jnp.sqrt(rel_x * rel_x + rel_y * rel_y + depth_z * depth_z)
        basis = sh_basis(rel_x * inv_dist, rel_y * inv_dist, depth_z * inv_dist)
        colours = []
        for channel in range(3):
            total = sh_c0 * coeffs[channel * SH] + 0.5
            for k in range(1, SH):
                total = total + coeffs[channel * SH + k] * basis[k]
            colours.append(jnp.maximum(total, 0.0))
        views.append(
            [
                ratio_u + centre_x,
                ratio_v + centre_y,
                cov_c * inv_det,
                -cov_b * inv_det,
                cov_a * inv_det,
                log_alpha,
            ]
            + colours
        )
    return views


def window_taps():
    raw_taps = [math.exp(-((tap_idx - RADIUS) ** 2) / 4.5) for tap_idx in range(2 * RADIUS + 1)]
    total = sum(raw_taps)
    return [tap / total for tap in raw_taps]


def band(out_count, in_count, offset):
    taps = window_taps()
    shape = (out_count, in_count)
    gap = lax.broadcasted_iota(jnp.int32, shape, 1) - lax.broadcasted_iota(jnp.int32, shape, 0)
    gap = jnp.abs(gap - offset)
    matrix = jnp.zeros(shape, f32)
    for far in range(RADIUS + 1):
        matrix = jnp.where(gap == far, taps[RADIUS + far], matrix)
    return matrix


def pieces(x, count):
    out = []
    for _ in range(count - 1):
        part = x.astype(bf16).astype(f32)
        out.append(part)
        x = x - part
    out.append(x)
    return out


def stack(x, count, axis=0):
    return jnp.concatenate(pieces(x, count), axis=axis).astype(bf16)


def dot(a, b):
    return lax.dot_general(a, b, (((1,), (0,)), ((), ())), preferred_element_type=f32)


def dot_t(a, b):
    return lax.dot_general(a, b, (((1,), (1,)), ((), ())), preferred_element_type=f32)


def dot_exact(a, b):
    return lax.dot_general(
        a, b, (((1,), (0,)), ((), ())), precision=lax.Precision.HIGHEST, preferred_element_type=f32
    )


def fold(x, count):
    size = x.shape[0] // count
    total = x[:size]
    for i in range(1, count):
        total = total + x[i * size : (i + 1) * size]
    return total


def loop(low, high, step):
    if high - low <= 8:
        for i in range(low, high):
            step(i)
    else:

        @pl.loop(low, high)
        def _(i):
            step(i)


def params(par, opacity):
    return (
        [par[:, 48 + i, :] for i in range(3)],
        [par[:, 56 + i, :] for i in range(4)],
        [par[:, 64 + i, :] for i in range(3)],
        opacity[...],
        [par[:, i, :] for i in range(48)],
    )


def pick_of(send, d, shard):
    local_row = lax.broadcasted_iota(jnp.int32, (shard, send.shape[2]), 0)
    return jnp.where(local_row == send[0, pl.ds(d, 1), :], 1.0, 0.0).astype(bf16)


def split_taps():
    high = [float(np.asarray(tap, ml_dtypes.bfloat16)) for tap in window_taps()]
    return high, [float(tap) - top for tap, top in zip(window_taps(), high)]


def band_split(out_count, in_rows, offset, axis):
    high, low = split_taps()
    count = len(in_rows)
    shape = (out_count, 3 * count) if axis == 1 else (3 * count, out_count)
    inner = lax.broadcasted_iota(jnp.int32, shape, axis)
    part = inner // count
    place = lax.rem(inner, count)
    start = in_rows[0]
    jump = [k for k in range(1, count) if in_rows[k] != in_rows[k - 1] + 1]
    row = place + start
    for k in jump:
        row = row + jnp.where(place >= k, in_rows[k] - in_rows[k - 1] - 1, 0)
    gap = jnp.abs(row - lax.broadcasted_iota(jnp.int32, shape, 1 - axis) - offset)
    matrix = jnp.zeros(shape, f32)
    for far in range(RADIUS + 1):
        tap = jnp.where(part == 2, low[RADIUS + far], high[RADIUS + far])
        matrix = jnp.where(gap == far, tap, matrix)
    return matrix.astype(bf16)


def stack_mixed(x, axis):
    high, low = pieces(x, 2)
    return jnp.concatenate([high, low, high], axis=axis).astype(bf16)


def side_by_side(x, count):
    size = x.shape[1] // count
    return jnp.concatenate([x[:, i * size : (i + 1) * size] for i in range(count)], axis=0)


def pad_rows(x):
    return jnp.concatenate([x, jnp.zeros((ROWS_MSG - x.shape[0], x.shape[1]), f32)], axis=0)


def flip(index, bits):
    bit = 1
    while bit <= bits:
        if bits & bit:
            index = index + bit * (1 - 2 * lax.rem(lax.div(index, bit), 2))
        bit *= 2
    return index


def spread_of(quats, log_scales):
    inv_norm = 1.0 / jnp.sqrt(
        quats[0] * quats[0] + quats[1] * quats[1] + quats[2] * quats[2] + quats[3] * quats[3]
    )
    w, x, y, z = [quat * inv_norm for quat in quats]
    rotation = [
        [1.0 - 2.0 * (y * y + z * z), 2.0 * (x * y - w * z), 2.0 * (x * z + w * y)],
        [2.0 * (x * y + w * z), 1.0 - 2.0 * (x * x + z * z), 2.0 * (y * z - w * x)],
        [2.0 * (x * z - w * y), 2.0 * (y * z + w * x), 1.0 - 2.0 * (x * x + y * y)],
    ]
    scales = [jnp.exp(log_scale) for log_scale in log_scales]
    return [[rotation[i][j] * scales[j] for j in range(3)] for i in range(3)]


def basis_slopes(x, y, z):
    xx, yy, zz = x * x, y * y, z * z
    xy, yz, xz = x * y, y * z, x * z
    gap = xx - yy
    four = 4.0 * zz
    return [
        {
            3: -sh_c1,
            4: sh_c2[0] * y,
            6: -2.0 * sh_c2[2] * x,
            7: sh_c2[3] * z,
            8: 2.0 * sh_c2[4] * x,
            9: 6.0 * sh_c3[0] * xy,
            10: sh_c3[1] * yz,
            11: -2.0 * sh_c3[2] * xy,
            12: -6.0 * sh_c3[3] * xz,
            13: sh_c3[4] * (four - 3.0 * xx - yy),
            14: 2.0 * sh_c3[5] * xz,
            15: 3.0 * sh_c3[6] * gap,
        },
        {
            1: -sh_c1,
            4: sh_c2[0] * x,
            5: sh_c2[1] * z,
            6: -2.0 * sh_c2[2] * y,
            8: -2.0 * sh_c2[4] * y,
            9: 3.0 * sh_c3[0] * gap,
            10: sh_c3[1] * xz,
            11: sh_c3[2] * (four - xx - 3.0 * yy),
            12: -6.0 * sh_c3[3] * yz,
            13: -2.0 * sh_c3[4] * xy,
            14: -2.0 * sh_c3[5] * yz,
            15: -6.0 * sh_c3[6] * xy,
        },
        {
            2: sh_c1,
            5: sh_c2[1] * y,
            6: 4.0 * sh_c2[2] * z,
            7: sh_c2[3] * x,
            10: sh_c3[1] * xy,
            11: 8.0 * sh_c3[2] * yz,
            12: sh_c3[3] * (6.0 * zz - 3.0 * xx - 3.0 * yy),
            13: 8.0 * sh_c3[4] * xz,
            14: sh_c3[5] * gap,
        },
    ]


N_KEPT = 42


def keep_view(kept, par, spread, means, inv_depth, jac_diag, cam_x, cam_y):
    rel_x = means[0] - cam_x
    rel_y = means[1] - cam_y
    ratio_u = jac_diag * rel_x
    ratio_v = jac_diag * rel_y
    jac_u = -ratio_u * inv_depth
    jac_v = -ratio_v * inv_depth
    top = [jac_diag * spread[0][j] + jac_u * spread[2][j] for j in range(3)]
    low = [jac_diag * spread[1][j] + jac_v * spread[2][j] for j in range(3)]
    cov_a = top[0] * top[0] + top[1] * top[1] + top[2] * top[2] + cov_blur
    cov_b = top[0] * low[0] + top[1] * low[1] + top[2] * low[2]
    cov_c = low[0] * low[0] + low[1] * low[1] + low[2] * low[2] + cov_blur
    inv_det = 1.0 / (cov_a * cov_c - cov_b * cov_b)
    out = [rel_x, rel_y, ratio_u, ratio_v, jac_u, jac_v] + top + low
    out += [cov_c * inv_det, -cov_b * inv_det, cov_a * inv_det]
    for i, x in enumerate(out):
        kept[i] = x
    inv_dist = 1.0 / jnp.sqrt(rel_x * rel_x + rel_y * rel_y + means[2] * means[2])
    turn = [rel_x * inv_dist, rel_y * inv_dist, means[2] * inv_dist]
    basis = sh_basis(*turn)
    slopes = basis_slopes(*turn)
    for k in range(1, SH):
        kept[26 + k] = basis[k]
    for channel in range(3):
        raw = sh_c0 * par[:, channel * SH, :] + 0.5
        slope = [None, None, None]
        for k in range(1, SH):
            coeff = par[:, channel * SH + k, :]
            raw = raw + coeff * basis[k]
            for i in range(3):
                if k in slopes[i]:
                    term = coeff * slopes[i][k]
                    slope[i] = term if slope[i] is None else slope[i] + term
        along = turn[0] * slope[0] + turn[1] * slope[1] + turn[2] * slope[2]
        for i in range(3):
            kept[15 + 3 * channel + i] = (slope[i] - turn[i] * along) * inv_dist
        kept[24 + channel] = jnp.where(raw > 0.0, 1.0, jnp.where(raw == 0.0, 0.5, 0.0))


def pull_view(kept, cots, inv_depth, jac_diag, spread):
    rel_x, rel_y, ratio_u, ratio_v, jac_u, jac_v = [kept[i] for i in range(6)]
    top = [kept[6 + j] for j in range(3)]
    low = [kept[9 + j] for j in range(3)]
    k0, k1, k2 = [kept[12 + i] for i in range(3)]
    g0, g1, g2 = cots[2], cots[3], cots[4]
    cov_a = -(k0 * k0 * g0 + k0 * k1 * g1 + k1 * k1 * g2)
    cov_b = -2.0 * (k0 * k1 * g0 + k1 * k2 * g2) - (k0 * k2 + k1 * k1) * g1
    cov_c = -(k1 * k1 * g0 + k1 * k2 * g1 + k2 * k2 * g2)
    d_top = [2.0 * cov_a * top[j] + cov_b * low[j] for j in range(3)]
    d_low = [2.0 * cov_c * low[j] + cov_b * top[j] for j in range(3)]
    d_base = [jac_u * d_top[j] + jac_v * d_low[j] for j in range(3)]
    d_jac_u = d_top[0] * spread[2][0] + d_top[1] * spread[2][1] + d_top[2] * spread[2][2]
    d_jac_v = d_low[0] * spread[2][0] + d_low[1] * spread[2][1] + d_low[2] * spread[2][2]
    d_ratio_u = cots[0] - inv_depth * d_jac_u
    d_ratio_v = cots[1] - inv_depth * d_jac_v
    shades = [cots[6 + c] * kept[24 + c] for c in range(3)]
    turn = [
        shades[0] * kept[15 + i] + shades[1] * kept[18 + i] + shades[2] * kept[21 + i]
        for i in range(3)
    ]
    d_x = jac_diag * d_ratio_u + turn[0]
    d_y = jac_diag * d_ratio_v + turn[1]
    d_diag = rel_x * d_ratio_u + rel_y * d_ratio_v
    d_inv = -(ratio_u * d_jac_u + ratio_v * d_jac_v)
    return d_top + d_low + d_base + [d_x, d_y, turn[2], d_diag, d_inv, cots[5]], shades


def octets(x):
    return [x[k : k + 8] for k in range(0, x.shape[0], 8)]


def products_before(parts):
    sub = lax.broadcasted_iota(jnp.int32, parts[0].shape, 0)
    run, before = parts[0], [None]
    for part in parts[1:]:
        before.append(run)
        run = run * part
    lead = jnp.where(sub >= 1, pltpu.roll(run, 1, 0), 1.0)
    for step in (1, 2, 4):
        lead = lead * jnp.where(sub >= step, pltpu.roll(lead, step, 0), 1.0)
    return [lead if x is None else x * lead for x in before]


def sums_after(parts):
    sub = lax.broadcasted_iota(jnp.int32, parts[0].shape, 0)
    run, after = parts[-1], [None]
    for part in parts[-2::-1]:
        after.append(run)
        run = run + part
    tail = jnp.where(sub < 7, pltpu.roll(run, 7, 0), 0.0)
    for step in (1, 2, 4):
        tail = tail + jnp.where(sub < 8 - step, pltpu.roll(tail, 8 - step, 0), 0.0)
    return [tail if x is None else x + tail for x in after[::-1]]


def near_kernel(
    n_gs,
    n_view,
    means_in,
    quats_in,
    scales_in,
    opacity_in,
    sh_in,
    camera_in,
    targets_in,
    send_in,
    lists_in,
    lens_in,
    pic_out,
    means_out,
    quats_out,
    scales_out,
    opacity_out,
    sh_out,
    par,
    opacity,
    send,
    means,
    quats,
    scales,
    sh,
    camera,
    targets,
    lists,
    lens,
    cams,
    row_buf,
    msg_out,
    msg_in,
    slot_mask,
    slot_mask_t,
    row_mask,
    bases,
    bases_t,
    tile_buf,
    ratio_buf,
    weight_buf,
    shade_buf,
    split_buf,
    power_buf,
    pic,
    halo,
    t_halo,
    cot,
    back_out,
    back_in,
    placed,
    kept,
    cot_views,
    g_sum,
    g_par,
    load_sems,
    send_cam,
    recv_cam,
    send_one,
    recv_one,
    send_halo,
    recv_halo,
    send_tgt,
    recv_tgt,
    send_two,
    recv_two,
    send_three,
    recv_three,
):
    gs = lax.axis_index("gs")
    view = lax.axis_index("view")
    shard = means.shape[1]
    chunks = shard // LANES
    cap = send.shape[2]
    tiles, list_size = lists.shape
    groups = n_view // 2
    core = lax.rem(view, 2)
    group = lax.div(view, 2)
    has_up = gs > 0
    has_down = gs < n_gs - 1
    near = range(1, n_gs)
    far = range(n_gs - 1, 0, -1)

    def cousin(j):
        return lax.rem(view + 2 * j, n_view)

    barrier = pltpu.get_barrier_semaphore()

    def greet(strip, cam):
        pl.semaphore_signal(barrier, inc=1, device_id=(strip, cam), device_id_type=MESH)

    for k in range(n_gs - 1, -1, -1):
        for j in range(groups):
            if k or j:
                greet(flip(gs, k), cousin(j))
    for j in range(groups):
        greet(gs, flip(cousin(j), 1))
    greeted = n_gs - 1 + (groups - 1) * n_gs + groups

    loads = [
        pltpu.make_async_copy(src, dst, load_sems.at[k])
        for k, (src, dst) in enumerate(
            [
                (sh_in, sh),
                (means_in, means),
                (quats_in, quats),
                (scales_in, scales),
                (opacity_in, opacity),
                (camera_in, camera),
                (send_in, send),
                (lists_in.at[0, 0], lists),
                (lens_in.at[0], lens),
                (targets_in, targets),
            ]
        )
    ]
    for load in loads:
        load.start()

    for load in loads[:7]:
        load.wait()

    for c in range(chunks):
        cols = slice(c * LANES, (c + 1) * LANES)
        par[c, 0:48, :] = sh[:, cols]
        par[c, 48:51, :] = means[:, cols]
        par[c, 56:60, :] = quats[:, cols]
        par[c, 64:67, :] = scales[:, cols]

    centre_x = 0.5 * tiles * TILE
    centre_y = 0.5 * n_gs * TILE
    cam_x = camera[0:1, 0:1]
    cam_y = camera[0:1, 1:2]
    rows = project(*params(par, opacity), [(cam_x, cam_y)], centre_x, centre_y)[0]
    row_buf[...] = jnp.zeros_like(row_buf)
    for i in range(9):
        row_buf[:, i, :] = rows[i]
    table = stack(jnp.concatenate([row_buf[c] for c in range(chunks)], axis=1), 3)

    def fill(d):
        msg_out[d] = fold(dot(table, pick_of(send, d, shard)), 3)[0:9]

    def first_copy(d, s):
        return pltpu.make_async_remote_copy(
            src_ref=msg_out.at[d],
            dst_ref=msg_in.at[s],
            send_sem=send_one.at[d],
            recv_sem=recv_one.at[s],
            device_id=(d, view),
            device_id_type=MESH,
        )

    for k in far:
        fill(flip(gs, k))
    pl.semaphore_wait(barrier, greeted)

    for k in far:
        first_copy(flip(gs, k), gs).start()
    fill(gs)
    msg_in[gs] = msg_out[gs]

    def cam_copy(to, of):
        return pltpu.make_async_remote_copy(
            src_ref=cams.at[of],
            dst_ref=cams.at[of],
            send_sem=send_cam.at[to],
            recv_sem=recv_cam.at[of],
            device_id=(gs, to),
            device_id_type=MESH,
        )

    lane_one = lax.broadcasted_iota(jnp.int32, (1, LANES), 1)
    cams[view] = jnp.where(lane_one == 0, cam_x, cam_y)
    for k in range(1, n_view):
        cam_copy(lax.rem(view + k, n_view), view).start()

    def halo_copy(src, dst, sends, recvs, side):
        other = gs + 1 if side == 0 else gs - 1
        return pltpu.make_async_remote_copy(
            src_ref=src,
            dst_ref=dst.at[side],
            send_sem=sends.at[side],
            recv_sem=recvs.at[side],
            device_id=(other, view),
            device_id_type=MESH,
        )

    def exchange(src, dst, sends, recvs, start, ends=(False, True)):
        def act(copy, recv):
            if start:
                copy.start()
            elif recv:
                copy.wait_recv()
            else:
                copy.wait_send()

        for recv in ends:
            if start and recv:
                continue

            @pl.when(has_down)
            def _():
                act(halo_copy(src, dst, sends, recvs, 1 if recv else 0), recv)

            @pl.when(has_up)
            def _():
                act(halo_copy(src, dst, sends, recvs, 0 if recv else 1), recv)

    for load in loads[7:]:
        load.wait()
    exchange(targets.at[0], t_halo, send_tgt, recv_tgt, True)

    @pl.when(jnp.logical_not(has_up))
    def _():
        halo[0] = jnp.zeros_like(halo[0])
        t_halo[0] = jnp.zeros_like(t_halo[0])

    @pl.when(jnp.logical_not(has_down))
    def _():
        halo[1] = jnp.zeros_like(halo[1])
        t_halo[1] = jnp.zeros_like(t_halo[1])

    n_chunk, _, wide = weight_buf.shape
    width = tiles * TILE
    per = wide // width
    deep = list_size // 8
    place = lax.broadcasted_iota(jnp.int32, (list_size, list_size), 1)
    moved = lax.broadcasted_iota(jnp.int32, (list_size, list_size), 0) == (
        lax.rem(place, 8) * deep + place // 8
    )
    placed_lists = dot_exact(lists[...].astype(f32), jnp.where(moved, 1.0, 0.0))
    placed_lists = jnp.floor(placed_lists + 0.5)
    whole_lists = placed_lists.astype(jnp.int32)
    slot_row = lax.broadcasted_iota(jnp.int32, (cap, list_size), 0)
    for k in range(n_gs):
        here = slot_row + flip(gs, k) * cap
        for t in range(tiles):
            slot_mask[k, :, t * list_size : (t + 1) * list_size] = jnp.where(
                here == whole_lists[t : t + 1, :], 1.0, 0.0
            ).astype(bf16)
    lists_t = jnp.transpose(placed_lists)
    slot_lane = lax.broadcasted_iota(jnp.int32, (list_size, cap), 1)
    for t in range(tiles):
        listed = jnp.broadcast_to(lists_t[:, t : t + 1], (list_size, cap))
        for k in range(n_gs):
            here = (slot_lane + flip(gs, k) * cap).astype(f32)
            slot_mask_t[k, t * list_size : (t + 1) * list_size, :] = jnp.where(
                here == listed, 1.0, 0.0
            ).astype(bf16)

    lane = lax.broadcasted_iota(jnp.int32, (tiles, wide), 1)
    in_tile = lax.rem(lane, width) // TILE == lax.broadcasted_iota(jnp.int32, (tiles, wide), 0)
    off_q = (lax.rem(lane, TILE) - TILE // 2).astype(f32)
    half_r = (lane // width).astype(f32)
    for i in range(n_chunk):
        off_r = half_r + float(i * per - TILE // 2)
        out = [jnp.ones_like(off_q), off_q, off_r, off_q * off_q, off_q * off_r, off_r * off_r]
        base = jnp.concatenate([jnp.where(in_tile, x, 0.0) for x in out], axis=0)
        bases[i] = base.astype(bf16)
        bases_t[i * wide : (i + 1) * wide, :] = jnp.transpose(base).astype(bf16)
    shape = (9 * tiles, 3 * width)
    row_of, lane_of = [lax.broadcasted_iota(jnp.int32, shape, k) for k in range(2)]
    at_tile = lax.rem(row_of, tiles) == lax.rem(lane_of, width) // TILE
    at_channel = lax.rem(row_of // tiles, 3) == lane_of // width
    widen = jnp.where(jnp.logical_and(at_tile, at_channel), 1.0, 0.0).astype(bf16)
    p_means, p_quats, p_scales, p_opacity, _ = params(par, opacity)
    spread, pull_spread = jax.vjp(spread_of, p_quats, p_scales)
    inv_depth = 1.0 / p_means[2]
    jac_diag = focal_length * inv_depth

    def keep(h, j, of):
        at = cams[of]
        keep_view(
            kept.at[h, j], par, spread, p_means, inv_depth, jac_diag, at[:, 0:1], at[:, 1:2]
        )

    keep(0, group, view)
    for t in range(tiles):
        tile_buf[t] = jnp.zeros((ROWS_MSG, list_size), f32)

    def gather(k, s):
        got = fold(dot(stack(pad_rows(msg_in[s]), 3), slot_mask[k]), 3)
        for t in range(tiles):
            tile_buf[t] += got[:, t * list_size : (t + 1) * list_size]

    gather(0, gs)
    for k in near:
        s = flip(gs, k)
        first_copy(gs, s).wait_recv()
        gather(k, s)

    diagonal = lax.broadcasted_iota(jnp.int32, (tiles, tiles), 0) == lax.broadcasted_iota(
        jnp.int32, (tiles, tiles), 1
    )
    used = jnp.sum(jnp.where(diagonal, lens[...].astype(f32), 0.0), axis=1, keepdims=True)
    entry = lax.broadcasted_iota(jnp.int32, (tiles, list_size), 1)
    entry = lax.rem(entry, 8) * deep + entry // 8
    live = entry.astype(f32) < used
    mid_q = (lax.broadcasted_iota(jnp.int32, (tiles, list_size), 0) * TILE + TILE // 2).astype(f32)
    mid_r = (gs * TILE + TILE // 2).astype(f32)
    off_u = tile_buf[:, 0, :] - mid_q
    off_w = tile_buf[:, 1, :] - mid_r
    k0 = tile_buf[:, 2, :]
    k1 = tile_buf[:, 3, :]
    k2 = tile_buf[:, 4, :]
    lin_u = k0 * off_u + k1 * off_w
    lin_w = k2 * off_w + k1 * off_u
    terms = [
        jnp.where(live, tile_buf[:, 5, :] - 0.5 * (off_u * lin_u + off_w * lin_w), -10000.0),
        jnp.where(live, lin_u, 0.0),
        jnp.where(live, lin_w, 0.0),
        jnp.where(live, -0.5 * k0, 0.0),
        jnp.where(live, -k1, 0.0),
        jnp.where(live, -0.5 * k2, 0.0),
    ]
    term_t = jnp.transpose(jnp.concatenate(pieces(jnp.concatenate(terms, axis=0), 3), axis=0))
    term_t = term_t.astype(bf16)
    colour = jnp.concatenate([tile_buf[:, 6 + c, :] for c in range(3)], axis=0)
    col_t = jnp.transpose(jnp.concatenate(pieces(colour, 3), axis=0)).astype(bf16)
    shade_buf[...] = dot(col_t, widen)

    for i in range(n_chunk):
        base = bases[i]
        ratio_buf[i] = jnp.exp(dot(term_t, jnp.concatenate([base, base, base], axis=0)))
    for i in range(n_chunk):
        for half in range(per):
            lanes = slice(half * width, (half + 1) * width)
            alpha = octets(ratio_buf[i, :, lanes])
            before = products_before([1.0 - x for x in alpha])
            weight = [x * y for x, y in zip(alpha, before)]
            weight_buf[i, :, lanes] = jnp.concatenate(weight, axis=0)
            row = i * per + half
            for c in range(3):
                shade = octets(shade_buf[:, c * width : (c + 1) * width])
                total = weight[0] * shade[0]
                for x, y in zip(weight[1:], shade[1:]):
                    total = total + x * y
                pic[c, row : row + 1, :] = jnp.sum(total, axis=0, keepdims=True)

    exchange(pic, halo, send_halo, recv_halo, True)
    pic_out[0] = pic[...]
    exchange(targets.at[0], t_halo, send_tgt, recv_tgt, False)
    tall = 2 * TILE
    across = band_split(width, list(range(width)), 0, 0)
    tgts = [
        jnp.concatenate([t_halo[0, c], targets[0, c], t_halo[1, c]], axis=0) for c in range(3)
    ]
    planes = []
    for c in range(3):
        planes += [tgts[c], tgts[c] * tgts[c]]
    rows_all = list(range(3 * TILE))
    band_all = band_split(tall, rows_all, TILE // 2, 1)
    down = dot(band_all, stack_mixed(jnp.concatenate(planes, axis=1), 0))
    blur_tgt = dot(stack_mixed(side_by_side(down, 6), 1), across)
    own = []
    for c in range(3):
        img = pic[c]
        own += [img, img * img, img * targets[0, c]]
    band_own = band_split(tall, rows_all[TILE : 2 * TILE], TILE // 2, 1)
    down_own = dot(band_own, stack_mixed(jnp.concatenate(own, axis=1), 0))
    band_far = band_split(tall, rows_all[:TILE] + rows_all[2 * TILE :], TILE // 2, 1)
    band_back = band_split(TILE, list(range(tall)), TILE // 2, 1)
    directs = []
    for c in range(3):
        res = pic[c] - targets[0, c]
        directs.append(
            (1.0 - ssim_weight) / (TILE * TILE) * res / jnp.sqrt(res * res + charb_eps)
        )
    for i in range(n_chunk):
        split_buf[i] = stack(jnp.transpose(weight_buf[i]), 2, 1)
        for half in range(per):
            lanes = slice(half * width, (half + 1) * width)
            alpha = ratio_buf[i, :, lanes]
            ratio = alpha / (1.0 - alpha)
            weight = weight_buf[i, :, lanes]
            for c in range(3):
                share = weight * shade_buf[:, c * width : (c + 1) * width]
                after = jnp.concatenate(sums_after(octets(share)), axis=0)
                power_buf[c, i, :, lanes] = share - ratio * after
    exchange(pic, halo, send_halo, recv_halo, False)

    beyond = []
    for c in range(3):
        img = jnp.concatenate([halo[0, c], halo[1, c]], axis=0)
        tgt = jnp.concatenate([t_halo[0, c], t_halo[1, c]], axis=0)
        beyond += [img, img * img, img * tgt]
    down = down_own + dot(band_far, stack_mixed(jnp.concatenate(beyond, axis=1), 0))
    blurred = dot(stack_mixed(side_by_side(down, 9), 1), across)
    at_row = lax.broadcasted_iota(jnp.int32, (tall, width), 0) + gs * TILE - TILE // 2
    inside = jnp.logical_and(at_row >= 0, at_row < n_gs * TILE)
    scale = -ssim_weight / (TILE * TILE)
    cots = []
    for c in range(3):
        mean_x, raw_xx, raw_xy = [
            blurred[(3 * c + i) * tall : (3 * c + i + 1) * tall] for i in range(3)
        ]
        mean_y, raw_yy = [
            blur_tgt[(2 * c + i) * tall : (2 * c + i + 1) * tall] for i in range(2)
        ]
        top_a = 2.0 * mean_x * mean_y + ssim_one
        top_b = 2.0 * (raw_xy - mean_x * mean_y) + ssim_two
        low_c = mean_x * mean_x + mean_y * mean_y + ssim_one
        low_d = (raw_xx - mean_x * mean_x) + (raw_yy - mean_y * mean_y) + ssim_two
        inv_cd = 1.0 / (low_c * low_d)
        inv_dd = inv_cd * low_c
        ssim = top_a * top_b * inv_cd
        d_mean = 2.0 * mean_y * (top_b - top_a) * inv_cd - 2.0 * mean_x * ssim * (
            inv_cd * low_d - inv_dd
        )
        d_xx = -ssim * inv_dd
        d_xy = 2.0 * top_a * inv_cd
        cots += [jnp.where(inside, scale * part, 0.0) for part in (d_mean, d_xx, d_xy)]
    spread_rows = dot(band_back, stack_mixed(jnp.concatenate(cots, axis=1), 0))
    spread_rows = dot(stack_mixed(side_by_side(spread_rows, 9), 1), across)
    grad_rows = []
    for c in range(3):
        s_mean, s_xx, s_xy = [spread_rows[(3 * c + i) * TILE : (3 * c + i + 1) * TILE] for i in range(3)]
        grad_rows.append(directs[c] + s_mean + 2.0 * pic[c] * s_xx + targets[0, c] * s_xy)

    d_terms = jnp.zeros((2 * list_size, 6 * tiles), f32)
    d_colour = jnp.zeros((6 * tiles, 2 * list_size), f32)
    for i in range(n_chunk):
        lines = [
            jnp.concatenate(
                [grad_rows[c][i * per + half : i * per + half + 1] for half in range(per)], axis=1
            )
            for c in range(3)
        ]
        shades = stack(jnp.concatenate([jnp.where(in_tile, x, 0.0) for x in lines], axis=0), 2)
        d_power = lines[0] * power_buf[0, i] + lines[1] * power_buf[1, i] + lines[2] * power_buf[2, i]
        d_terms = d_terms + dot(stack(d_power, 2), bases_t[i * wide : (i + 1) * wide, :])
        d_colour = d_colour + dot(shades, split_buf[i])
    d_terms = jnp.transpose(fold(d_terms, 2))
    d_colour = fold(d_colour[:, :list_size] + d_colour[:, list_size:], 2)

    d0, d1, d2, d3, d4, d5 = [d_terms[k * tiles : (k + 1) * tiles] for k in range(6)]
    e1 = d1 - off_u * d0
    e2 = d2 - off_w * d0
    cot[...] = jnp.zeros_like(cot)
    cot[:, 0, :] = k0 * e1 + k1 * e2
    cot[:, 1, :] = k2 * e2 + k1 * e1
    cot[:, 2, :] = -0.5 * d3 + off_u * (d1 - 0.5 * off_u * d0)
    cot[:, 3, :] = off_w * e1 + off_u * d2 - d4
    cot[:, 4, :] = -0.5 * d5 + off_w * (d2 - 0.5 * off_w * d0)
    cot[:, 5, :] = d0
    for c in range(3):
        cot[:, 6 + c, :] = d_colour[c * tiles : (c + 1) * tiles]
    cots = jnp.concatenate([stack(cot[t], 2) for t in range(tiles)], axis=1)

    def out_copy(j, d):
        return pltpu.make_async_remote_copy(
            src_ref=back_out.at[d],
            dst_ref=back_in.at[group, gs],
            send_sem=send_two.at[j, d],
            recv_sem=recv_two.at[group, gs],
            device_id=(d, cousin(j)),
            device_id_type=MESH,
        )

    def in_copy(j, s):
        of = lax.div(cousin(j), 2)
        return pltpu.make_async_remote_copy(
            src_ref=back_out.at[s],
            dst_ref=back_in.at[of, s],
            send_sem=send_two.at[j, s],
            recv_sem=recv_two.at[of, s],
            device_id=(s, cousin(j)),
            device_id_type=MESH,
        )

    for k in list(far) + [0]:
        d = flip(gs, k)
        back_out[d] = fold(dot(cots, slot_mask_t[k]), 2)[0:9]
        for j in range(groups):
            if k or j:
                out_copy(j, d).start()
    back_in[group, gs] = back_out[gs]

    send_t = jnp.transpose(send[0].astype(f32))
    shard_lane = lax.broadcasted_iota(jnp.int32, (cap, shard), 1).astype(f32)
    for s in range(n_gs):
        row_mask[s] = jnp.where(shard_lane == send_t[:, s : s + 1], 1.0, 0.0).astype(bf16)
    for k in range(1, n_view):
        cam_copy(view, lax.rem(view + n_view - k, n_view)).wait_recv()
    for j in range(1, groups):
        keep(0, lax.div(cousin(j), 2), cousin(j))
    for j in range(groups):
        keep(1, j, 2 * j + 1 - core)


    def put_back(s, first):
        both = [stack(pad_rows(back_in[j, s]), 2) for j in range(groups)]
        got = dot(jnp.concatenate(both, axis=0), row_mask[s])
        placed[...] = got if first else placed[...] + got

    for k in range(n_gs):
        s = flip(gs, k)
        for j in range(groups):
            if k or j:
                in_copy(j, s).wait_recv()
        put_back(s, k == 0)
    for j in range(groups):
        mine = fold(placed[2 * ROWS_MSG * j : 2 * ROWS_MSG * (j + 1)], 2)
        for c in range(chunks):
            cot_views[core, j, :, c, :] = mine[0:9, c * LANES : (c + 1) * LANES]

    def third_copy(of):
        return pltpu.make_async_remote_copy(
            src_ref=cot_views.at[of],
            dst_ref=cot_views.at[of],
            send_sem=send_three.at[0],
            recv_sem=recv_three.at[0],
            device_id=(gs, flip(view, 1)),
            device_id_type=MESH,
        )

    third_copy(core).start()

    def pull_half(h):
        side = core if h == 0 else 1 - core
        total = None
        tints = []
        for j in range(groups):
            cots = [cot_views[side, j, i] for i in range(9)]
            got, shades = pull_view(kept.at[h, j], cots, inv_depth, jac_diag, spread)
            total = got if total is None else [a + b for a, b in zip(total, got)]
            tints.append(shades)
        for i in range(15):
            if h == 0:
                g_sum[i] = total[i]
            else:
                total[i] = total[i] + g_sum[i]
        for k in range(SH):
            for c in range(3):
                part = None
                for j in range(groups):
                    term = tints[j][c] * (sh_c0 if k == 0 else kept[h, j, 26 + k])
                    part = term if part is None else part + term
                if h == 1:
                    part = part + g_par[:, c * SH + k, :]
                g_par[:, c * SH + k, :] = part
        return total

    pull_half(0)
    third_copy(1 - core).wait_recv()
    total = pull_half(1)
    d_top, d_low, d_base = total[0:3], total[3:6], total[6:9]
    d_x, d_y, d_z, d_diag, d_inv, d_log = total[9:15]
    for j in range(3):
        d_diag = d_diag + d_top[j] * spread[0][j] + d_low[j] * spread[1][j]
    d_inv = d_inv + focal_length * d_diag
    d_z = d_z - inv_depth * inv_depth * d_inv
    d_quats, d_scales = pull_spread(
        [[jac_diag * x for x in d_top], [jac_diag * x for x in d_low], list(d_base)]
    )
    decay = jnp.exp(-p_opacity)
    opacity_out[...] = d_log * decay / (1.0 + decay)
    for i, x in enumerate([d_x, d_y, d_z]):
        g_par[:, 48 + i, :] = x
    for i in range(4):
        g_par[:, 56 + i, :] = d_quats[i]
    for i in range(3):
        g_par[:, 64 + i, :] = d_scales[i]
    for c in range(chunks):
        cols = slice(c * LANES, (c + 1) * LANES)
        sh_out[:, cols] = g_par[c, 0:48, :]
        means_out[:, cols] = g_par[c, 48:51, :]
        quats_out[:, cols] = g_par[c, 56:60, :]
        scales_out[:, cols] = g_par[c, 64:67, :]

    for k in near:
        first_copy(flip(gs, k), gs).wait_send()
    for k in range(1, n_view):
        cam_copy(lax.rem(view + k, n_view), view).wait_send()
    for k in range(n_gs):
        for j in range(groups):
            if k or j:
                out_copy(j, flip(gs, k)).wait_send()
    third_copy(core).wait_send()


def store_kernel(*refs):
    count = len(refs) // 2
    sources, places, sems = refs[:count], refs[count : 2 * count], refs[-1]
    stores = [
        pltpu.make_async_copy(src, dst, sems.at[k])
        for k, (src, dst) in enumerate(zip(sources, places))
    ]
    for store in stores:
        store.start()
    for store in stores:
        store.wait()


def far_kernel(
    n_gs,
    n_view,
    means_in,
    quats_in,
    scales_in,
    opacity_in,
    sh_in,
    camera_in,
    targets_in,
    send_in,
    lists_in,
    lens_in,
    pic_out,
    views_out,
    par,
    opacity,
    send,
    means,
    quats,
    scales,
    sh,
    camera,
    targets,
    lists,
    lens,
    row_buf,
    msg_out,
    msg_in,
    tile_buf,
    ratio_buf,
    weight_buf,
    pic,
    halo,
    t_halo,
    cot,
    back_out,
    back_in,
    placed,
    load_sems,
    send_one,
    recv_one,
    send_halo,
    recv_halo,
    send_tgt,
    recv_tgt,
    send_two,
    recv_two,
    send_three,
    recv_three,
):
    loads = [
        pltpu.make_async_copy(src, dst, load_sems.at[k])
        for k, (src, dst) in enumerate(
            [
                (sh_in, sh),
                (means_in, means),
                (quats_in, quats),
                (scales_in, scales),
                (opacity_in, opacity),
                (camera_in, camera),
                (send_in, send),
                (targets_in, targets),
                (lists_in.at[0, 0], lists),
                (lens_in.at[0], lens),
            ]
        )
    ]
    for load in loads:
        load.start()
    gs = lax.axis_index("gs")
    view = lax.axis_index("view")
    chunks = means.shape[1] // LANES
    cap = send.shape[2]
    shard = means.shape[1]
    tiles = lists.shape[0]
    list_size = lists.shape[1]
    has_up = gs > 0
    has_down = gs < n_gs - 1

    barrier = pltpu.get_barrier_semaphore()

    def greet(strip, cam):
        pl.semaphore_signal(barrier, inc=1, device_id=(strip, cam), device_id_type=MESH)

    loop(1, n_gs, lambda k: greet(lax.rem(gs + k, n_gs), view))
    loop(1, n_view, lambda k: greet(gs, lax.rem(view + k, n_view)))

    for load in loads:
        load.wait()

    for c in range(chunks):
        cols = slice(c * LANES, (c + 1) * LANES)
        par[c, 0:48, :] = sh[:, cols]
        par[c, 48:51, :] = means[:, cols]
        par[c, 56:60, :] = quats[:, cols]
        par[c, 64:67, :] = scales[:, cols]

    centre_x = 0.5 * tiles * TILE
    centre_y = 0.5 * n_gs * TILE
    cam_x = camera[0:1, 0:1]
    cam_y = camera[0:1, 1:2]
    rows = project(*params(par, opacity), [(cam_x, cam_y)], centre_x, centre_y)[0]
    row_buf[...] = jnp.zeros_like(row_buf)
    for i in range(9):
        row_buf[:, i, :] = rows[i]
    table = stack(jnp.concatenate([row_buf[c] for c in range(chunks)], axis=1), 3)

    def fill(d):
        msg_out[d] = fold(dot(table, pick_of(send, d, shard)), 3)

    def first_copy(d, s):
        return pltpu.make_async_remote_copy(
            src_ref=msg_out.at[d],
            dst_ref=msg_in.at[s],
            send_sem=send_one.at[d],
            recv_sem=recv_one.at[s],
            device_id=(d, view),
            device_id_type=MESH,
        )

    pl.semaphore_wait(barrier, n_gs + n_view - 2)

    def send_first(k):
        d = lax.rem(gs + k, n_gs)
        fill(d)
        first_copy(d, gs).start()

    loop(1, n_gs, send_first)
    fill(gs)
    msg_in[gs] = msg_out[gs]

    def halo_copy(src, dst, sends, recvs, side):
        other = gs + 1 if side == 0 else gs - 1
        return pltpu.make_async_remote_copy(
            src_ref=src,
            dst_ref=dst.at[side],
            send_sem=sends.at[side],
            recv_sem=recvs.at[side],
            device_id=(other, view),
            device_id_type=MESH,
        )

    def exchange(src, dst, sends, recvs, start):
        def act(copy, recv):
            if start:
                if not recv:
                    copy.start()
            elif recv:
                copy.wait_recv()
            else:
                copy.wait_send()

        for recv in (False, True):
            if start and recv:
                continue

            @pl.when(has_down)
            def _():
                act(halo_copy(src, dst, sends, recvs, 1 if recv else 0), recv)

            @pl.when(has_up)
            def _():
                act(halo_copy(src, dst, sends, recvs, 0 if recv else 1), recv)

    exchange(targets.at[0], t_halo, send_tgt, recv_tgt, True)

    @pl.when(jnp.logical_not(has_up))
    def _():
        halo[0] = jnp.zeros_like(halo[0])
        t_halo[0] = jnp.zeros_like(t_halo[0])

    @pl.when(jnp.logical_not(has_down))
    def _():
        halo[1] = jnp.zeros_like(halo[1])
        t_halo[1] = jnp.zeros_like(t_halo[1])


    slot_row = lax.broadcasted_iota(jnp.int32, (cap, list_size), 0)

    def slot_pick(s, t):
        return jnp.where(slot_row + s * cap == lists[t : t + 1, :], 1.0, 0.0).astype(bf16)

    tile_buf[...] = jnp.zeros_like(tile_buf)

    def gather(s):
        got = stack(msg_in[s], 3)
        for t in range(tiles):
            tile_buf[t] += fold(dot(got, slot_pick(s, t)), 3)

    gather(gs)

    def gather_next(k):
        s = lax.rem(gs + n_gs - k, n_gs)
        first_copy(gs, s).wait_recv()
        gather(s)

    loop(1, n_gs, gather_next)

    diagonal = lax.broadcasted_iota(jnp.int32, (tiles, tiles), 0) == lax.broadcasted_iota(
        jnp.int32, (tiles, tiles), 1
    )
    used = jnp.sum(jnp.where(diagonal, lens[...].astype(f32), 0.0), axis=1, keepdims=True)
    entry = lax.broadcasted_iota(jnp.int32, (tiles, list_size), 1)
    live = entry.astype(f32) < used
    mid_q = (lax.broadcasted_iota(jnp.int32, (tiles, list_size), 0) * TILE + TILE // 2).astype(f32)
    mid_r = (gs * TILE + TILE // 2).astype(f32)
    off_u = tile_buf[:, 0, :] - mid_q
    off_w = tile_buf[:, 1, :] - mid_r
    k0 = tile_buf[:, 2, :]
    k1 = tile_buf[:, 3, :]
    k2 = tile_buf[:, 4, :]
    lin_u = k0 * off_u + k1 * off_w
    lin_w = k2 * off_w + k1 * off_u
    terms = [
        jnp.where(live, tile_buf[:, 5, :] - 0.5 * (off_u * lin_u + off_w * lin_w), -10000.0),
        jnp.where(live, lin_u, 0.0),
        jnp.where(live, lin_w, 0.0),
        jnp.where(live, -0.5 * k0, 0.0),
        jnp.where(live, -k1, 0.0),
        jnp.where(live, -0.5 * k2, 0.0),
    ]
    term_t = jnp.transpose(jnp.concatenate(pieces(jnp.concatenate(terms, axis=0), 3), axis=0))
    term_t = term_t.astype(bf16)
    colour = jnp.concatenate([tile_buf[:, 6 + c, :] for c in range(3)], axis=0)
    col_hi, col_lo = pieces(colour, 2)
    col_two = jnp.concatenate([col_hi, col_lo], axis=0)
    col_wide = jnp.concatenate([col_two, col_two], axis=1).astype(bf16)
    col_t = jnp.transpose(jnp.concatenate([col_hi, col_lo, col_hi], axis=0)).astype(bf16)

    n_chunk, _, wide = weight_buf.shape
    width = tiles * TILE
    lane = lax.broadcasted_iota(jnp.int32, (tiles, wide), 1)
    in_tile = lax.rem(lane, width) // TILE == lax.broadcasted_iota(jnp.int32, (tiles, wide), 0)

    off_q = (lax.rem(lane, TILE) - TILE // 2).astype(f32)
    half_r = (lane // width).astype(f32)

    def basis(i):
        off_r = half_r + float(i * (wide // width) - TILE // 2)
        out = [jnp.ones_like(off_q), off_q, off_r, off_q * off_q, off_q * off_r, off_r * off_r]
        return jnp.concatenate([jnp.where(in_tile, x, 0.0) for x in out], axis=0).astype(bf16)

    shape = (list_size, 2 * list_size)
    list_row = lax.broadcasted_iota(jnp.int32, shape, 0)
    list_col = lax.rem(lax.broadcasted_iota(jnp.int32, shape, 1), list_size)
    prefix = jnp.where(list_col < list_row, 1.0, 0.0).astype(bf16)
    suffix = jnp.where(list_col > list_row, 1.0, 0.0).astype(bf16)

    for i in range(n_chunk):
        base = basis(i)
        alpha = jnp.exp(dot(term_t, jnp.concatenate([base, base, base], axis=0)))
        keep = 1.0 - alpha
        weight = alpha * jnp.exp(dot(prefix, stack(jnp.log(keep), 2)))
        ratio_buf[i] = alpha / keep
        weight_buf[i] = weight
        drawn = fold(dot(col_wide, stack(weight, 2)), 2)
        for c in range(3):
            mine = jnp.where(in_tile, drawn[c * tiles : (c + 1) * tiles], 0.0)
            line = jnp.sum(mine, axis=0, keepdims=True)
            for half in range(wide // width):
                row = i * (wide // width) + half
                pic[c, row : row + 1, :] = line[:, half * width : (half + 1) * width]

    exchange(pic, halo, send_halo, recv_halo, True)
    pic_out[0] = pic[...]
    exchange(targets.at[0], t_halo, send_tgt, recv_tgt, False)
    exchange(pic, halo, send_halo, recv_halo, False)

    tall = 2 * TILE
    across = band(width, width, 0)
    stacked = []
    images = []
    for c in range(3):
        img = jnp.concatenate([halo[0, c], pic[c], halo[1, c]], axis=0)
        tgt = jnp.concatenate([t_halo[0, c], targets[0, c], t_halo[1, c]], axis=0)
        images.append((img, tgt))
        stacked += [img, tgt, img * img, tgt * tgt, img * tgt]
    down = dot_exact(band(tall, 3 * TILE, TILE // 2), jnp.concatenate(stacked, axis=1))
    down = jnp.concatenate([down[:, i * width : (i + 1) * width] for i in range(15)], axis=0)
    blurred = dot_exact(down, across)
    at_row = lax.broadcasted_iota(jnp.int32, (tall, width), 0) + gs * TILE - TILE // 2
    inside = jnp.logical_and(at_row >= 0, at_row < n_gs * TILE)
    scale = -ssim_weight / (TILE * TILE)
    cots = []
    for c in range(3):
        mean_x, mean_y, raw_xx, raw_yy, raw_xy = [
            blurred[(5 * c + i) * tall : (5 * c + i + 1) * tall] for i in range(5)
        ]
        top_a = 2.0 * mean_x * mean_y + ssim_one
        top_b = 2.0 * (raw_xy - mean_x * mean_y) + ssim_two
        low_c = mean_x * mean_x + mean_y * mean_y + ssim_one
        low_d = (raw_xx - mean_x * mean_x) + (raw_yy - mean_y * mean_y) + ssim_two
        inv_cd = 1.0 / (low_c * low_d)
        inv_dd = inv_cd * low_c
        ssim = top_a * top_b * inv_cd
        d_mean = 2.0 * mean_y * (top_b - top_a) * inv_cd - 2.0 * mean_x * ssim * (
            inv_cd * low_d - inv_dd
        )
        d_xx = -ssim * inv_dd
        d_xy = 2.0 * top_a * inv_cd
        cots += [jnp.where(inside, scale * part, 0.0) for part in (d_mean, d_xx, d_xy)]
    spread = dot_exact(band(TILE, tall, TILE // 2), jnp.concatenate(cots, axis=1))
    spread = jnp.concatenate([spread[:, i * width : (i + 1) * width] for i in range(9)], axis=0)
    spread = dot_exact(spread, across)
    grad_rows = []
    for c in range(3):
        img = pic[c]
        tgt = targets[0, c]
        s_mean, s_xx, s_xy = [spread[(3 * c + i) * TILE : (3 * c + i + 1) * TILE] for i in range(3)]
        res = img - tgt
        direct = (1.0 - ssim_weight) / (TILE * TILE) * res / jnp.sqrt(res * res + charb_eps)
        grad_rows.append(direct + s_mean + 2.0 * img * s_xx + tgt * s_xy)

    d_terms = jnp.zeros((6 * tiles, list_size), f32)
    d_colour = jnp.zeros((3 * tiles, list_size), f32)
    for i in range(n_chunk):
        per = wide // width
        parts = []
        for c in range(3):
            line = jnp.concatenate(
                [grad_rows[c][i * per + half : i * per + half + 1] for half in range(per)], axis=1
            )
            parts.append(jnp.where(in_tile, line, 0.0))
        hi, lo = pieces(jnp.concatenate(parts, axis=0), 2)
        shade = dot(col_t, jnp.concatenate([hi, hi, lo], axis=0).astype(bf16))
        weight = weight_buf[i]
        share = weight * shade
        d_power = share - ratio_buf[i] * dot(suffix, stack(share, 2))
        both = dot_t(basis(i), stack(d_power, 2))
        d_terms = d_terms + both[:, :list_size] + both[:, list_size:]
        both = fold(dot_t(jnp.concatenate([hi, lo], axis=0).astype(bf16), stack(weight, 2)), 2)
        d_colour = d_colour + both[:, :list_size] + both[:, list_size:]

    d0, d1, d2, d3, d4, d5 = [d_terms[k * tiles : (k + 1) * tiles] for k in range(6)]
    e1 = d1 - off_u * d0
    e2 = d2 - off_w * d0
    cot[...] = jnp.zeros_like(cot)
    cot[:, 0, :] = k0 * e1 + k1 * e2
    cot[:, 1, :] = k2 * e2 + k1 * e1
    cot[:, 2, :] = -0.5 * d3 + off_u * (d1 - 0.5 * off_u * d0)
    cot[:, 3, :] = off_w * e1 + off_u * d2 - d4
    cot[:, 4, :] = -0.5 * d5 + off_w * (d2 - 0.5 * off_w * d0)
    cot[:, 5, :] = d0
    for c in range(3):
        cot[:, 6 + c, :] = d_colour[c * tiles : (c + 1) * tiles]
    cot_pieces = [stack(cot[t], 3) for t in range(tiles)]

    def scatter(s):
        total = jnp.zeros((3 * ROWS_MSG, cap), f32)
        for t in range(tiles):
            total = total + dot_t(cot_pieces[t], slot_pick(s, t))
        back_out[s] = fold(total, 3)

    def second_copy(d, s):
        return pltpu.make_async_remote_copy(
            src_ref=back_out.at[d],
            dst_ref=back_in.at[s],
            send_sem=send_two.at[d],
            recv_sem=recv_two.at[s],
            device_id=(d, view),
            device_id_type=MESH,
        )

    def send_second(k):
        d = lax.rem(gs + k, n_gs)
        scatter(d)
        second_copy(d, gs).start()

    loop(1, n_gs, send_second)
    scatter(gs)
    back_in[gs] = back_out[gs]
    placed[...] = jnp.zeros_like(placed)

    def put_back(s):
        placed[...] += dot_t(stack(back_in[s], 3), pick_of(send, s, shard))

    put_back(gs)

    def put_next(k):
        s = lax.rem(gs + n_gs - k, n_gs)
        second_copy(gs, s).wait_recv()
        put_back(s)

    loop(1, n_gs, put_next)
    whole = fold(placed[...], 3)
    for c in range(chunks):
        views_out[view, 0:9, c, :] = whole[0:9, c * LANES : (c + 1) * LANES]
    first_row = lax.broadcasted_iota(jnp.int32, (chunks, LANES), 0) == 0
    views_out[view, 9] = jnp.where(first_row, cam_x, cam_y)

    def third_copy(to, of):
        return pltpu.make_async_remote_copy(
            src_ref=views_out.at[of],
            dst_ref=views_out.at[of],
            send_sem=send_three.at[to],
            recv_sem=recv_three.at[of],
            device_id=(gs, to),
            device_id_type=MESH,
        )

    def send_third(k):
        third_copy(lax.rem(view + k, n_view), view).start()

    def wait_third(k):
        third_copy(view, lax.rem(view + n_view - k, n_view)).wait_recv()

    loop(1, n_view, send_third)
    loop(1, n_view, wait_third)

    def done_first(k):
        first_copy(lax.rem(gs + k, n_gs), gs).wait_send()
        second_copy(lax.rem(gs + k, n_gs), gs).wait_send()

    def done_third(k):
        third_copy(lax.rem(view + k, n_view), view).wait_send()

    loop(1, n_gs, done_first)
    loop(1, n_view, done_third)


def pull_kernel(
    n_view,
    pic,
    views,
    par,
    opacity,
    pic_out,
    means_out,
    quats_out,
    scales_out,
    opacity_out,
    sh_out,
    g_par,
    g_means,
    g_quats,
    g_scales,
    g_opacity,
    g_sh,
    store_sems,
):
    chunks = par.shape[0]
    pic_copy = pltpu.make_async_copy(pic, pic_out, store_sems.at[0])
    pic_copy.start()
    cams = [(views[v, 9, 0:1, 0:1], views[v, 9, 1:2, 0:1]) for v in range(n_view)]
    _, pull = jax.vjp(lambda *args: project(*args, cams, 0.0, 0.0), *params(par, opacity))
    grads = pull([[views[v, i] for i in range(9)] for v in range(n_view)])
    for i in range(3):
        g_par[:, 48 + i, :] = grads[0][i]
        g_par[:, 64 + i, :] = grads[2][i]
    for i in range(4):
        g_par[:, 56 + i, :] = grads[1][i]
    for i in range(48):
        g_par[:, i, :] = grads[4][i]
    g_opacity[...] = grads[3]
    for c in range(chunks):
        cols = slice(c * LANES, (c + 1) * LANES)
        g_sh[:, cols] = g_par[c, 0:48, :]
        g_means[:, cols] = g_par[c, 48:51, :]
        g_quats[:, cols] = g_par[c, 56:60, :]
        g_scales[:, cols] = g_par[c, 64:67, :]
    stores = [
        pltpu.make_async_copy(src, dst, store_sems.at[k + 1])
        for k, (src, dst) in enumerate(
            [
                (g_sh, sh_out),
                (g_means, means_out),
                (g_quats, quats_out),
                (g_scales, scales_out),
                (g_opacity, opacity_out),
            ]
        )
    ]
    for store in stores:
        store.start()
    pic_copy.wait()
    for store in stores:
        store.wait()


def far_shards(
    means, quats, log_scales, opacity, sh_coeffs, cameras, targets, send_rows, tile_lists, list_lengths
):
    n_gs = lax.axis_size("gs")
    n_view = lax.axis_size("view")
    shard = means.shape[1]
    chunks = shard // LANES
    cap = send_rows.shape[2]
    tiles, list_size = tile_lists.shape[2:]
    width = tiles * TILE
    n_chunk = TILE // 2
    wide = 2 * width
    opacity = opacity.reshape(chunks, LANES)
    args = (
        means,
        quats,
        log_scales,
        opacity,
        sh_coeffs,
        cameras,
        targets,
        send_rows,
        tile_lists,
        list_lengths,
    )
    shape = jax.ShapeDtypeStruct
    dma = pltpu.SemaphoreType.DMA
    vmem = pl.BlockSpec(memory_space=VMEM)
    hbm = pl.BlockSpec(memory_space=pltpu.HBM)
    mids = pl.pallas_call(
        lambda *refs: far_kernel(n_gs, n_view, *refs),
        out_shape=(
            shape(targets.shape, f32),
            shape((n_view, 10, chunks, LANES), f32),
            shape((chunks, 72, LANES), f32),
            shape((chunks, LANES), f32),
        ),
        in_specs=[hbm] * len(args),
        out_specs=(vmem,) * 4,
        scratch_shapes=[
            VMEM(send_rows.shape, jnp.int32),
            VMEM(means.shape, f32),
            VMEM(quats.shape, f32),
            VMEM(log_scales.shape, f32),
            VMEM(sh_coeffs.shape, f32),
            VMEM(cameras.shape, f32),
            VMEM(targets.shape, f32),
            VMEM((tiles, list_size), jnp.int32),
            VMEM((1, tiles), jnp.int32),
            VMEM((chunks, ROWS_MSG, LANES), f32),
            VMEM((n_gs, ROWS_MSG, cap), f32),
            VMEM((n_gs, ROWS_MSG, cap), f32),
            VMEM((tiles, ROWS_MSG, list_size), f32),
            VMEM((n_chunk, list_size, wide), f32),
            VMEM((n_chunk, list_size, wide), f32),
            VMEM((3, TILE, width), f32),
            VMEM((2, 3, TILE, width), f32),
            VMEM((2, 3, TILE, width), f32),
            VMEM((tiles, ROWS_MSG, list_size), f32),
            VMEM((n_gs, ROWS_MSG, cap), f32),
            VMEM((n_gs, ROWS_MSG, cap), f32),
            VMEM((3 * ROWS_MSG, shard), f32),
            dma((10,)),
            dma((n_gs,)),
            dma((n_gs,)),
            dma((2,)),
            dma((2,)),
            dma((2,)),
            dma((2,)),
            dma((n_gs,)),
            dma((n_gs,)),
            dma((n_view,)),
            dma((n_view,)),
        ],
        compiler_params=pltpu.CompilerParams(
            collective_id=0, has_side_effects=True, vmem_limit_bytes=48 * 1024 * 1024
        ),
    )(*[pltpu.with_memory_space_constraint(x, pltpu.HBM) for x in args])
    outs = pl.pallas_call(
        lambda *refs: pull_kernel(n_view, *refs),
        out_shape=(
            shape(targets.shape, f32),
            shape(means.shape, f32),
            shape(quats.shape, f32),
            shape(log_scales.shape, f32),
            shape((chunks, LANES), f32),
            shape(sh_coeffs.shape, f32),
        ),
        in_specs=[vmem] * 4,
        out_specs=(hbm,) * 6,
        scratch_shapes=[
            VMEM((chunks, 72, LANES), f32),
            VMEM(means.shape, f32),
            VMEM(quats.shape, f32),
            VMEM(log_scales.shape, f32),
            VMEM((chunks, LANES), f32),
            VMEM(sh_coeffs.shape, f32),
            dma((6,)),
        ],
        compiler_params=pltpu.CompilerParams(vmem_limit_bytes=48 * 1024 * 1024),
    )(*mids)
    return (*outs[:4], outs[4].reshape(shard), outs[5])


def shards(
    means, quats, log_scales, opacity, sh_coeffs, cameras, targets, send_rows, tile_lists, list_lengths
):
    n_gs = lax.axis_size("gs")
    n_view = lax.axis_size("view")
    shard = means.shape[1]
    cap = send_rows.shape[2]
    args = (
        means,
        quats,
        log_scales,
        opacity,
        sh_coeffs,
        cameras,
        targets,
        send_rows,
        tile_lists,
        list_lengths,
    )
    if n_gs not in (2, 4, 8) or cap % LANES or n_view % 2:
        return far_shards(*args)
    chunks = shard // LANES
    tiles, list_size = tile_lists.shape[2:]
    width = tiles * TILE
    n_chunk = TILE // 2
    wide = 2 * width
    groups = n_view // 2
    args = args[:3] + (opacity.reshape(chunks, LANES),) + args[4:]
    shape = jax.ShapeDtypeStruct
    dma = pltpu.SemaphoreType.DMA
    vmem = pl.BlockSpec(memory_space=VMEM)
    hbm = pl.BlockSpec(memory_space=pltpu.HBM)
    out_shape = (
        shape(targets.shape, f32),
        shape(means.shape, f32),
        shape(quats.shape, f32),
        shape(log_scales.shape, f32),
        shape((chunks, LANES), f32),
        shape(sh_coeffs.shape, f32),
    )
    mids = pl.pallas_call(
        lambda *refs: near_kernel(n_gs, n_view, *refs),
        out_shape=out_shape,
        in_specs=[hbm] * len(args),
        out_specs=(vmem,) * 6,
        scratch_shapes=[
            VMEM((chunks, 72, LANES), f32),
            VMEM((chunks, LANES), f32),
            VMEM(send_rows.shape, jnp.int32),
            VMEM(means.shape, f32),
            VMEM(quats.shape, f32),
            VMEM(log_scales.shape, f32),
            VMEM(sh_coeffs.shape, f32),
            VMEM(cameras.shape, f32),
            VMEM(targets.shape, f32),
            VMEM((tiles, list_size), jnp.int32),
            VMEM((1, tiles), jnp.int32),
            VMEM((n_view, 1, LANES), f32),
            VMEM((chunks, ROWS_MSG, LANES), f32),
            VMEM((n_gs, 9, cap), f32),
            VMEM((n_gs, 9, cap), f32),
            VMEM((n_gs, cap, tiles * list_size), bf16),
            VMEM((n_gs, tiles * list_size, cap), bf16),
            VMEM((n_gs, cap, shard), bf16),
            VMEM((n_chunk, 6 * tiles, wide), bf16),
            VMEM((n_chunk * wide, 6 * tiles), bf16),
            VMEM((tiles, ROWS_MSG, list_size), f32),
            VMEM((n_chunk, list_size, wide), f32),
            VMEM((n_chunk, list_size, wide), f32),
            VMEM((list_size, 3 * width), f32),
            VMEM((n_chunk, wide, 2 * list_size), bf16),
            VMEM((3, n_chunk, list_size, wide), f32),
            VMEM((3, TILE, width), f32),
            VMEM((2, 3, TILE, width), f32),
            VMEM((2, 3, TILE, width), f32),
            VMEM((tiles, ROWS_MSG, list_size), f32),
            VMEM((n_gs, 9, cap), f32),
            VMEM((groups, n_gs, 9, cap), f32),
            VMEM((2 * ROWS_MSG * groups, shard), f32),
            VMEM((2, groups, N_KEPT, chunks, LANES), f32),
            VMEM((2, groups, 9, chunks, LANES), f32),
            VMEM((15, chunks, LANES), f32),
            VMEM((chunks, 72, LANES), f32),
            dma((10,)),
            dma((n_view,)),
            dma((n_view,)),
            dma((n_gs,)),
            dma((n_gs,)),
            dma((2,)),
            dma((2,)),
            dma((2,)),
            dma((2,)),
            dma((groups, n_gs)),
            dma((groups, n_gs)),
            dma((1,)),
            dma((1,)),
        ],
        compiler_params=pltpu.CompilerParams(
            collective_id=1, has_side_effects=True, vmem_limit_bytes=48 * 1024 * 1024
        ),
    )(*[pltpu.with_memory_space_constraint(x, pltpu.HBM) for x in args])
    outs = pl.pallas_call(
        store_kernel,
        out_shape=out_shape,
        in_specs=[vmem] * 6,
        out_specs=(hbm,) * 6,
        scratch_shapes=[dma((6,))],
        compiler_params=pltpu.CompilerParams(vmem_limit_bytes=48 * 1024 * 1024),
    )(*mids)
    return (*outs[:4], outs[4].reshape(shard), outs[5])


def solution(mesh):
    return jax.shard_map(
        shards,
        mesh=mesh,
        in_specs=(
            P(None, "gs"),
            P(None, "gs"),
            P(None, "gs"),
            P("gs"),
            P(None, "gs"),
            P("view", None),
            P("view", None, "gs", None),
            P("gs", None, None),
            P("view", "gs", None, None),
            P("view", "gs", None),
        ),
        out_specs=(
            P("view", None, "gs", None),
            P(None, "gs"),
            P(None, "gs"),
            P(None, "gs"),
            P("gs"),
            P(None, "gs"),
        ),
        check_vma=False,
    )
```

```python
import math

import jax
import jax.numpy as jnp
import ml_dtypes
import numpy as np
from jax import lax
from jax.experimental import pallas as pl
from jax.experimental.pallas import tpu as pltpu
from jax.sharding import PartitionSpec as P

TILE = 16
SH = 16
RADIUS = 5
LANES = 128
ROWS_MSG = 16
VMEM = pltpu.VMEM
MESH = pl.DeviceIdType.MESH

focal_length = 1000.0
cov_blur = 0.3
ssim_weight = 0.2
charb_eps = 0.0001
ssim_one = 0.0001
ssim_two = 0.0009
sh_c0 = 0.28209479177387814
sh_c1 = 0.4886025119029199
sh_c2 = [
    1.0925484305920792,
    -1.0925484305920792,
    0.31539156525252005,
    -1.0925484305920792,
    0.5462742152960396,
]
sh_c3 = [
    -0.5900435899266435,
    2.890611442640554,
    -0.4570457994644658,
    0.3731763325901154,
    -0.4570457994644658,
    1.445305721320277,
    -0.5900435899266435,
]

f32 = jnp.float32
bf16 = jnp.bfloat16


def sh_basis(dir_x, dir_y, dir_z):
    sq_x = dir_x * dir_x
    sq_y = dir_y * dir_y
    sq_z = dir_z * dir_z
    return [
        None,
        -sh_c1 * dir_y,
        sh_c1 * dir_z,
        -sh_c1 * dir_x,
        sh_c2[0] * dir_x * dir_y,
        sh_c2[1] * dir_y * dir_z,
        sh_c2[2] * (2.0 * sq_z - sq_x - sq_y),
        sh_c2[3] * dir_x * dir_z,
        sh_c2[4] * (sq_x - sq_y),
        sh_c3[0] * dir_y * (3.0 * sq_x - sq_y),
        sh_c3[1] * dir_x * dir_y * dir_z,
        sh_c3[2] * dir_y * (4.0 * sq_z - sq_x - sq_y),
        sh_c3[3] * dir_z * (2.0 * sq_z - 3.0 * sq_x - 3.0 * sq_y),
        sh_c3[4] * dir_x * (4.0 * sq_z - sq_x - sq_y),
        sh_c3[5] * dir_z * (sq_x - sq_y),
        sh_c3[6] * dir_x * (sq_x - 3.0 * sq_y),
    ]


def project(means, quats, log_scales, opacity, coeffs, cameras, centre_x, centre_y):
    inv_norm = 1.0 / jnp.sqrt(
        quats[0] * quats[0] + quats[1] * quats[1] + quats[2] * quats[2] + quats[3] * quats[3]
    )
    quat_w, quat_x, quat_y, quat_z = [quat * inv_norm for quat in quats]
    scales = [jnp.exp(log_scale) for log_scale in log_scales]
    rotation = [
        [
            1.0 - 2.0 * (quat_y * quat_y + quat_z * quat_z),
            2.0 * (quat_x * quat_y - quat_w * quat_z),
            2.0 * (quat_x * quat_z + quat_w * quat_y),
        ],
        [
            2.0 * (quat_x * quat_y + quat_w * quat_z),
            1.0 - 2.0 * (quat_x * quat_x + quat_z * quat_z),
            2.0 * (quat_y * quat_z - quat_w * quat_x),
        ],
        [
            2.0 * (quat_x * quat_z - quat_w * quat_y),
            2.0 * (quat_y * quat_z + quat_w * quat_x),
            1.0 - 2.0 * (quat_x * quat_x + quat_y * quat_y),
        ],
    ]
    spread = [[rotation[i][j] * scales[j] for j in range(3)] for i in range(3)]
    depth_z = means[2]
    inv_depth = 1.0 / depth_z
    jac_diag = focal_length * inv_depth
    diag_top = [jac_diag * spread[0][j] for j in range(3)]
    diag_low = [jac_diag * spread[1][j] for j in range(3)]
    log_alpha = -jnp.log(1.0 + jnp.exp(-opacity))
    views = []
    for cam_x, cam_y in cameras:
        rel_x = means[0] - cam_x
        rel_y = means[1] - cam_y
        ratio_u = jac_diag * rel_x
        ratio_v = jac_diag * rel_y
        jac_u = -ratio_u * inv_depth
        jac_v = -ratio_v * inv_depth
        top = [diag_top[j] + jac_u * spread[2][j] for j in range(3)]
        low = [diag_low[j] + jac_v * spread[2][j] for j in range(3)]
        cov_a = top[0] * top[0] + top[1] * top[1] + top[2] * top[2] + cov_blur
        cov_b = top[0] * low[0] + top[1] * low[1] + top[2] * low[2]
        cov_c = low[0] * low[0] + low[1] * low[1] + low[2] * low[2] + cov_blur
        inv_det = 1.0 / (cov_a * cov_c - cov_b * cov_b)
        inv_dist = 1.0 / jnp.sqrt(rel_x * rel_x + rel_y * rel_y + depth_z * depth_z)
        basis = sh_basis(rel_x * inv_dist, rel_y * inv_dist, depth_z * inv_dist)
        colours = []
        for channel in range(3):
            total = sh_c0 * coeffs[channel * SH] + 0.5
            for k in range(1, SH):
                total = total + coeffs[channel * SH + k] * basis[k]
            colours.append(jnp.maximum(total, 0.0))
        views.append(
            [
                ratio_u + centre_x,
                ratio_v + centre_y,
                cov_c * inv_det,
                -cov_b * inv_det,
                cov_a * inv_det,
                log_alpha,
            ]
            + colours
        )
    return views


def window_taps():
    raw_taps = [math.exp(-((tap_idx - RADIUS) ** 2) / 4.5) for tap_idx in range(2 * RADIUS + 1)]
    total = sum(raw_taps)
    return [tap / total for tap in raw_taps]


def band(out_count, in_count, offset):
    taps = window_taps()
    shape = (out_count, in_count)
    gap = lax.broadcasted_iota(jnp.int32, shape, 1) - lax.broadcasted_iota(jnp.int32, shape, 0)
    gap = jnp.abs(gap - offset)
    matrix = jnp.zeros(shape, f32)
    for far in range(RADIUS + 1):
        matrix = jnp.where(gap == far, taps[RADIUS + far], matrix)
    return matrix


def pieces(x, count):
    out = []
    for _ in range(count - 1):
        part = x.astype(bf16).astype(f32)
        out.append(part)
        x = x - part
    out.append(x)
    return out


def stack(x, count, axis=0):
    return jnp.concatenate(pieces(x, count), axis=axis).astype(bf16)


def dot(a, b):
    return lax.dot_general(a, b, (((1,), (0,)), ((), ())), preferred_element_type=f32)


def dot_t(a, b):
    return lax.dot_general(a, b, (((1,), (1,)), ((), ())), preferred_element_type=f32)


def dot_exact(a, b):
    return lax.dot_general(
        a, b, (((1,), (0,)), ((), ())), precision=lax.Precision.HIGHEST, preferred_element_type=f32
    )


def fold(x, count):
    size = x.shape[0] // count
    total = x[:size]
    for i in range(1, count):
        total = total + x[i * size : (i + 1) * size]
    return total


def loop(low, high, step):
    if high - low <= 8:
        for i in range(low, high):
            step(i)
    else:

        @pl.loop(low, high)
        def _(i):
            step(i)


def params(par, opacity):
    return (
        [par[:, 48 + i, :] for i in range(3)],
        [par[:, 56 + i, :] for i in range(4)],
        [par[:, 64 + i, :] for i in range(3)],
        opacity[...],
        [par[:, i, :] for i in range(48)],
    )


def pick_of(send, d, shard):
    local_row = lax.broadcasted_iota(jnp.int32, (shard, send.shape[2]), 0)
    return jnp.where(local_row == send[0, pl.ds(d, 1), :], 1.0, 0.0).astype(bf16)


def split_taps():
    high = [float(np.asarray(tap, ml_dtypes.bfloat16)) for tap in window_taps()]
    return high, [float(tap) - top for tap, top in zip(window_taps(), high)]


def band_split(out_count, in_rows, offset, axis):
    high, low = split_taps()
    count = len(in_rows)
    shape = (out_count, 3 * count) if axis == 1 else (3 * count, out_count)
    inner = lax.broadcasted_iota(jnp.int32, shape, axis)
    part = inner // count
    place = lax.rem(inner, count)
    start = in_rows[0]
    jump = [k for k in range(1, count) if in_rows[k] != in_rows[k - 1] + 1]
    row = place + start
    for k in jump:
        row = row + jnp.where(place >= k, in_rows[k] - in_rows[k - 1] - 1, 0)
    gap = jnp.abs(row - lax.broadcasted_iota(jnp.int32, shape, 1 - axis) - offset)
    matrix = jnp.zeros(shape, f32)
    for far in range(RADIUS + 1):
        tap = jnp.where(part == 2, low[RADIUS + far], high[RADIUS + far])
        matrix = jnp.where(gap == far, tap, matrix)
    return matrix.astype(bf16)


def stack_mixed(x, axis):
    high, low = pieces(x, 2)
    return jnp.concatenate([high, low, high], axis=axis).astype(bf16)


def side_by_side(x, count):
    size = x.shape[1] // count
    return jnp.concatenate([x[:, i * size : (i + 1) * size] for i in range(count)], axis=0)


def pad_rows(x):
    return jnp.concatenate([x, jnp.zeros((ROWS_MSG - x.shape[0], x.shape[1]), f32)], axis=0)


def flip(index, bits):
    bit = 1
    while bit <= bits:
        if bits & bit:
            index = index + bit * (1 - 2 * lax.rem(lax.div(index, bit), 2))
        bit *= 2
    return index


def spread_of(quats, log_scales):
    inv_norm = 1.0 / jnp.sqrt(
        quats[0] * quats[0] + quats[1] * quats[1] + quats[2] * quats[2] + quats[3] * quats[3]
    )
    w, x, y, z = [quat * inv_norm for quat in quats]
    rotation = [
        [1.0 - 2.0 * (y * y + z * z), 2.0 * (x * y - w * z), 2.0 * (x * z + w * y)],
        [2.0 * (x * y + w * z), 1.0 - 2.0 * (x * x + z * z), 2.0 * (y * z - w * x)],
        [2.0 * (x * z - w * y), 2.0 * (y * z + w * x), 1.0 - 2.0 * (x * x + y * y)],
    ]
    scales = [jnp.exp(log_scale) for log_scale in log_scales]
    return [[rotation[i][j] * scales[j] for j in range(3)] for i in range(3)]


def basis_slopes(x, y, z):
    xx, yy, zz = x * x, y * y, z * z
    xy, yz, xz = x * y, y * z, x * z
    gap = xx - yy
    four = 4.0 * zz
    return [
        {
            3: -sh_c1,
            4: sh_c2[0] * y,
            6: -2.0 * sh_c2[2] * x,
            7: sh_c2[3] * z,
            8: 2.0 * sh_c2[4] * x,
            9: 6.0 * sh_c3[0] * xy,
            10: sh_c3[1] * yz,
            11: -2.0 * sh_c3[2] * xy,
            12: -6.0 * sh_c3[3] * xz,
            13: sh_c3[4] * (four - 3.0 * xx - yy),
            14: 2.0 * sh_c3[5] * xz,
            15: 3.0 * sh_c3[6] * gap,
        },
        {
            1: -sh_c1,
            4: sh_c2[0] * x,
            5: sh_c2[1] * z,
            6: -2.0 * sh_c2[2] * y,
            8: -2.0 * sh_c2[4] * y,
            9: 3.0 * sh_c3[0] * gap,
            10: sh_c3[1] * xz,
            11: sh_c3[2] * (four - xx - 3.0 * yy),
            12: -6.0 * sh_c3[3] * yz,
            13: -2.0 * sh_c3[4] * xy,
            14: -2.0 * sh_c3[5] * yz,
            15: -6.0 * sh_c3[6] * xy,
        },
        {
            2: sh_c1,
            5: sh_c2[1] * y,
            6: 4.0 * sh_c2[2] * z,
            7: sh_c2[3] * x,
            10: sh_c3[1] * xy,
            11: 8.0 * sh_c3[2] * yz,
            12: sh_c3[3] * (6.0 * zz - 3.0 * xx - 3.0 * yy),
            13: 8.0 * sh_c3[4] * xz,
            14: sh_c3[5] * gap,
        },
    ]


N_KEPT = 42


def keep_view(kept, par, spread, means, inv_depth, jac_diag, cam_x, cam_y):
    rel_x = means[0] - cam_x
    rel_y = means[1] - cam_y
    ratio_u = jac_diag * rel_x
    ratio_v = jac_diag * rel_y
    jac_u = -ratio_u * inv_depth
    jac_v = -ratio_v * inv_depth
    top = [jac_diag * spread[0][j] + jac_u * spread[2][j] for j in range(3)]
    low = [jac_diag * spread[1][j] + jac_v * spread[2][j] for j in range(3)]
    cov_a = top[0] * top[0] + top[1] * top[1] + top[2] * top[2] + cov_blur
    cov_b = top[0] * low[0] + top[1] * low[1] + top[2] * low[2]
    cov_c = low[0] * low[0] + low[1] * low[1] + low[2] * low[2] + cov_blur
    inv_det = 1.0 / (cov_a * cov_c - cov_b * cov_b)
    out = [rel_x, rel_y, ratio_u, ratio_v, jac_u, jac_v] + top + low
    out += [cov_c * inv_det, -cov_b * inv_det, cov_a * inv_det]
    for i, x in enumerate(out):
        kept[i] = x
    inv_dist = 1.0 / jnp.sqrt(rel_x * rel_x + rel_y * rel_y + means[2] * means[2])
    turn = [rel_x * inv_dist, rel_y * inv_dist, means[2] * inv_dist]
    basis = sh_basis(*turn)
    slopes = basis_slopes(*turn)
    for k in range(1, SH):
        kept[26 + k] = basis[k]
    for channel in range(3):
        raw = sh_c0 * par[:, channel * SH, :] + 0.5
        slope = [None, None, None]
        for k in range(1, SH):
            coeff = par[:, channel * SH + k, :]
            raw = raw + coeff * basis[k]
            for i in range(3):
                if k in slopes[i]:
                    term = coeff * slopes[i][k]
                    slope[i] = term if slope[i] is None else slope[i] + term
        along = turn[0] * slope[0] + turn[1] * slope[1] + turn[2] * slope[2]
        for i in range(3):
            kept[15 + 3 * channel + i] = (slope[i] - turn[i] * along) * inv_dist
        kept[24 + channel] = jnp.where(raw > 0.0, 1.0, jnp.where(raw == 0.0, 0.5, 0.0))


def pull_view(kept, cots, inv_depth, jac_diag, spread):
    rel_x, rel_y, ratio_u, ratio_v, jac_u, jac_v = [kept[i] for i in range(6)]
    top = [kept[6 + j] for j in range(3)]
    low = [kept[9 + j] for j in range(3)]
    k0, k1, k2 = [kept[12 + i] for i in range(3)]
    g0, g1, g2 = cots[2], cots[3], cots[4]
    cov_a = -(k0 * k0 * g0 + k0 * k1 * g1 + k1 * k1 * g2)
    cov_b = -2.0 * (k0 * k1 * g0 + k1 * k2 * g2) - (k0 * k2 + k1 * k1) * g1
    cov_c = -(k1 * k1 * g0 + k1 * k2 * g1 + k2 * k2 * g2)
    d_top = [2.0 * cov_a * top[j] + cov_b * low[j] for j in range(3)]
    d_low = [2.0 * cov_c * low[j] + cov_b * top[j] for j in range(3)]
    d_base = [jac_u * d_top[j] + jac_v * d_low[j] for j in range(3)]
    d_jac_u = d_top[0] * spread[2][0] + d_top[1] * spread[2][1] + d_top[2] * spread[2][2]
    d_jac_v = d_low[0] * spread[2][0] + d_low[1] * spread[2][1] + d_low[2] * spread[2][2]
    d_ratio_u = cots[0] - inv_depth * d_jac_u
    d_ratio_v = cots[1] - inv_depth * d_jac_v
    shades = [cots[6 + c] * kept[24 + c] for c in range(3)]
    turn = [
        shades[0] * kept[15 + i] + shades[1] * kept[18 + i] + shades[2] * kept[21 + i]
        for i in range(3)
    ]
    d_x = jac_diag * d_ratio_u + turn[0]
    d_y = jac_diag * d_ratio_v + turn[1]
    d_diag = rel_x * d_ratio_u + rel_y * d_ratio_v
    d_inv = -(ratio_u * d_jac_u + ratio_v * d_jac_v)
    return d_top + d_low + d_base + [d_x, d_y, turn[2], d_diag, d_inv, cots[5]], shades


def octets(x):
    return [x[k : k + 8] for k in range(0, x.shape[0], 8)]


def products_before(parts):
    sub = lax.broadcasted_iota(jnp.int32, parts[0].shape, 0)
    run, before = parts[0], [None]
    for part in parts[1:]:
        before.append(run)
        run = run * part
    lead = jnp.where(sub >= 1, pltpu.roll(run, 1, 0), 1.0)
    for step in (1, 2, 4):
        lead = lead * jnp.where(sub >= step, pltpu.roll(lead, step, 0), 1.0)
    return [lead if x is None else x * lead for x in before]


def sums_after(parts):
    sub = lax.broadcasted_iota(jnp.int32, parts[0].shape, 0)
    run, after = parts[-1], [None]
    for part in parts[-2::-1]:
        after.append(run)
        run = run + part
    tail = jnp.where(sub < 7, pltpu.roll(run, 7, 0), 0.0)
    for step in (1, 2, 4):
        tail = tail + jnp.where(sub < 8 - step, pltpu.roll(tail, 8 - step, 0), 0.0)
    return [tail if x is None else x + tail for x in after[::-1]]


def near_kernel(
    n_gs,
    n_view,
    means_in,
    quats_in,
    scales_in,
    opacity_in,
    sh_in,
    camera_in,
    targets_in,
    send_in,
    lists_in,
    lens_in,
    pic_out,
    means_out,
    quats_out,
    scales_out,
    opacity_out,
    sh_out,
    par,
    opacity,
    send,
    means,
    quats,
    scales,
    sh,
    camera,
    targets,
    lists,
    lens,
    cams,
    row_buf,
    msg_out,
    msg_in,
    slot_mask,
    slot_mask_t,
    row_mask,
    bases,
    bases_t,
    tile_buf,
    ratio_buf,
    weight_buf,
    shade_buf,
    split_buf,
    power_buf,
    pic,
    halo,
    t_halo,
    cot,
    back_out,
    back_in,
    placed,
    kept,
    cot_views,
    g_sum,
    g_par,
    load_sems,
    send_cam,
    recv_cam,
    send_one,
    recv_one,
    send_halo,
    recv_halo,
    send_tgt,
    recv_tgt,
    send_two,
    recv_two,
    send_three,
    recv_three,
):
    gs = lax.axis_index("gs")
    view = lax.axis_index("view")
    shard = means.shape[1]
    chunks = shard // LANES
    cap = send.shape[2]
    tiles, list_size = lists.shape
    groups = n_view // 2
    core = lax.rem(view, 2)
    group = lax.div(view, 2)
    has_up = gs > 0
    has_down = gs < n_gs - 1
    near = range(1, n_gs)
    far = range(n_gs - 1, 0, -1)

    def cousin(j):
        return lax.rem(view + 2 * j, n_view)

    reach = 2 * RADIUS
    halo[...] = jnp.zeros_like(halo)
    t_halo[...] = jnp.zeros_like(t_halo)

    barrier = pltpu.get_barrier_semaphore()

    def greet(strip, cam):
        pl.semaphore_signal(barrier, inc=1, device_id=(strip, cam), device_id_type=MESH)

    for k in range(n_gs - 1, -1, -1):
        for j in range(groups):
            if k or j:
                greet(flip(gs, k), cousin(j))
    for j in range(groups):
        greet(gs, flip(cousin(j), 1))
    greeted = n_gs - 1 + (groups - 1) * n_gs + groups

    loads = [
        pltpu.make_async_copy(src, dst, load_sems.at[k])
        for k, (src, dst) in enumerate(
            [
                (sh_in, sh),
                (means_in, means),
                (quats_in, quats),
                (scales_in, scales),
                (opacity_in, opacity),
                (camera_in, camera),
                (send_in, send),
                (lists_in.at[0, 0], lists),
                (lens_in.at[0], lens),
                (targets_in, targets),
            ]
        )
    ]
    for load in loads:
        load.start()

    for load in loads[:7]:
        load.wait()

    for c in range(chunks):
        cols = slice(c * LANES, (c + 1) * LANES)
        par[c, 0:48, :] = sh[:, cols]
        par[c, 48:51, :] = means[:, cols]
        par[c, 56:60, :] = quats[:, cols]
        par[c, 64:67, :] = scales[:, cols]

    centre_x = 0.5 * tiles * TILE
    centre_y = 0.5 * n_gs * TILE
    cam_x = camera[0:1, 0:1]
    cam_y = camera[0:1, 1:2]
    rows = project(*params(par, opacity), [(cam_x, cam_y)], centre_x, centre_y)[0]
    row_buf[...] = jnp.zeros_like(row_buf)
    for i in range(9):
        row_buf[:, i, :] = rows[i]
    table = stack(jnp.concatenate([row_buf[c] for c in range(chunks)], axis=1), 3)

    def fill(d):
        msg_out[d] = fold(dot(table, pick_of(send, d, shard)), 3)[0:9]

    def first_copy(d, s):
        return pltpu.make_async_remote_copy(
            src_ref=msg_out.at[d],
            dst_ref=msg_in.at[s],
            send_sem=send_one.at[d],
            recv_sem=recv_one.at[s],
            device_id=(d, view),
            device_id_type=MESH,
        )

    for k in far:
        fill(flip(gs, k))
    pl.semaphore_wait(barrier, greeted)

    for k in far:
        first_copy(flip(gs, k), gs).start()
    fill(gs)
    msg_in[gs] = msg_out[gs]

    def cam_copy(to, of):
        return pltpu.make_async_remote_copy(
            src_ref=cams.at[of],
            dst_ref=cams.at[of],
            send_sem=send_cam.at[to],
            recv_sem=recv_cam.at[of],
            device_id=(gs, to),
            device_id_type=MESH,
        )

    lane_one = lax.broadcasted_iota(jnp.int32, (1, LANES), 1)
    cams[view] = jnp.where(lane_one == 0, cam_x, cam_y)
    for k in range(1, n_view):
        cam_copy(lax.rem(view + k, n_view), view).start()

    def halo_copy(src, dst, sends, recvs, side):
        other = gs + 1 if side == 0 else gs - 1
        rows = pl.ds(TILE - reach if side == 0 else 0, reach)
        return pltpu.make_async_remote_copy(
            src_ref=src.at[:, rows],
            dst_ref=dst.at[side, :, rows],
            send_sem=sends.at[side],
            recv_sem=recvs.at[side],
            device_id=(other, view),
            device_id_type=MESH,
        )

    def exchange(src, dst, sends, recvs, start, ends=(False, True)):
        def act(copy, recv):
            if start:
                copy.start()
            elif recv:
                copy.wait_recv()
            else:
                copy.wait_send()

        for recv in ends:
            if start and recv:
                continue

            @pl.when(has_down)
            def _():
                act(halo_copy(src, dst, sends, recvs, 1 if recv else 0), recv)

            @pl.when(has_up)
            def _():
                act(halo_copy(src, dst, sends, recvs, 0 if recv else 1), recv)

    for load in loads[7:]:
        load.wait()
    exchange(targets.at[0], t_halo, send_tgt, recv_tgt, True)

    n_chunk, _, wide = weight_buf.shape
    width = tiles * TILE
    per = wide // width
    deep = list_size // 8
    place = lax.broadcasted_iota(jnp.int32, (list_size, list_size), 1)
    moved = lax.broadcasted_iota(jnp.int32, (list_size, list_size), 0) == (
        lax.rem(place, 8) * deep + place // 8
    )
    placed_lists = dot_exact(lists[...].astype(f32), jnp.where(moved, 1.0, 0.0))
    placed_lists = jnp.floor(placed_lists + 0.5)
    whole_lists = placed_lists.astype(jnp.int32)
    slot_row = lax.broadcasted_iota(jnp.int32, (cap, list_size), 0)
    for k in range(n_gs):
        here = slot_row + flip(gs, k) * cap
        for t in range(tiles):
            slot_mask[k, :, t * list_size : (t + 1) * list_size] = jnp.where(
                here == whole_lists[t : t + 1, :], 1.0, 0.0
            ).astype(bf16)
    lists_t = jnp.transpose(placed_lists)
    slot_lane = lax.broadcasted_iota(jnp.int32, (list_size, cap), 1)
    for t in range(tiles):
        listed = jnp.broadcast_to(lists_t[:, t : t + 1], (list_size, cap))
        for k in range(n_gs):
            here = (slot_lane + flip(gs, k) * cap).astype(f32)
            slot_mask_t[k, t * list_size : (t + 1) * list_size, :] = jnp.where(
                here == listed, 1.0, 0.0
            ).astype(bf16)

    lane = lax.broadcasted_iota(jnp.int32, (tiles, wide), 1)
    in_tile = lax.rem(lane, width) // TILE == lax.broadcasted_iota(jnp.int32, (tiles, wide), 0)
    off_q = (lax.rem(lane, TILE) - TILE // 2).astype(f32)
    half_r = (lane // width).astype(f32)
    for i in range(n_chunk):
        off_r = half_r + float(i * per - TILE // 2)
        out = [jnp.ones_like(off_q), off_q, off_r, off_q * off_q, off_q * off_r, off_r * off_r]
        base = jnp.concatenate([jnp.where(in_tile, x, 0.0) for x in out], axis=0)
        bases[i] = base.astype(bf16)
        bases_t[i * wide : (i + 1) * wide, :] = jnp.transpose(base).astype(bf16)
    shape = (9 * tiles, 3 * width)
    row_of, lane_of = [lax.broadcasted_iota(jnp.int32, shape, k) for k in range(2)]
    at_tile = lax.rem(row_of, tiles) == lax.rem(lane_of, width) // TILE
    at_channel = lax.rem(row_of // tiles, 3) == lane_of // width
    widen = jnp.where(jnp.logical_and(at_tile, at_channel), 1.0, 0.0).astype(bf16)
    p_means, p_quats, p_scales, p_opacity, _ = params(par, opacity)
    spread, pull_spread = jax.vjp(spread_of, p_quats, p_scales)
    inv_depth = 1.0 / p_means[2]
    jac_diag = focal_length * inv_depth

    def keep(h, j, of):
        at = cams[of]
        keep_view(
            kept.at[h, j], par, spread, p_means, inv_depth, jac_diag, at[:, 0:1], at[:, 1:2]
        )

    keep(0, group, view)
    for t in range(tiles):
        tile_buf[t] = jnp.zeros((ROWS_MSG, list_size), f32)

    def gather(k, s):
        got = fold(dot(stack(pad_rows(msg_in[s]), 3), slot_mask[k]), 3)
        for t in range(tiles):
            tile_buf[t] += got[:, t * list_size : (t + 1) * list_size]

    gather(0, gs)
    for k in near:
        s = flip(gs, k)
        first_copy(gs, s).wait_recv()
        gather(k, s)

    diagonal = lax.broadcasted_iota(jnp.int32, (tiles, tiles), 0) == lax.broadcasted_iota(
        jnp.int32, (tiles, tiles), 1
    )
    used = jnp.sum(jnp.where(diagonal, lens[...].astype(f32), 0.0), axis=1, keepdims=True)
    entry = lax.broadcasted_iota(jnp.int32, (tiles, list_size), 1)
    entry = lax.rem(entry, 8) * deep + entry // 8
    live = entry.astype(f32) < used
    mid_q = (lax.broadcasted_iota(jnp.int32, (tiles, list_size), 0) * TILE + TILE // 2).astype(f32)
    mid_r = (gs * TILE + TILE // 2).astype(f32)
    off_u = tile_buf[:, 0, :] - mid_q
    off_w = tile_buf[:, 1, :] - mid_r
    k0 = tile_buf[:, 2, :]
    k1 = tile_buf[:, 3, :]
    k2 = tile_buf[:, 4, :]
    lin_u = k0 * off_u + k1 * off_w
    lin_w = k2 * off_w + k1 * off_u
    terms = [
        jnp.where(live, tile_buf[:, 5, :] - 0.5 * (off_u * lin_u + off_w * lin_w), -10000.0),
        jnp.where(live, lin_u, 0.0),
        jnp.where(live, lin_w, 0.0),
        jnp.where(live, -0.5 * k0, 0.0),
        jnp.where(live, -k1, 0.0),
        jnp.where(live, -0.5 * k2, 0.0),
    ]
    term_t = jnp.transpose(jnp.concatenate(pieces(jnp.concatenate(terms, axis=0), 3), axis=0))
    term_t = term_t.astype(bf16)
    colour = jnp.concatenate([tile_buf[:, 6 + c, :] for c in range(3)], axis=0)
    col_t = jnp.transpose(jnp.concatenate(pieces(colour, 3), axis=0)).astype(bf16)
    shade_buf[...] = dot(col_t, widen)

    for i in range(n_chunk):
        base = bases[i]
        ratio_buf[i] = jnp.exp(dot(term_t, jnp.concatenate([base, base, base], axis=0)))
    for i in range(n_chunk):
        for half in range(per):
            lanes = slice(half * width, (half + 1) * width)
            alpha = octets(ratio_buf[i, :, lanes])
            before = products_before([1.0 - x for x in alpha])
            weight = [x * y for x, y in zip(alpha, before)]
            weight_buf[i, :, lanes] = jnp.concatenate(weight, axis=0)
            row = i * per + half
            for c in range(3):
                shade = octets(shade_buf[:, c * width : (c + 1) * width])
                total = weight[0] * shade[0]
                for x, y in zip(weight[1:], shade[1:]):
                    total = total + x * y
                pic[c, row : row + 1, :] = jnp.sum(total, axis=0, keepdims=True)

    exchange(pic, halo, send_halo, recv_halo, True)
    pic_out[0] = pic[...]
    exchange(targets.at[0], t_halo, send_tgt, recv_tgt, False)
    tall = 2 * TILE
    across = band_split(width, list(range(width)), 0, 0)
    tgts = [
        jnp.concatenate([t_halo[0, c], targets[0, c], t_halo[1, c]], axis=0) for c in range(3)
    ]
    planes = []
    for c in range(3):
        planes += [tgts[c], tgts[c] * tgts[c]]
    rows_all = list(range(3 * TILE))
    band_all = band_split(tall, rows_all, TILE // 2, 1)
    down = dot(band_all, stack_mixed(jnp.concatenate(planes, axis=1), 0))
    blur_tgt = dot(stack_mixed(side_by_side(down, 6), 1), across)
    own = []
    for c in range(3):
        img = pic[c]
        own += [img, img * img, img * targets[0, c]]
    band_own = band_split(tall, rows_all[TILE : 2 * TILE], TILE // 2, 1)
    down_own = dot(band_own, stack_mixed(jnp.concatenate(own, axis=1), 0))
    band_far = band_split(tall, rows_all[:TILE] + rows_all[2 * TILE :], TILE // 2, 1)
    band_back = band_split(TILE, list(range(tall)), TILE // 2, 1)
    directs = []
    for c in range(3):
        res = pic[c] - targets[0, c]
        directs.append(
            (1.0 - ssim_weight) / (TILE * TILE) * res / jnp.sqrt(res * res + charb_eps)
        )
    for i in range(n_chunk):
        split_buf[i] = stack(jnp.transpose(weight_buf[i]), 2, 1)
        for half in range(per):
            lanes = slice(half * width, (half + 1) * width)
            alpha = ratio_buf[i, :, lanes]
            ratio = alpha / (1.0 - alpha)
            weight = weight_buf[i, :, lanes]
            for c in range(3):
                share = weight * shade_buf[:, c * width : (c + 1) * width]
                after = jnp.concatenate(sums_after(octets(share)), axis=0)
                power_buf[c, i, :, lanes] = share - ratio * after
    exchange(pic, halo, send_halo, recv_halo, False)

    beyond = []
    for c in range(3):
        img = jnp.concatenate([halo[0, c], halo[1, c]], axis=0)
        tgt = jnp.concatenate([t_halo[0, c], t_halo[1, c]], axis=0)
        beyond += [img, img * img, img * tgt]
    down = down_own + dot(band_far, stack_mixed(jnp.concatenate(beyond, axis=1), 0))
    blurred = dot(stack_mixed(side_by_side(down, 9), 1), across)
    at_row = lax.broadcasted_iota(jnp.int32, (tall, width), 0) + gs * TILE - TILE // 2
    inside = jnp.logical_and(at_row >= 0, at_row < n_gs * TILE)
    scale = -ssim_weight / (TILE * TILE)
    cots = []
    for c in range(3):
        mean_x, raw_xx, raw_xy = [
            blurred[(3 * c + i) * tall : (3 * c + i + 1) * tall] for i in range(3)
        ]
        mean_y, raw_yy = [
            blur_tgt[(2 * c + i) * tall : (2 * c + i + 1) * tall] for i in range(2)
        ]
        top_a = 2.0 * mean_x * mean_y + ssim_one
        top_b = 2.0 * (raw_xy - mean_x * mean_y) + ssim_two
        low_c = mean_x * mean_x + mean_y * mean_y + ssim_one
        low_d = (raw_xx - mean_x * mean_x) + (raw_yy - mean_y * mean_y) + ssim_two
        inv_cd = 1.0 / (low_c * low_d)
        inv_dd = inv_cd * low_c
        ssim = top_a * top_b * inv_cd
        d_mean = 2.0 * mean_y * (top_b - top_a) * inv_cd - 2.0 * mean_x * ssim * (
            inv_cd * low_d - inv_dd
        )
        d_xx = -ssim * inv_dd
        d_xy = 2.0 * top_a * inv_cd
        cots += [jnp.where(inside, scale * part, 0.0) for part in (d_mean, d_xx, d_xy)]
    spread_rows = dot(band_back, stack_mixed(jnp.concatenate(cots, axis=1), 0))
    spread_rows = dot(stack_mixed(side_by_side(spread_rows, 9), 1), across)
    grad_rows = []
    for c in range(3):
        s_mean, s_xx, s_xy = [spread_rows[(3 * c + i) * TILE : (3 * c + i + 1) * TILE] for i in range(3)]
        grad_rows.append(directs[c] + s_mean + 2.0 * pic[c] * s_xx + targets[0, c] * s_xy)

    d_terms = jnp.zeros((2 * list_size, 6 * tiles), f32)
    d_colour = jnp.zeros((6 * tiles, 2 * list_size), f32)
    for i in range(n_chunk):
        lines = [
            jnp.concatenate(
                [grad_rows[c][i * per + half : i * per + half + 1] for half in range(per)], axis=1
            )
            for c in range(3)
        ]
        shades = stack(jnp.concatenate([jnp.where(in_tile, x, 0.0) for x in lines], axis=0), 2)
        d_power = lines[0] * power_buf[0, i] + lines[1] * power_buf[1, i] + lines[2] * power_buf[2, i]
        d_terms = d_terms + dot(stack(d_power, 2), bases_t[i * wide : (i + 1) * wide, :])
        d_colour = d_colour + dot(shades, split_buf[i])
    d_terms = jnp.transpose(fold(d_terms, 2))
    d_colour = fold(d_colour[:, :list_size] + d_colour[:, list_size:], 2)

    d0, d1, d2, d3, d4, d5 = [d_terms[k * tiles : (k + 1) * tiles] for k in range(6)]
    e1 = d1 - off_u * d0
    e2 = d2 - off_w * d0
    cot[...] = jnp.zeros_like(cot)
    cot[:, 0, :] = k0 * e1 + k1 * e2
    cot[:, 1, :] = k2 * e2 + k1 * e1
    cot[:, 2, :] = -0.5 * d3 + off_u * (d1 - 0.5 * off_u * d0)
    cot[:, 3, :] = off_w * e1 + off_u * d2 - d4
    cot[:, 4, :] = -0.5 * d5 + off_w * (d2 - 0.5 * off_w * d0)
    cot[:, 5, :] = d0
    for c in range(3):
        cot[:, 6 + c, :] = d_colour[c * tiles : (c + 1) * tiles]
    cots = jnp.concatenate([stack(cot[t], 2) for t in range(tiles)], axis=1)

    def out_copy(j, d):
        return pltpu.make_async_remote_copy(
            src_ref=back_out.at[d],
            dst_ref=back_in.at[group, gs],
            send_sem=send_two.at[j, d],
            recv_sem=recv_two.at[group, gs],
            device_id=(d, cousin(j)),
            device_id_type=MESH,
        )

    def in_copy(j, s):
        of = lax.div(cousin(j), 2)
        return pltpu.make_async_remote_copy(
            src_ref=back_out.at[s],
            dst_ref=back_in.at[of, s],
            send_sem=send_two.at[j, s],
            recv_sem=recv_two.at[of, s],
            device_id=(s, cousin(j)),
            device_id_type=MESH,
        )

    for k in list(far) + [0]:
        d = flip(gs, k)
        back_out[d] = fold(dot(cots, slot_mask_t[k]), 2)[0:9]
        for j in range(groups):
            if k or j:
                out_copy(j, d).start()
    back_in[group, gs] = back_out[gs]

    send_t = jnp.transpose(send[0].astype(f32))
    shard_lane = lax.broadcasted_iota(jnp.int32, (cap, shard), 1).astype(f32)
    for s in range(n_gs):
        row_mask[s] = jnp.where(shard_lane == send_t[:, s : s + 1], 1.0, 0.0).astype(bf16)
    for k in range(1, n_view):
        cam_copy(view, lax.rem(view + n_view - k, n_view)).wait_recv()
    for j in range(1, groups):
        keep(0, lax.div(cousin(j), 2), cousin(j))
    for j in range(groups):
        keep(1, j, 2 * j + 1 - core)


    def put_back(s, first):
        both = [stack(pad_rows(back_in[j, s]), 2) for j in range(groups)]
        got = dot(jnp.concatenate(both, axis=0), row_mask[s])
        placed[...] = got if first else placed[...] + got

    for k in range(n_gs):
        s = flip(gs, k)
        for j in range(groups):
            if k or j:
                in_copy(j, s).wait_recv()
        put_back(s, k == 0)
    for j in range(groups):
        mine = fold(placed[2 * ROWS_MSG * j : 2 * ROWS_MSG * (j + 1)], 2)
        for c in range(chunks):
            cot_views[core, j, :, c, :] = mine[0:9, c * LANES : (c + 1) * LANES]

    def third_copy(of):
        return pltpu.make_async_remote_copy(
            src_ref=cot_views.at[of],
            dst_ref=cot_views.at[of],
            send_sem=send_three.at[0],
            recv_sem=recv_three.at[0],
            device_id=(gs, flip(view, 1)),
            device_id_type=MESH,
        )

    third_copy(core).start()

    def pull_half(h):
        side = core if h == 0 else 1 - core
        total = None
        tints = []
        for j in range(groups):
            cots = [cot_views[side, j, i] for i in range(9)]
            got, shades = pull_view(kept.at[h, j], cots, inv_depth, jac_diag, spread)
            total = got if total is None else [a + b for a, b in zip(total, got)]
            tints.append(shades)
        for i in range(15):
            if h == 0:
                g_sum[i] = total[i]
            else:
                total[i] = total[i] + g_sum[i]
        for k in range(SH):
            for c in range(3):
                part = None
                for j in range(groups):
                    term = tints[j][c] * (sh_c0 if k == 0 else kept[h, j, 26 + k])
                    part = term if part is None else part + term
                if h == 1:
                    part = part + g_par[:, c * SH + k, :]
                g_par[:, c * SH + k, :] = part
        return total

    pull_half(0)
    third_copy(1 - core).wait_recv()
    total = pull_half(1)
    d_top, d_low, d_base = total[0:3], total[3:6], total[6:9]
    d_x, d_y, d_z, d_diag, d_inv, d_log = total[9:15]
    for j in range(3):
        d_diag = d_diag + d_top[j] * spread[0][j] + d_low[j] * spread[1][j]
    d_inv = d_inv + focal_length * d_diag
    d_z = d_z - inv_depth * inv_depth * d_inv
    d_quats, d_scales = pull_spread(
        [[jac_diag * x for x in d_top], [jac_diag * x for x in d_low], list(d_base)]
    )
    decay = jnp.exp(-p_opacity)
    opacity_out[...] = d_log * decay / (1.0 + decay)
    for i, x in enumerate([d_x, d_y, d_z]):
        g_par[:, 48 + i, :] = x
    for i in range(4):
        g_par[:, 56 + i, :] = d_quats[i]
    for i in range(3):
        g_par[:, 64 + i, :] = d_scales[i]
    for c in range(chunks):
        cols = slice(c * LANES, (c + 1) * LANES)
        sh_out[:, cols] = g_par[c, 0:48, :]
        means_out[:, cols] = g_par[c, 48:51, :]
        quats_out[:, cols] = g_par[c, 56:60, :]
        scales_out[:, cols] = g_par[c, 64:67, :]

    for k in near:
        first_copy(flip(gs, k), gs).wait_send()
    for k in range(1, n_view):
        cam_copy(lax.rem(view + k, n_view), view).wait_send()
    for k in range(n_gs):
        for j in range(groups):
            if k or j:
                out_copy(j, flip(gs, k)).wait_send()
    third_copy(core).wait_send()


def store_kernel(*refs):
    count = len(refs) // 2
    sources, places, sems = refs[:count], refs[count : 2 * count], refs[-1]
    stores = [
        pltpu.make_async_copy(src, dst, sems.at[k])
        for k, (src, dst) in enumerate(zip(sources, places))
    ]
    for store in stores:
        store.start()
    for store in stores:
        store.wait()


def far_kernel(
    n_gs,
    n_view,
    means_in,
    quats_in,
    scales_in,
    opacity_in,
    sh_in,
    camera_in,
    targets_in,
    send_in,
    lists_in,
    lens_in,
    pic_out,
    views_out,
    par,
    opacity,
    send,
    means,
    quats,
    scales,
    sh,
    camera,
    targets,
    lists,
    lens,
    row_buf,
    msg_out,
    msg_in,
    tile_buf,
    ratio_buf,
    weight_buf,
    pic,
    halo,
    t_halo,
    cot,
    back_out,
    back_in,
    placed,
    load_sems,
    send_one,
    recv_one,
    send_halo,
    recv_halo,
    send_tgt,
    recv_tgt,
    send_two,
    recv_two,
    send_three,
    recv_three,
):
    loads = [
        pltpu.make_async_copy(src, dst, load_sems.at[k])
        for k, (src, dst) in enumerate(
            [
                (sh_in, sh),
                (means_in, means),
                (quats_in, quats),
                (scales_in, scales),
                (opacity_in, opacity),
                (camera_in, camera),
                (send_in, send),
                (targets_in, targets),
                (lists_in.at[0, 0], lists),
                (lens_in.at[0], lens),
            ]
        )
    ]
    for load in loads:
        load.start()
    gs = lax.axis_index("gs")
    view = lax.axis_index("view")
    chunks = means.shape[1] // LANES
    cap = send.shape[2]
    shard = means.shape[1]
    tiles = lists.shape[0]
    list_size = lists.shape[1]
    has_up = gs > 0
    has_down = gs < n_gs - 1

    barrier = pltpu.get_barrier_semaphore()

    def greet(strip, cam):
        pl.semaphore_signal(barrier, inc=1, device_id=(strip, cam), device_id_type=MESH)

    loop(1, n_gs, lambda k: greet(lax.rem(gs + k, n_gs), view))
    loop(1, n_view, lambda k: greet(gs, lax.rem(view + k, n_view)))

    for load in loads:
        load.wait()

    for c in range(chunks):
        cols = slice(c * LANES, (c + 1) * LANES)
        par[c, 0:48, :] = sh[:, cols]
        par[c, 48:51, :] = means[:, cols]
        par[c, 56:60, :] = quats[:, cols]
        par[c, 64:67, :] = scales[:, cols]

    centre_x = 0.5 * tiles * TILE
    centre_y = 0.5 * n_gs * TILE
    cam_x = camera[0:1, 0:1]
    cam_y = camera[0:1, 1:2]
    rows = project(*params(par, opacity), [(cam_x, cam_y)], centre_x, centre_y)[0]
    row_buf[...] = jnp.zeros_like(row_buf)
    for i in range(9):
        row_buf[:, i, :] = rows[i]
    table = stack(jnp.concatenate([row_buf[c] for c in range(chunks)], axis=1), 3)

    def fill(d):
        msg_out[d] = fold(dot(table, pick_of(send, d, shard)), 3)

    def first_copy(d, s):
        return pltpu.make_async_remote_copy(
            src_ref=msg_out.at[d],
            dst_ref=msg_in.at[s],
            send_sem=send_one.at[d],
            recv_sem=recv_one.at[s],
            device_id=(d, view),
            device_id_type=MESH,
        )

    pl.semaphore_wait(barrier, n_gs + n_view - 2)

    def send_first(k):
        d = lax.rem(gs + k, n_gs)
        fill(d)
        first_copy(d, gs).start()

    loop(1, n_gs, send_first)
    fill(gs)
    msg_in[gs] = msg_out[gs]

    def halo_copy(src, dst, sends, recvs, side):
        other = gs + 1 if side == 0 else gs - 1
        return pltpu.make_async_remote_copy(
            src_ref=src,
            dst_ref=dst.at[side],
            send_sem=sends.at[side],
            recv_sem=recvs.at[side],
            device_id=(other, view),
            device_id_type=MESH,
        )

    def exchange(src, dst, sends, recvs, start):
        def act(copy, recv):
            if start:
                if not recv:
                    copy.start()
            elif recv:
                copy.wait_recv()
            else:
                copy.wait_send()

        for recv in (False, True):
            if start and recv:
                continue

            @pl.when(has_down)
            def _():
                act(halo_copy(src, dst, sends, recvs, 1 if recv else 0), recv)

            @pl.when(has_up)
            def _():
                act(halo_copy(src, dst, sends, recvs, 0 if recv else 1), recv)

    exchange(targets.at[0], t_halo, send_tgt, recv_tgt, True)

    @pl.when(jnp.logical_not(has_up))
    def _():
        halo[0] = jnp.zeros_like(halo[0])
        t_halo[0] = jnp.zeros_like(t_halo[0])

    @pl.when(jnp.logical_not(has_down))
    def _():
        halo[1] = jnp.zeros_like(halo[1])
        t_halo[1] = jnp.zeros_like(t_halo[1])


    slot_row = lax.broadcasted_iota(jnp.int32, (cap, list_size), 0)

    def slot_pick(s, t):
        return jnp.where(slot_row + s * cap == lists[t : t + 1, :], 1.0, 0.0).astype(bf16)

    tile_buf[...] = jnp.zeros_like(tile_buf)

    def gather(s):
        got = stack(msg_in[s], 3)
        for t in range(tiles):
            tile_buf[t] += fold(dot(got, slot_pick(s, t)), 3)

    gather(gs)

    def gather_next(k):
        s = lax.rem(gs + n_gs - k, n_gs)
        first_copy(gs, s).wait_recv()
        gather(s)

    loop(1, n_gs, gather_next)

    diagonal = lax.broadcasted_iota(jnp.int32, (tiles, tiles), 0) == lax.broadcasted_iota(
        jnp.int32, (tiles, tiles), 1
    )
    used = jnp.sum(jnp.where(diagonal, lens[...].astype(f32), 0.0), axis=1, keepdims=True)
    entry = lax.broadcasted_iota(jnp.int32, (tiles, list_size), 1)
    live = entry.astype(f32) < used
    mid_q = (lax.broadcasted_iota(jnp.int32, (tiles, list_size), 0) * TILE + TILE // 2).astype(f32)
    mid_r = (gs * TILE + TILE // 2).astype(f32)
    off_u = tile_buf[:, 0, :] - mid_q
    off_w = tile_buf[:, 1, :] - mid_r
    k0 = tile_buf[:, 2, :]
    k1 = tile_buf[:, 3, :]
    k2 = tile_buf[:, 4, :]
    lin_u = k0 * off_u + k1 * off_w
    lin_w = k2 * off_w + k1 * off_u
    terms = [
        jnp.where(live, tile_buf[:, 5, :] - 0.5 * (off_u * lin_u + off_w * lin_w), -10000.0),
        jnp.where(live, lin_u, 0.0),
        jnp.where(live, lin_w, 0.0),
        jnp.where(live, -0.5 * k0, 0.0),
        jnp.where(live, -k1, 0.0),
        jnp.where(live, -0.5 * k2, 0.0),
    ]
    term_t = jnp.transpose(jnp.concatenate(pieces(jnp.concatenate(terms, axis=0), 3), axis=0))
    term_t = term_t.astype(bf16)
    colour = jnp.concatenate([tile_buf[:, 6 + c, :] for c in range(3)], axis=0)
    col_hi, col_lo = pieces(colour, 2)
    col_two = jnp.concatenate([col_hi, col_lo], axis=0)
    col_wide = jnp.concatenate([col_two, col_two], axis=1).astype(bf16)
    col_t = jnp.transpose(jnp.concatenate([col_hi, col_lo, col_hi], axis=0)).astype(bf16)

    n_chunk, _, wide = weight_buf.shape
    width = tiles * TILE
    lane = lax.broadcasted_iota(jnp.int32, (tiles, wide), 1)
    in_tile = lax.rem(lane, width) // TILE == lax.broadcasted_iota(jnp.int32, (tiles, wide), 0)

    off_q = (lax.rem(lane, TILE) - TILE // 2).astype(f32)
    half_r = (lane // width).astype(f32)

    def basis(i):
        off_r = half_r + float(i * (wide // width) - TILE // 2)
        out = [jnp.ones_like(off_q), off_q, off_r, off_q * off_q, off_q * off_r, off_r * off_r]
        return jnp.concatenate([jnp.where(in_tile, x, 0.0) for x in out], axis=0).astype(bf16)

    shape = (list_size, 2 * list_size)
    list_row = lax.broadcasted_iota(jnp.int32, shape, 0)
    list_col = lax.rem(lax.broadcasted_iota(jnp.int32, shape, 1), list_size)
    prefix = jnp.where(list_col < list_row, 1.0, 0.0).astype(bf16)
    suffix = jnp.where(list_col > list_row, 1.0, 0.0).astype(bf16)

    for i in range(n_chunk):
        base = basis(i)
        alpha = jnp.exp(dot(term_t, jnp.concatenate([base, base, base], axis=0)))
        keep = 1.0 - alpha
        weight = alpha * jnp.exp(dot(prefix, stack(jnp.log(keep), 2)))
        ratio_buf[i] = alpha / keep
        weight_buf[i] = weight
        drawn = fold(dot(col_wide, stack(weight, 2)), 2)
        for c in range(3):
            mine = jnp.where(in_tile, drawn[c * tiles : (c + 1) * tiles], 0.0)
            line = jnp.sum(mine, axis=0, keepdims=True)
            for half in range(wide // width):
                row = i * (wide // width) + half
                pic[c, row : row + 1, :] = line[:, half * width : (half + 1) * width]

    exchange(pic, halo, send_halo, recv_halo, True)
    pic_out[0] = pic[...]
    exchange(targets.at[0], t_halo, send_tgt, recv_tgt, False)
    exchange(pic, halo, send_halo, recv_halo, False)

    tall = 2 * TILE
    across = band(width, width, 0)
    stacked = []
    images = []
    for c in range(3):
        img = jnp.concatenate([halo[0, c], pic[c], halo[1, c]], axis=0)
        tgt = jnp.concatenate([t_halo[0, c], targets[0, c], t_halo[1, c]], axis=0)
        images.append((img, tgt))
        stacked += [img, tgt, img * img, tgt * tgt, img * tgt]
    down = dot_exact(band(tall, 3 * TILE, TILE // 2), jnp.concatenate(stacked, axis=1))
    down = jnp.concatenate([down[:, i * width : (i + 1) * width] for i in range(15)], axis=0)
    blurred = dot_exact(down, across)
    at_row = lax.broadcasted_iota(jnp.int32, (tall, width), 0) + gs * TILE - TILE // 2
    inside = jnp.logical_and(at_row >= 0, at_row < n_gs * TILE)
    scale = -ssim_weight / (TILE * TILE)
    cots = []
    for c in range(3):
        mean_x, mean_y, raw_xx, raw_yy, raw_xy = [
            blurred[(5 * c + i) * tall : (5 * c + i + 1) * tall] for i in range(5)
        ]
        top_a = 2.0 * mean_x * mean_y + ssim_one
        top_b = 2.0 * (raw_xy - mean_x * mean_y) + ssim_two
        low_c = mean_x * mean_x + mean_y * mean_y + ssim_one
        low_d = (raw_xx - mean_x * mean_x) + (raw_yy - mean_y * mean_y) + ssim_two
        inv_cd = 1.0 / (low_c * low_d)
        inv_dd = inv_cd * low_c
        ssim = top_a * top_b * inv_cd
        d_mean = 2.0 * mean_y * (top_b - top_a) * inv_cd - 2.0 * mean_x * ssim * (
            inv_cd * low_d - inv_dd
        )
        d_xx = -ssim * inv_dd
        d_xy = 2.0 * top_a * inv_cd
        cots += [jnp.where(inside, scale * part, 0.0) for part in (d_mean, d_xx, d_xy)]
    spread = dot_exact(band(TILE, tall, TILE // 2), jnp.concatenate(cots, axis=1))
    spread = jnp.concatenate([spread[:, i * width : (i + 1) * width] for i in range(9)], axis=0)
    spread = dot_exact(spread, across)
    grad_rows = []
    for c in range(3):
        img = pic[c]
        tgt = targets[0, c]
        s_mean, s_xx, s_xy = [spread[(3 * c + i) * TILE : (3 * c + i + 1) * TILE] for i in range(3)]
        res = img - tgt
        direct = (1.0 - ssim_weight) / (TILE * TILE) * res / jnp.sqrt(res * res + charb_eps)
        grad_rows.append(direct + s_mean + 2.0 * img * s_xx + tgt * s_xy)

    d_terms = jnp.zeros((6 * tiles, list_size), f32)
    d_colour = jnp.zeros((3 * tiles, list_size), f32)
    for i in range(n_chunk):
        per = wide // width
        parts = []
        for c in range(3):
            line = jnp.concatenate(
                [grad_rows[c][i * per + half : i * per + half + 1] for half in range(per)], axis=1
            )
            parts.append(jnp.where(in_tile, line, 0.0))
        hi, lo = pieces(jnp.concatenate(parts, axis=0), 2)
        shade = dot(col_t, jnp.concatenate([hi, hi, lo], axis=0).astype(bf16))
        weight = weight_buf[i]
        share = weight * shade
        d_power = share - ratio_buf[i] * dot(suffix, stack(share, 2))
        both = dot_t(basis(i), stack(d_power, 2))
        d_terms = d_terms + both[:, :list_size] + both[:, list_size:]
        both = fold(dot_t(jnp.concatenate([hi, lo], axis=0).astype(bf16), stack(weight, 2)), 2)
        d_colour = d_colour + both[:, :list_size] + both[:, list_size:]

    d0, d1, d2, d3, d4, d5 = [d_terms[k * tiles : (k + 1) * tiles] for k in range(6)]
    e1 = d1 - off_u * d0
    e2 = d2 - off_w * d0
    cot[...] = jnp.zeros_like(cot)
    cot[:, 0, :] = k0 * e1 + k1 * e2
    cot[:, 1, :] = k2 * e2 + k1 * e1
    cot[:, 2, :] = -0.5 * d3 + off_u * (d1 - 0.5 * off_u * d0)
    cot[:, 3, :] = off_w * e1 + off_u * d2 - d4
    cot[:, 4, :] = -0.5 * d5 + off_w * (d2 - 0.5 * off_w * d0)
    cot[:, 5, :] = d0
    for c in range(3):
        cot[:, 6 + c, :] = d_colour[c * tiles : (c + 1) * tiles]
    cot_pieces = [stack(cot[t], 3) for t in range(tiles)]

    def scatter(s):
        total = jnp.zeros((3 * ROWS_MSG, cap), f32)
        for t in range(tiles):
            total = total + dot_t(cot_pieces[t], slot_pick(s, t))
        back_out[s] = fold(total, 3)

    def second_copy(d, s):
        return pltpu.make_async_remote_copy(
            src_ref=back_out.at[d],
            dst_ref=back_in.at[s],
            send_sem=send_two.at[d],
            recv_sem=recv_two.at[s],
            device_id=(d, view),
            device_id_type=MESH,
        )

    def send_second(k):
        d = lax.rem(gs + k, n_gs)
        scatter(d)
        second_copy(d, gs).start()

    loop(1, n_gs, send_second)
    scatter(gs)
    back_in[gs] = back_out[gs]
    placed[...] = jnp.zeros_like(placed)

    def put_back(s):
        placed[...] += dot_t(stack(back_in[s], 3), pick_of(send, s, shard))

    put_back(gs)

    def put_next(k):
        s = lax.rem(gs + n_gs - k, n_gs)
        second_copy(gs, s).wait_recv()
        put_back(s)

    loop(1, n_gs, put_next)
    whole = fold(placed[...], 3)
    for c in range(chunks):
        views_out[view, 0:9, c, :] = whole[0:9, c * LANES : (c + 1) * LANES]
    first_row = lax.broadcasted_iota(jnp.int32, (chunks, LANES), 0) == 0
    views_out[view, 9] = jnp.where(first_row, cam_x, cam_y)

    def third_copy(to, of):
        return pltpu.make_async_remote_copy(
            src_ref=views_out.at[of],
            dst_ref=views_out.at[of],
            send_sem=send_three.at[to],
            recv_sem=recv_three.at[of],
            device_id=(gs, to),
            device_id_type=MESH,
        )

    def send_third(k):
        third_copy(lax.rem(view + k, n_view), view).start()

    def wait_third(k):
        third_copy(view, lax.rem(view + n_view - k, n_view)).wait_recv()

    loop(1, n_view, send_third)
    loop(1, n_view, wait_third)

    def done_first(k):
        first_copy(lax.rem(gs + k, n_gs), gs).wait_send()
        second_copy(lax.rem(gs + k, n_gs), gs).wait_send()

    def done_third(k):
        third_copy(lax.rem(view + k, n_view), view).wait_send()

    loop(1, n_gs, done_first)
    loop(1, n_view, done_third)


def pull_kernel(
    n_view,
    pic,
    views,
    par,
    opacity,
    pic_out,
    means_out,
    quats_out,
    scales_out,
    opacity_out,
    sh_out,
    g_par,
    g_means,
    g_quats,
    g_scales,
    g_opacity,
    g_sh,
    store_sems,
):
    chunks = par.shape[0]
    pic_copy = pltpu.make_async_copy(pic, pic_out, store_sems.at[0])
    pic_copy.start()
    cams = [(views[v, 9, 0:1, 0:1], views[v, 9, 1:2, 0:1]) for v in range(n_view)]
    _, pull = jax.vjp(lambda *args: project(*args, cams, 0.0, 0.0), *params(par, opacity))
    grads = pull([[views[v, i] for i in range(9)] for v in range(n_view)])
    for i in range(3):
        g_par[:, 48 + i, :] = grads[0][i]
        g_par[:, 64 + i, :] = grads[2][i]
    for i in range(4):
        g_par[:, 56 + i, :] = grads[1][i]
    for i in range(48):
        g_par[:, i, :] = grads[4][i]
    g_opacity[...] = grads[3]
    for c in range(chunks):
        cols = slice(c * LANES, (c + 1) * LANES)
        g_sh[:, cols] = g_par[c, 0:48, :]
        g_means[:, cols] = g_par[c, 48:51, :]
        g_quats[:, cols] = g_par[c, 56:60, :]
        g_scales[:, cols] = g_par[c, 64:67, :]
    stores = [
        pltpu.make_async_copy(src, dst, store_sems.at[k + 1])
        for k, (src, dst) in enumerate(
            [
                (g_sh, sh_out),
                (g_means, means_out),
                (g_quats, quats_out),
                (g_scales, scales_out),
                (g_opacity, opacity_out),
            ]
        )
    ]
    for store in stores:
        store.start()
    pic_copy.wait()
    for store in stores:
        store.wait()


def far_shards(
    means, quats, log_scales, opacity, sh_coeffs, cameras, targets, send_rows, tile_lists, list_lengths
):
    n_gs = lax.axis_size("gs")
    n_view = lax.axis_size("view")
    shard = means.shape[1]
    chunks = shard // LANES
    cap = send_rows.shape[2]
    tiles, list_size = tile_lists.shape[2:]
    width = tiles * TILE
    n_chunk = TILE // 2
    wide = 2 * width
    opacity = opacity.reshape(chunks, LANES)
    args = (
        means,
        quats,
        log_scales,
        opacity,
        sh_coeffs,
        cameras,
        targets,
        send_rows,
        tile_lists,
        list_lengths,
    )
    shape = jax.ShapeDtypeStruct
    dma = pltpu.SemaphoreType.DMA
    vmem = pl.BlockSpec(memory_space=VMEM)
    hbm = pl.BlockSpec(memory_space=pltpu.HBM)
    mids = pl.pallas_call(
        lambda *refs: far_kernel(n_gs, n_view, *refs),
        out_shape=(
            shape(targets.shape, f32),
            shape((n_view, 10, chunks, LANES), f32),
            shape((chunks, 72, LANES), f32),
            shape((chunks, LANES), f32),
        ),
        in_specs=[hbm] * len(args),
        out_specs=(vmem,) * 4,
        scratch_shapes=[
            VMEM(send_rows.shape, jnp.int32),
            VMEM(means.shape, f32),
            VMEM(quats.shape, f32),
            VMEM(log_scales.shape, f32),
            VMEM(sh_coeffs.shape, f32),
            VMEM(cameras.shape, f32),
            VMEM(targets.shape, f32),
            VMEM((tiles, list_size), jnp.int32),
            VMEM((1, tiles), jnp.int32),
            VMEM((chunks, ROWS_MSG, LANES), f32),
            VMEM((n_gs, ROWS_MSG, cap), f32),
            VMEM((n_gs, ROWS_MSG, cap), f32),
            VMEM((tiles, ROWS_MSG, list_size), f32),
            VMEM((n_chunk, list_size, wide), f32),
            VMEM((n_chunk, list_size, wide), f32),
            VMEM((3, TILE, width), f32),
            VMEM((2, 3, TILE, width), f32),
            VMEM((2, 3, TILE, width), f32),
            VMEM((tiles, ROWS_MSG, list_size), f32),
            VMEM((n_gs, ROWS_MSG, cap), f32),
            VMEM((n_gs, ROWS_MSG, cap), f32),
            VMEM((3 * ROWS_MSG, shard), f32),
            dma((10,)),
            dma((n_gs,)),
            dma((n_gs,)),
            dma((2,)),
            dma((2,)),
            dma((2,)),
            dma((2,)),
            dma((n_gs,)),
            dma((n_gs,)),
            dma((n_view,)),
            dma((n_view,)),
        ],
        compiler_params=pltpu.CompilerParams(
            collective_id=0, has_side_effects=True, vmem_limit_bytes=48 * 1024 * 1024
        ),
    )(*[pltpu.with_memory_space_constraint(x, pltpu.HBM) for x in args])
    outs = pl.pallas_call(
        lambda *refs: pull_kernel(n_view, *refs),
        out_shape=(
            shape(targets.shape, f32),
            shape(means.shape, f32),
            shape(quats.shape, f32),
            shape(log_scales.shape, f32),
            shape((chunks, LANES), f32),
            shape(sh_coeffs.shape, f32),
        ),
        in_specs=[vmem] * 4,
        out_specs=(hbm,) * 6,
        scratch_shapes=[
            VMEM((chunks, 72, LANES), f32),
            VMEM(means.shape, f32),
            VMEM(quats.shape, f32),
            VMEM(log_scales.shape, f32),
            VMEM((chunks, LANES), f32),
            VMEM(sh_coeffs.shape, f32),
            dma((6,)),
        ],
        compiler_params=pltpu.CompilerParams(vmem_limit_bytes=48 * 1024 * 1024),
    )(*mids)
    return (*outs[:4], outs[4].reshape(shard), outs[5])


def shards(
    means, quats, log_scales, opacity, sh_coeffs, cameras, targets, send_rows, tile_lists, list_lengths
):
    n_gs = lax.axis_size("gs")
    n_view = lax.axis_size("view")
    shard = means.shape[1]
    cap = send_rows.shape[2]
    args = (
        means,
        quats,
        log_scales,
        opacity,
        sh_coeffs,
        cameras,
        targets,
        send_rows,
        tile_lists,
        list_lengths,
    )
    if n_gs not in (2, 4, 8) or cap % LANES or n_view % 2:
        return far_shards(*args)
    chunks = shard // LANES
    tiles, list_size = tile_lists.shape[2:]
    width = tiles * TILE
    n_chunk = TILE // 2
    wide = 2 * width
    groups = n_view // 2
    args = args[:3] + (opacity.reshape(chunks, LANES),) + args[4:]
    shape = jax.ShapeDtypeStruct
    dma = pltpu.SemaphoreType.DMA
    vmem = pl.BlockSpec(memory_space=VMEM)
    hbm = pl.BlockSpec(memory_space=pltpu.HBM)
    out_shape = (
        shape(targets.shape, f32),
        shape(means.shape, f32),
        shape(quats.shape, f32),
        shape(log_scales.shape, f32),
        shape((chunks, LANES), f32),
        shape(sh_coeffs.shape, f32),
    )
    mids = pl.pallas_call(
        lambda *refs: near_kernel(n_gs, n_view, *refs),
        out_shape=out_shape,
        in_specs=[hbm] * len(args),
        out_specs=(vmem,) * 6,
        scratch_shapes=[
            VMEM((chunks, 72, LANES), f32),
            VMEM((chunks, LANES), f32),
            VMEM(send_rows.shape, jnp.int32),
            VMEM(means.shape, f32),
            VMEM(quats.shape, f32),
            VMEM(log_scales.shape, f32),
            VMEM(sh_coeffs.shape, f32),
            VMEM(cameras.shape, f32),
            VMEM(targets.shape, f32),
            VMEM((tiles, list_size), jnp.int32),
            VMEM((1, tiles), jnp.int32),
            VMEM((n_view, 1, LANES), f32),
            VMEM((chunks, ROWS_MSG, LANES), f32),
            VMEM((n_gs, 9, cap), f32),
            VMEM((n_gs, 9, cap), f32),
            VMEM((n_gs, cap, tiles * list_size), bf16),
            VMEM((n_gs, tiles * list_size, cap), bf16),
            VMEM((n_gs, cap, shard), bf16),
            VMEM((n_chunk, 6 * tiles, wide), bf16),
            VMEM((n_chunk * wide, 6 * tiles), bf16),
            VMEM((tiles, ROWS_MSG, list_size), f32),
            VMEM((n_chunk, list_size, wide), f32),
            VMEM((n_chunk, list_size, wide), f32),
            VMEM((list_size, 3 * width), f32),
            VMEM((n_chunk, wide, 2 * list_size), bf16),
            VMEM((3, n_chunk, list_size, wide), f32),
            VMEM((3, TILE, width), f32),
            VMEM((2, 3, TILE, width), f32),
            VMEM((2, 3, TILE, width), f32),
            VMEM((tiles, ROWS_MSG, list_size), f32),
            VMEM((n_gs, 9, cap), f32),
            VMEM((groups, n_gs, 9, cap), f32),
            VMEM((2 * ROWS_MSG * groups, shard), f32),
            VMEM((2, groups, N_KEPT, chunks, LANES), f32),
            VMEM((2, groups, 9, chunks, LANES), f32),
            VMEM((15, chunks, LANES), f32),
            VMEM((chunks, 72, LANES), f32),
            dma((10,)),
            dma((n_view,)),
            dma((n_view,)),
            dma((n_gs,)),
            dma((n_gs,)),
            dma((2,)),
            dma((2,)),
            dma((2,)),
            dma((2,)),
            dma((groups, n_gs)),
            dma((groups, n_gs)),
            dma((1,)),
            dma((1,)),
        ],
        compiler_params=pltpu.CompilerParams(
            collective_id=1, has_side_effects=True, vmem_limit_bytes=48 * 1024 * 1024
        ),
    )(*[pltpu.with_memory_space_constraint(x, pltpu.HBM) for x in args])
    outs = pl.pallas_call(
        store_kernel,
        out_shape=out_shape,
        in_specs=[vmem] * 6,
        out_specs=(hbm,) * 6,
        scratch_shapes=[dma((6,))],
        compiler_params=pltpu.CompilerParams(vmem_limit_bytes=48 * 1024 * 1024),
    )(*mids)
    return (*outs[:4], outs[4].reshape(shard), outs[5])


def solution(mesh):
    return jax.shard_map(
        shards,
        mesh=mesh,
        in_specs=(
            P(None, "gs"),
            P(None, "gs"),
            P(None, "gs"),
            P("gs"),
            P(None, "gs"),
            P("view", None),
            P("view", None, "gs", None),
            P("gs", None, None),
            P("view", "gs", None, None),
            P("view", "gs", None),
        ),
        out_specs=(
            P("view", None, "gs", None),
            P(None, "gs"),
            P(None, "gs"),
            P(None, "gs"),
            P("gs"),
            P(None, "gs"),
        ),
        check_vma=False,
    )
```
